32 devices in a mesh: leaf: 8 (over z, x), rows: 4 (over y, core).
Axes of the slice: x: 2, y: 2, z: 4, core: 2. Of those that a mesh axis runs over, the one named last changes fastest.
Arguments:
- leaf_basis: float32 [1024, 64, 256], P(('leaf', 'rows')), may hold values from -0.375 to 0.375
- leaf_transfer: float32 [1024, 64, 64], P(('leaf', 'rows'))
- device_transfer: float32 [32, 64, 64], P(('leaf', 'rows'))
- upper_transfer: float32 [30, 64, 64], replicated
- couplings: float32 [1024, 64, 64], P(('leaf', 'rows')), may hold values from -0.1875 to 0.1875
- couple_offset: int32 [1024], P(('leaf', 'rows')), may hold values from 4 to 28, as said below
Outputs:
- leaf_orth: float32 [1024, 64, 256], P(('leaf', 'rows'))
- leaf_bridge: float32 [1024, 64, 64], P(('leaf', 'rows'))
- new_transfers: float32 [32, 5, 64, 64], P(('leaf', 'rows'))
- coupled: float32 [1024, 64, 64], P(('leaf', 'rows'))
The draws below stay inside these ranges and needn't reach their ends.
Inputs may be any that keep to these rules, and one draw needn't show every extreme that they name: couple_offset[b] is 4 times a number of 1 to 7, so block b couples device cluster b // 32 with a cluster of another branch at the same position within its branch; among the 32 blocks of one device cluster, at most 6 name the same column cluster, and on every device some column cluster is named exactly 6 times.
All inputs are finite; a program needn't handle non-finite values.
Results may differ from the reference program's by a relative error of at most 0.0001.
Values sent between devices are 32-bit elements; how exact they have to be, the bound alone decides.
No kernel may reach another device: no remote copies, remote signals or barrier semaphores. Data moves between devices by JAX's collectives and lax.ppermute only.
A program may use at most 128 MiB of HBM per device.

```python
import jax
import jax.numpy as jnp
from jax import lax

LEAF = 256
RANK = 64
LEAF_DEV = 32
BLK_DEV = 32
LEAVES = 1024
BLOCKS = 1024
N_LEAF = 8
N_ROWS = 4


def near_identity(noise):
    eye = (lax.broadcasted_iota(jnp.int32, (RANK, RANK), 0) == lax.broadcasted_iota(jnp.int32, (RANK, RANK), 1)).astype(jnp.float32)
    return eye[None] + 0.3 / RANK ** 0.5 * noise


def draw_leaf_transfer(key, part):
    key = jax.random.fold_in(key, 11)
    shape = (LEAF_DEV * N_LEAF * N_ROWS, RANK, RANK)
    noise = jax.random.normal(key, shape, jnp.float32)
    return near_identity(noise)


def draw_device_transfer(key, part):
    key = jax.random.fold_in(key, 23)
    shape = (N_LEAF * N_ROWS, RANK, RANK)
    noise = jax.random.normal(key, shape, jnp.float32)
    return near_identity(noise)


def draw_upper_transfer(key, part):
    key = jax.random.fold_in(key, 37)
    shape = (N_LEAF * N_ROWS - 2, RANK, RANK)
    noise = jax.random.normal(key, shape, jnp.float32)
    return near_identity(noise)


def draw_couple_offset(key, part):
    key = jax.random.fold_in(key, 41)
    clusters = N_LEAF * N_ROWS
    others = N_LEAF - 1
    scores = jax.random.randint(key, (clusters, others), 0, 1 << 20)
    scores = scores * others + lax.broadcasted_iota(jnp.int32, (clusters, others), 1)
    order = jnp.argsort(scores, axis=1).astype(jnp.int32)
    slots = lax.broadcasted_iota(jnp.int32, (clusters, BLK_DEV), 1)
    picks = jnp.maximum(slots - 1, 0) % others
    chosen = jnp.take_along_axis(order, picks, axis=1) + 1
    return (N_ROWS * chosen).reshape(clusters * BLK_DEV).astype(jnp.int32)


def steps_of(stream_key, extent, shards, low, top_value):
    loudness = 1.0
    for dim, blocks in shards:
        steps = jax.random.uniform(jax.random.fold_in(jax.random.fold_in(stream_key, 6), dim), (blocks,), jnp.float32, low / len(shards), top_value / len(shards))
        loudness = loudness * jnp.repeat(jnp.exp(steps), extent[dim] // blocks).reshape((-1,) + (1,) * (len(extent) - 1 - dim))
    return loudness


def normal_values(rng, extent, spread, reach, cuts=(), kind=jnp.bfloat16):
    result = jax.random.normal(rng, extent, jnp.float32) * spread
    if len(cuts) > 0:
        result = steps_of(rng, extent, cuts, -0.22, 0.18) * result
    return jnp.clip(result, min=-reach, max=reach).astype(kind)


def setup_inputs(seed: int = 0) -> dict:
    seeds = jax.random.split(jax.random.key(seed), 7)
    leaf_basis = normal_values(seeds[0], (LEAVES, RANK, LEAF), 0.0625, 0.375, ((0, 32),), jnp.float32)
    leaf_transfer = draw_leaf_transfer(jax.random.fold_in(seeds[6], 71), 0)
    device_transfer = draw_device_transfer(jax.random.fold_in(seeds[6], 71), 0)
    upper_transfer = draw_upper_transfer(jax.random.fold_in(seeds[6], 71), 0)
    couplings = normal_values(seeds[4], (BLOCKS, RANK, RANK), (1.0 / LEAF_DEV), 0.1875, ((0, 32),), jnp.float32)
    couple_offset = draw_couple_offset(jax.random.fold_in(seeds[6], 71), 0)
    return {"leaf_basis": leaf_basis, "leaf_transfer": leaf_transfer, "device_transfer": device_transfer, "upper_transfer": upper_transfer, "couplings": couplings, "couple_offset": couple_offset}


HIGH = lax.Precision.HIGHEST

def lower_solve(low, right):
    return lax.linalg.triangular_solve(low, right, left_side=True, lower=True)

def lift(grams, trans):
    inner = jnp.einsum('nkl,nlj->nkj', grams, trans, precision=HIGH)
    return jnp.einsum('nki,nkj->nij', trans, inner, precision=HIGH)

def reference(leaf_basis, leaf_transfer, device_transfer, upper_transfer, couplings, couple_offset):
    clusters = N_LEAF * N_ROWS
    levels = clusters.bit_length() - 1
    leaf_gram = jnp.einsum('nrk,nsk->nrs', leaf_basis, leaf_basis, precision=HIGH)
    leaf_low = jnp.linalg.cholesky(leaf_gram)
    leaf_orth = lower_solve(leaf_low, leaf_basis)
    moved = lift(leaf_gram, leaf_transfer)
    device_gram = jnp.sum(moved.reshape(clusters, LEAF_DEV, RANK, RANK), axis=1)
    grams = [device_gram]
    transfers = [device_transfer]
    lifted = lift(device_gram, device_transfer)
    for level in range(levels - 1, -1, -1):
        gram = lifted[0::2] + lifted[1::2]
        grams.append(gram)
        if level > 0:
            trans = upper_transfer[2 ** level - 2:2 ** (level + 1) - 2]
            transfers.append(trans)
            lifted = lift(gram, trans)
    lows = [jnp.linalg.cholesky(gram) for gram in grams]
    columns = []
    for step in range(levels):
        parent = jnp.repeat(lows[step + 1], 2, axis=0)
        right = jnp.einsum('nki,nkj->nij', transfers[step], lows[step], precision=HIGH)
        fresh = jnp.swapaxes(lower_solve(parent, right), 1, 2)
        columns.append(jnp.repeat(fresh, 2 ** step, axis=0))
    new_transfers = jnp.stack(columns, axis=1)
    device_low = jnp.repeat(lows[0], LEAF_DEV, axis=0)
    right = jnp.einsum('nki,nkj->nij', leaf_transfer, leaf_low, precision=HIGH)
    leaf_bridge = jnp.swapaxes(lower_solve(device_low, right), 1, 2)
    owners = (jnp.arange(BLK_DEV * clusters, dtype=jnp.int32) // BLK_DEV).astype(jnp.int32)
    targets = ((owners + couple_offset) % clusters).astype(jnp.int32)
    row_low = jnp.take(lows[0], owners, axis=0)
    col_low = jnp.take(lows[0], targets, axis=0)
    inner = jnp.einsum('nkl,nlj->nkj', couplings, col_low, precision=HIGH)
    coupled = jnp.einsum('nki,nkj->nij', row_low, inner, precision=HIGH)
    return (leaf_orth, leaf_bridge, new_transfers, coupled)
```

```python
import functools

import jax
import jax.numpy as jnp
from jax import lax
from jax.experimental import pallas as pl
from jax.experimental.pallas import tpu as pltpu
from jax.sharding import PartitionSpec as P

HIGH = lax.Precision.HIGHEST
SUB = 8


def mm(a, b):
    return lax.dot_general(
        a, b, (((1,), (0,)), ((), ())), precision=HIGH, preferred_element_type=jnp.float32
    )


def mm_nt(a, b):
    return lax.dot_general(
        a, b, (((1,), (1,)), ((), ())), precision=HIGH, preferred_element_type=jnp.float32
    )


def mm_tn(a, b):
    return lax.dot_general(
        a, b, (((0,), (0,)), ((), ())), precision=HIGH, preferred_element_type=jnp.float32
    )


def lift(gram, trans):
    return mm_tn(trans, mm(gram, trans))


def eliminate(w_ref, f_ref, s_ref):
    rank = w_ref.shape[0]
    lanes = w_ref.shape[2]
    groups = rank // SUB
    place = lax.broadcasted_iota(jnp.int32, (SUB, lanes), 0)

    def block(rows, cols):
        return w_ref[pl.ds(rows * SUB, SUB), pl.ds(cols * SUB, SUB), :]

    def spread(value, at):
        return jnp.broadcast_to(value[at : at + 1, :], (SUB, lanes))

    def corner(kb):
        rows = [w_ref[kb * SUB + p, pl.ds(kb * SUB, SUB), :] for p in range(SUB)]
        inverses = []
        for q in range(SUB):
            pivot = spread(rows[q], q)
            inverse = 1.0 / pivot
            root = lax.rsqrt(pivot)
            root = root * (1.5 - 0.5 * pivot * root * root)
            s_ref[kb * SUB + q] = root
            inverses.append(inverse)
            scaled = rows[q] * inverse
            unit = jnp.where(place == q, 1.0, rows[q])
            for p in range(q + 1, SUB):
                kept = jnp.where(place == q, 0.0, rows[p])
                rows[p] = kept - spread(scaled, p) * unit
        for p in range(SUB):
            w_ref[kb * SUB + p, pl.ds(kb * SUB, SUB), :] = rows[p]
        return rows, inverses

    def panel(kb, rows, inverses):
        mult = {(p, q): spread(rows[p], q) for p in range(SUB) for q in range(p)}
        for jv in range(groups):
            if jv == kb:
                continue
            old = [w_ref[kb * SUB + p, pl.ds(jv * SUB, SUB), :] for p in range(SUB)]
            for p in range(SUB):
                new = old[p]
                for q in range(p):
                    new = new + mult[p, q] * old[q]
                if p:
                    w_ref[kb * SUB + p, pl.ds(jv * SUB, SUB), :] = new
                if jv > kb:
                    scaled = new * inverses[p]
                    for s in range(SUB):
                        f_ref[p, jv * SUB + s] = spread(scaled, s)

    def trail(kb, rows, ib, jv):
        if jv == kb:
            acc = None
        else:
            acc = block(ib, jv)
        for q in range(SUB):
            if jv == kb:
                source = jnp.where(place < q, rows[q], jnp.where(place == q, 1.0, 0.0))
            else:
                source = w_ref[kb * SUB + q, pl.ds(jv * SUB, SUB), :]
            term = f_ref[q, pl.ds(ib * SUB, SUB)] * source[None]
            acc = -term if acc is None else acc - term
        w_ref[pl.ds(ib * SUB, SUB), pl.ds(jv * SUB, SUB), :] = acc

    rows, inverses = corner(0)
    for kb in range(groups):
        panel(kb, rows, inverses)
        if kb + 1 == groups:
            break
        trail(kb, rows, kb + 1, kb + 1)
        ahead = corner(kb + 1)
        for jv in range(groups):
            for ib in range(kb + 1, groups):
                if (ib, jv) == (kb + 1, kb + 1):
                    continue
                if jv > kb and ib > jv:
                    continue
                trail(kb, rows, ib, jv)
        rows, inverses = ahead


def read_factors(w_ref, s_ref, k):
    rank = w_ref.shape[0]
    lanes = w_ref.shape[2]
    row = w_ref[k]
    root = jnp.broadcast_to(s_ref[k][:1], (rank, lanes))
    place = lax.broadcasted_iota(jnp.int32, (rank, lanes), 0)
    upper = jnp.where(place >= k, row * root, 0.0)
    inverse = jnp.where(place < k, row * root, jnp.where(place == k, root, 0.0))
    return jnp.concatenate([upper, inverse], axis=0).T


def gram_kernel(steps, basis_ref, trans_ref, dev_ref, grams_ref, lift_ref, acc_ref):
    step = pl.program_id(0)
    chunk, rank = basis_ref.shape[0], basis_ref.shape[1]
    parts = []
    for n in range(chunk):
        basis = basis_ref[n]
        gram = mm_nt(basis, basis)
        grams_ref[step * chunk + n] = gram
        parts.append(mm(gram, trans_ref[n]))
    inner = jnp.concatenate(parts, axis=0)
    total = mm_tn(trans_ref[...].reshape(chunk * rank, rank), inner)

    @pl.when(step == 0)
    def _():
        acc_ref[...] = total

    @pl.when(step > 0)
    def _():
        acc_ref[...] += total

    @pl.when(step == steps - 1)
    def _():
        gram = acc_ref[...]
        grams_ref[steps * chunk] = gram
        lift_ref[...] = lift(gram, dev_ref[0])


def factor_kernel(grams_ref, out_ref, w_ref, f_ref, s_ref):
    count, rank = grams_ref.shape[0], grams_ref.shape[1]
    flat = grams_ref.reshape(count * rank, rank)
    for i in range(rank):
        w_ref[i] = flat[pl.ds(i, count, stride=rank), :].T
    eliminate(w_ref, f_ref, s_ref)
    out = out_ref.reshape(count * rank, 2 * rank)
    for k in range(rank):
        out[pl.ds(k, count, stride=rank), :] = read_factors(w_ref, s_ref, k)


def branch_kernel(n_rows, n_leaf, *refs):
    own_ref = refs[0]
    got = refs[1:n_rows]
    upper_ref, factor_ref, send_ref, path_ref = refs[n_rows:]
    rank = own_ref.shape[0]
    branch, row = lax.axis_index("leaf"), lax.axis_index("rows")
    lifted = [own_ref[...]] + [ref[...] for ref in got]
    level = (n_rows * n_leaf).bit_length() - 1
    node = branch * n_rows + row
    step = 0
    while len(lifted) > 1:
        grams = [lifted[2 * n] + lifted[2 * n + 1] for n in range(len(lifted) // 2)]
        level -= 1
        node = node >> 1
        path_ref[step] = grams[0]
        step += 1
        lifted = [
            lift(gram, upper_ref[2**level - 2 + (node ^ n)]) for n, gram in enumerate(grams)
        ]
    send_ref[0] = factor_ref[0, :, :rank]
    send_ref[1] = lifted[0]


def leaf_kernel(basis_ref, trans_ref, coup_ref, factor_ref, own_ref, orth_ref, bridge_ref, half_ref):
    chunk, rank = basis_ref.shape[0], basis_ref.shape[1]
    own_upper = own_ref[0, :, :rank]
    own_inverse = own_ref[0, :, rank:]
    parts = []
    for n in range(chunk):
        upper = factor_ref[n, :, :rank]
        inverse = factor_ref[n, :, rank:]
        orth_ref[n] = mm(inverse, basis_ref[n])
        parts.append(mm(upper, trans_ref[n]))
        half_ref[n] = mm(own_upper, coup_ref[n])
    moved = mm_nt(jnp.concatenate(parts, axis=0), own_inverse)
    bridge_ref[...] = moved.reshape(chunk, rank, rank)


def top_kernel(n_rows, n_leaf, *refs):
    send_ref = refs[0]
    got = refs[1:n_leaf]
    (
        upper_ref,
        dev_ref,
        path_ref,
        own_ref,
        half_ref,
        offset_ref,
        fresh_ref,
        coupled_ref,
        grams_ref,
        cols_ref,
        out_ref,
        w_ref,
        f_ref,
        s_ref,
    ) = refs[n_leaf:]
    rank = send_ref.shape[1]
    row_bits = n_rows.bit_length() - 1
    leaf_bits = n_leaf.bit_length() - 1
    levels = row_bits + leaf_bits
    branch, row = lax.axis_index("leaf"), lax.axis_index("rows")
    myself = branch * n_rows + row
    every = [send_ref] + list(got)
    for n, ref in enumerate(every):
        cols_ref[n] = ref[0]
    lifted = [ref[1] for ref in every]
    for n in range(row_bits):
        grams_ref[n] = path_ref[n]
    level, node, step = leaf_bits, branch, row_bits
    while len(lifted) > 1:
        grams = [lifted[2 * n] + lifted[2 * n + 1] for n in range(len(lifted) // 2)]
        level -= 1
        node = node >> 1
        grams_ref[step] = grams[0]
        step += 1
        if level == 0:
            break
        lifted = [
            lift(gram, upper_ref[2**level - 2 + (node ^ n)]) for n, gram in enumerate(grams)
        ]
    flat = grams_ref.reshape(levels * rank, rank)
    for i in range(rank):
        w_ref[i] = flat[pl.ds(i, levels, stride=rank), :].T
    eliminate(w_ref, f_ref, s_ref)
    out = out_ref.reshape(levels * rank, 2 * rank)
    for k in range(rank):
        out[pl.ds(k, levels, stride=rank), :] = read_factors(w_ref, s_ref, k)
    for k in range(levels):
        node_level = levels - k
        if k == 0:
            edge = dev_ref[0]
            low = own_ref[0, :, :rank]
        else:
            edge = upper_ref[2**node_level - 2 + (myself >> k)]
            low = out_ref[k - 1, :, :rank]
        fresh_ref[0, k] = mm_nt(mm(low, edge), out_ref[k, :, rank:])
    for b in range(half_ref.shape[0]):
        target = lax.rem(myself + offset_ref[b], n_rows * n_leaf)
        column = (target // n_rows) ^ branch
        coupled_ref[b] = mm_nt(half_ref[b], cols_ref[column])


def swaps(value, axis):
    size = lax.axis_size(axis)
    return [
        lax.ppermute(value, axis, [(source, source ^ mask) for source in range(size)])
        for mask in range(1, size)
    ]


def cost(flops, moved):
    return pl.CostEstimate(flops=flops, bytes_accessed=moved, transcendentals=0)


def per_device(
    leaf_basis, leaf_transfer, device_transfer, upper_transfer, couplings, couple_offset
):
    n_rows = lax.axis_size("rows")
    n_leaf = lax.axis_size("leaf")
    row_bits = n_rows.bit_length() - 1
    levels = row_bits + n_leaf.bit_length() - 1
    leaves, rank, points = leaf_basis.shape
    blocks = couplings.shape[0]
    f32 = jnp.float32
    params = pltpu.CompilerParams(vmem_limit_bytes=40 * 1024 * 1024)
    vmem = pl.BlockSpec(memory_space=pltpu.VMEM)
    smem = pl.BlockSpec(memory_space=pltpu.SMEM)
    chunk = 8
    steps = leaves // chunk

    def scratch(count):
        return [
            pltpu.VMEM((rank, rank, count), f32),
            pltpu.VMEM((SUB, rank, SUB, count), f32),
            pltpu.VMEM((rank, SUB, count), f32),
        ]

    def part(*tail):
        return pl.BlockSpec((chunk,) + tail, lambda n: (n,) + (0,) * len(tail))

    def whole(*shape):
        return pl.BlockSpec(shape, lambda n: (0,) * len(shape))

    grams, own_lift = pl.pallas_call(
        functools.partial(gram_kernel, steps),
        grid=(steps,),
        in_specs=[part(rank, points), part(rank, rank), whole(1, rank, rank)],
        out_specs=[whole(leaves + 1, rank, rank), whole(rank, rank)],
        out_shape=[
            jax.ShapeDtypeStruct((leaves + 1, rank, rank), f32),
            jax.ShapeDtypeStruct((rank, rank), f32),
        ],
        scratch_shapes=[pltpu.VMEM((rank, rank), f32)],
        compiler_params=params,
        cost_estimate=cost(10**9, 4 * 10**6),
        name="gram",
    )(leaf_basis, leaf_transfer, device_transfer)
    row_lifts = swaps(own_lift, "rows")
    factors = pl.pallas_call(
        factor_kernel,
        in_specs=[vmem],
        out_specs=vmem,
        out_shape=jax.ShapeDtypeStruct((leaves + 1, rank, 2 * rank), f32),
        scratch_shapes=scratch(leaves + 1),
        compiler_params=params,
        cost_estimate=cost(5 * 10**9, 8 * 10**6),
        name="factor",
    )(grams)
    sent, path = pl.pallas_call(
        functools.partial(branch_kernel, n_rows, n_leaf),
        grid=(1,),
        in_specs=[vmem] * (n_rows + 1)
        + [pl.BlockSpec((1, rank, 2 * rank), lambda n: (leaves, 0, 0))],
        out_specs=[vmem, vmem],
        out_shape=[
            jax.ShapeDtypeStruct((2, rank, rank), f32),
            jax.ShapeDtypeStruct((row_bits, rank, rank), f32),
        ],
        compiler_params=params,
        name="branch",
    )(own_lift, *row_lifts, upper_transfer, factors)
    others = swaps(sent, "leaf")
    leaf_orth, leaf_bridge, half = pl.pallas_call(
        leaf_kernel,
        grid=(steps,),
        in_specs=[
            part(rank, points),
            part(rank, rank),
            part(rank, rank),
            part(rank, 2 * rank),
            pl.BlockSpec((1, rank, 2 * rank), lambda n: (leaves, 0, 0)),
        ],
        out_specs=[part(rank, points), part(rank, rank), part(rank, rank)],
        out_shape=[
            jax.ShapeDtypeStruct(leaf_basis.shape, f32),
            jax.ShapeDtypeStruct(leaf_transfer.shape, f32),
            jax.ShapeDtypeStruct(couplings.shape, f32),
        ],
        compiler_params=params,
        cost_estimate=cost(5 * 10**9, 8 * 10**6),
        name="leaf",
    )(leaf_basis, leaf_transfer, couplings, factors, factors)
    new_transfers, coupled = pl.pallas_call(
        functools.partial(top_kernel, n_rows, n_leaf),
        grid=(1,),
        in_specs=[vmem] * (n_leaf + 3)
        + [pl.BlockSpec((1, rank, 2 * rank), lambda n: (leaves, 0, 0)), vmem, smem],
        out_specs=[vmem, vmem],
        out_shape=[
            jax.ShapeDtypeStruct((1, levels, rank, rank), f32),
            jax.ShapeDtypeStruct(couplings.shape, f32),
        ],
        scratch_shapes=[
            pltpu.VMEM((levels, rank, rank), f32),
            pltpu.VMEM((n_leaf, rank, rank), f32),
            pltpu.VMEM((levels, rank, 2 * rank), f32),
        ]
        + scratch(levels),
        compiler_params=params,
        name="top",
    )(sent, *others, upper_transfer, device_transfer, path, factors, half, couple_offset)
    return (leaf_orth, leaf_bridge, new_transfers, coupled)


def solution(mesh):
    in_specs = (
        P(("leaf", "rows"), None, None),
        P(("leaf", "rows"), None, None),
        P(("leaf", "rows"), None, None),
        P(),
        P(("leaf", "rows"), None, None),
        P(("leaf", "rows")),
    )
    out_specs = (
        P(("leaf", "rows"), None, None),
        P(("leaf", "rows"), None, None),
        P(("leaf", "rows"), None, None, None),
        P(("leaf", "rows"), None, None),
    )
    return jax.shard_map(
        per_device, mesh=mesh, in_specs=in_specs, out_specs=out_specs, check_vma=False
    )
```

```python
import functools

import jax
import jax.numpy as jnp
from jax import lax
from jax.experimental import pallas as pl
from jax.experimental.pallas import tpu as pltpu
from jax.sharding import PartitionSpec as P

HIGH = lax.Precision.HIGHEST
SUB = 8
LANES = 128
SET = LANES // SUB
F32 = jnp.float32
B16 = jnp.bfloat16


def mm(a, b, dims=((1,), (0,)), precision=None):
    return lax.dot_general(
        a, b, (dims, ((), ())), precision=precision, preferred_element_type=F32
    )


def mm_nt(a, b, precision=None):
    return mm(a, b, ((1,), (1,)), precision)


def mm_tn(a, b, precision=None):
    return mm(a, b, ((0,), (0,)), precision)


def lift(gram, trans):
    return mm_tn(trans, mm(gram, trans, precision=HIGH), HIGH)


def halves(x):
    high = x.astype(B16).astype(F32)
    return high, x - high


def pair(x):
    return jnp.concatenate(halves(x), axis=1).astype(B16)


def twice(x):
    return jnp.concatenate([x, x], axis=1)


def tall(x):
    high, low = halves(x)
    high, low = high.astype(B16), low.astype(B16)
    return jnp.concatenate([high, high, low, low], axis=0)


def broad(x):
    high, low = halves(x)
    return jnp.concatenate([high, high, low, low], axis=1).astype(B16)


def fold(x):
    half = x.shape[1] // 2
    return x[:, :half] + x[:, half:]


def spread(value, at):
    return jnp.broadcast_to(value[at : at + 1, :], (SUB, LANES))


def load_sets(flat, w_ref):
    sets, groups, rank = w_ref.shape[0], w_ref.shape[1], w_ref.shape[2]
    for t in range(sets):
        for ib in range(groups):
            rows = [
                flat[pl.ds(t * SET * rank + ib * SUB + s, SET, stride=rank), :]
                for s in range(SUB)
            ]
            w_ref[t, ib] = jnp.concatenate(rows, axis=0).T


def eliminate(w_ref, g_ref, out):
    sets, groups, rank = w_ref.shape[0], w_ref.shape[1], w_ref.shape[2]
    place = lax.broadcasted_iota(jnp.int32, (SUB, LANES), 0)
    lane = lax.broadcasted_iota(jnp.int32, (SUB, LANES), 1)
    group = lane // SET
    picks = [p * SET + lane % SET for p in range(SUB)]

    def tile(t, ib, jv):
        return w_ref[t, ib, pl.ds(jv * SUB, SUB), :]

    def picked(value, p):
        return jnp.take_along_axis(value, picks[p], axis=1, mode="promise_in_bounds")

    def corner(t, kb):
        diagonal = tile(t, kb, kb)
        rows = [picked(diagonal, p) for p in range(SUB)]
        inverses, roots = [], []
        for q in range(SUB):
            pivot = spread(rows[q], q)
            inverse = 1.0 / pivot
            root = lax.rsqrt(pivot)
            roots.append(root * (1.5 - 0.5 * pivot * root * root))
            inverses.append(inverse)
            scaled = rows[q] * inverse
            unit = jnp.where(place == q, 1.0, rows[q])
            for p in range(q + 1, SUB):
                kept = jnp.where(place == q, 0.0, rows[p])
                rows[p] = kept - spread(scaled, p) * unit
        return rows, inverses, roots

    def merged(parts):
        value = parts[0]
        for p in range(1, SUB):
            value = jnp.where(group == p, parts[p], value)
        return value

    def panel(t, kb, rows, inverses, roots):
        mult = {(p, q): spread(rows[p], q) for p in range(SUB) for q in range(p)}
        root = merged(roots)
        upper, lower = [], []
        for jv in range(groups):
            if jv == kb:
                for p in range(SUB):
                    unit = jnp.where(place == p, 1.0, 0.0)
                    g_ref[t, p, pl.ds(jv * SUB, SUB), :] = jnp.where(place < p, rows[p], unit)
                final = merged(rows) * root
                upper.append(jnp.where(place >= group, final, 0.0))
                unit = jnp.where(place == group, root, 0.0)
                lower.append(jnp.where(place < group, final, unit))
                continue
            value = tile(t, kb, jv)
            old = [picked(value, p) for p in range(SUB)]
            new = []
            for p in range(SUB):
                term = old[p]
                for q in range(p):
                    term = term + mult[p, q] * old[q]
                g_ref[t, p, pl.ds(jv * SUB, SUB), :] = term
                new.append(term)
            final = merged(new) * root
            zero = jnp.zeros((SUB, LANES), F32)
            upper.append(final if jv > kb else zero)
            lower.append(final if jv < kb else zero)
        return mult, jnp.concatenate(upper + lower, axis=0)

    def store(t, kb, factors):
        turned = factors.T
        for s in range(SUB):
            out[pl.ds(t * SET * rank + kb * SUB + s, SET, stride=rank), :] = turned[
                s * SET : (s + 1) * SET
            ]

    def weights(t, kb, ib, mult, inverses):
        value = tile(t, ib, kb)
        columns = [spread(value, q) for q in range(SUB)]
        found = []
        for q in range(SUB):
            term = columns[q]
            for r in range(q):
                term = term + mult[q, r] * columns[r]
            found.append(term * inverses[q])
        return found

    def trail(t, kb, ib, jv, found):
        acc = None if jv == kb else tile(t, ib, jv)
        for q in range(SUB):
            term = found[q] * g_ref[t, q, pl.ds(jv * SUB, SUB), :]
            acc = -term if acc is None else acc - term
        w_ref[t, ib, pl.ds(jv * SUB, SUB), :] = acc

    corners = [corner(t, 0) for t in range(sets)]
    for kb in range(groups):
        panels = [panel(t, kb, *corners[t]) for t in range(sets)]
        ahead = []
        if kb + 1 < groups:
            for t in range(sets):
                found = weights(t, kb, kb + 1, panels[t][0], corners[t][1])
                for jv in [kb + 1] + [jv for jv in range(groups) if jv != kb + 1]:
                    trail(t, kb, kb + 1, jv, found)
            ahead = [corner(t, kb + 1) for t in range(sets)]
        for t in range(sets):
            for ib in range(kb + 2, groups):
                found = weights(t, kb, ib, panels[t][0], corners[t][1])
                for jv in range(groups):
                    trail(t, kb, ib, jv, found)
            store(t, kb, panels[t][1])
        corners = ahead


def gram_kernel(
    steps,
    basis_hbm,
    trans_hbm,
    dev_ref,
    basis_ref,
    trans_ref,
    grams_ref,
    own_ref,
    lift_ref,
    basis_sem,
    trans_sem,
):
    leaves, rank = basis_ref.shape[0], basis_ref.shape[1]
    chunk = leaves // steps
    copies = []
    for step in range(steps):
        span = pl.ds(step * chunk, chunk)
        copies.append(
            (
                pltpu.make_async_copy(basis_hbm.at[span], basis_ref.at[span], basis_sem.at[step]),
                pltpu.make_async_copy(trans_hbm.at[span], trans_ref.at[span], trans_sem.at[step]),
            )
        )
        for copy in copies[-1]:
            copy.start()
    total = jnp.zeros((2 * rank, 2 * rank), F32)
    for step in range(steps):
        for copy in copies[step]:
            copy.wait()
        left, right = [], []
        for n in range(step * chunk, (step + 1) * chunk):
            basis = basis_ref[n]
            high, rest = halves(basis)
            middle, low = halves(rest)
            three = jnp.concatenate([high, middle, low], axis=0).astype(B16)
            product = mm_nt(three, three)
            rows = product[:rank] + product[rank : 2 * rank] + product[2 * rank :]
            gram = fold(rows[:, : 2 * rank]) + rows[:, 2 * rank :]
            grams_ref[n] = gram
            trans = pair(trans_ref[n])
            high, low = halves(gram)
            parts = mm(jnp.concatenate([high, low], axis=0).astype(B16), trans)
            left.append(trans)
            right.append(pair(fold(parts[:rank] + parts[rank:])))
        total = total + mm_tn(jnp.concatenate(left, axis=0), jnp.concatenate(right, axis=0))
    gram = fold(total[:rank] + total[rank:])
    own_ref[...] = gram
    lift_ref[...] = lift(gram, dev_ref[0])


def factor_kernel(grams_ref, out_ref, w_ref, g_ref):
    count, rank = grams_ref.shape[0], grams_ref.shape[1]
    load_sets(grams_ref.reshape(count * rank, rank), w_ref)
    eliminate(w_ref, g_ref, out_ref.reshape(count * rank, 2 * rank))


def branch_kernel(n_rows, n_leaf, *refs):
    own_ref, lift_ref = refs[:2]
    got = refs[2 : n_rows + 1]
    upper_ref, send_ref, path_ref = refs[n_rows + 1 :]
    branch, row = lax.axis_index("leaf"), lax.axis_index("rows")
    lifted = [lift_ref[...]] + [ref[...] for ref in got]
    level = (n_rows * n_leaf).bit_length() - 1
    node = branch * n_rows + row
    step = 0
    while len(lifted) > 1:
        grams = [lifted[2 * n] + lifted[2 * n + 1] for n in range(len(lifted) // 2)]
        level -= 1
        node = node >> 1
        path_ref[step] = grams[0]
        step += 1
        lifted = [
            lift(gram, upper_ref[2**level - 2 + (node ^ n)]) for n, gram in enumerate(grams)
        ]
    packed = jnp.concatenate([own_ref[...], lifted[0]], axis=1)
    for n in range(n_leaf):
        send_ref[n] = packed


def leaf_kernel(
    steps,
    basis_ref,
    trans_ref,
    coup_ref,
    factor_ref,
    orth_hbm,
    moved_ref,
    split_ref,
    orth_ref,
    orth_sem,
):
    leaves, rank = basis_ref.shape[0], basis_ref.shape[1]
    chunk = leaves // steps
    lane = lax.broadcasted_iota(jnp.int32, (rank, 2 * rank), 1)
    copies = []
    for step in range(steps):
        for n in range(step * chunk, (step + 1) * chunk):
            high, low = halves(factor_ref[n])
            low = jnp.concatenate([low[:, rank:], low[:, :rank]], axis=1)
            upper = jnp.where(lane < rank, high, low).astype(B16)
            inverse = jnp.where(lane < rank, low, high).astype(B16)
            orth_ref[n] = mm(twice(inverse), tall(basis_ref[n]))
            moved_ref[n] = pair(mm(twice(upper), tall(trans_ref[n])))
            split_ref[n] = pair(coup_ref[n])
        span = pl.ds(step * chunk, chunk)
        copy = pltpu.make_async_copy(orth_ref.at[span], orth_hbm.at[span], orth_sem.at[step])
        copy.start()
        copies.append(copy)
    for copy in copies:
        copy.wait()


def top_kernel(
    n_rows,
    n_leaf,
    steps,
    got_ref,
    upper_ref,
    dev_ref,
    path_ref,
    moved_ref,
    split_ref,
    offset_ref,
    fresh_ref,
    bridge_hbm,
    coupled_hbm,
    grams_ref,
    factor_ref,
    cols_ref,
    bridge_ref,
    coupled_ref,
    bridge_sem,
    coupled_sem,
    w_ref,
    g_ref,
):
    rank = got_ref.shape[1]
    row_bits = n_rows.bit_length() - 1
    leaf_bits = n_leaf.bit_length() - 1
    levels = row_bits + leaf_bits
    branch, row = lax.axis_index("leaf"), lax.axis_index("rows")
    myself = branch * n_rows + row
    for n in range(n_leaf):
        grams_ref[levels + n] = got_ref[n, :, :rank]
    for n in range(row_bits):
        grams_ref[n] = path_ref[n]
    lifted = [got_ref[branch ^ n, :, rank:] for n in range(n_leaf)]
    level, node, step = leaf_bits, branch, row_bits
    while len(lifted) > 1:
        grams = [lifted[2 * n] + lifted[2 * n + 1] for n in range(len(lifted) // 2)]
        level -= 1
        node = node >> 1
        grams_ref[step] = grams[0]
        step += 1
        if level == 0:
            break
        lifted = [
            lift(gram, upper_ref[2**level - 2 + (node ^ n)]) for n, gram in enumerate(grams)
        ]
    count = grams_ref.shape[0]
    load_sets(grams_ref.reshape(count * rank, rank), w_ref)
    eliminate(w_ref, g_ref, factor_ref.reshape(count * rank, 2 * rank))
    own = factor_ref[levels + branch]
    own_upper = twice(pair(own[:, :rank]))
    own_inverse = broad(own[:, rank:])
    for n in range(n_leaf):
        cols_ref[n] = broad(factor_ref[levels + n, :, :rank])
    copies = []
    leaves = moved_ref.shape[0]
    chunk = leaves // steps
    for step in range(steps):
        span = pl.ds(step * chunk, chunk)
        moved = twice(moved_ref[span].reshape(chunk * rank, 2 * rank))
        bridge_ref[span] = mm_nt(moved, own_inverse).reshape(chunk, rank, rank)
        copy = pltpu.make_async_copy(
            bridge_ref.at[span], bridge_hbm.at[span], bridge_sem.at[step]
        )
        copy.start()
        copies.append(copy)
    blocks = split_ref.shape[0]
    chunk = blocks // steps
    for step in range(steps):
        for b in range(step * chunk, (step + 1) * chunk):
            target = lax.rem(myself + offset_ref[b], n_rows * n_leaf)
            inner = mm_nt(twice(split_ref[b]), cols_ref[target // n_rows])
            coupled_ref[b] = mm(own_upper, tall(inner))
        span = pl.ds(step * chunk, chunk)
        copy = pltpu.make_async_copy(
            coupled_ref.at[span], coupled_hbm.at[span], coupled_sem.at[step]
        )
        copy.start()
        copies.append(copy)
    for k in range(levels):
        if k == 0:
            edge, low = dev_ref[0], own[:, :rank]
        else:
            edge = upper_ref[2 ** (levels - k) - 2 + (myself >> k)]
            low = factor_ref[k - 1, :, :rank]
        inner = mm(low, edge, precision=HIGH)
        fresh_ref[0, k] = mm_nt(inner, factor_ref[k, :, rank:], HIGH)
    for copy in copies:
        copy.wait()


def swaps(value, axis):
    size = lax.axis_size(axis)
    return [
        lax.ppermute(value, axis, [(source, source ^ mask) for source in range(size)])
        for mask in range(1, size)
    ]


def cost(flops, moved):
    return pl.CostEstimate(flops=flops, bytes_accessed=moved, transcendentals=0)


def per_device(
    leaf_basis, leaf_transfer, device_transfer, upper_transfer, couplings, couple_offset
):
    n_rows = lax.axis_size("rows")
    n_leaf = lax.axis_size("leaf")
    row_bits = n_rows.bit_length() - 1
    levels = row_bits + n_leaf.bit_length() - 1
    leaves, rank, _ = leaf_basis.shape
    blocks = couplings.shape[0]
    groups = rank // SUB
    params = pltpu.CompilerParams(vmem_limit_bytes=40 * 1024 * 1024)
    vmem = pl.BlockSpec(memory_space=pltpu.VMEM)
    smem = pl.BlockSpec(memory_space=pltpu.SMEM)
    hbm = pl.BlockSpec(memory_space=pltpu.HBM)
    steps = 4

    def like(array, kind=F32):
        return jax.ShapeDtypeStruct(array.shape, kind)

    def shape(*sizes, kind=F32):
        return jax.ShapeDtypeStruct(sizes, kind)

    def scratch(sets):
        return [
            pltpu.VMEM((sets, groups, rank, LANES), F32),
            pltpu.VMEM((sets, SUB, rank, LANES), F32),
        ]

    basis, trans, grams, own_gram, own_lift = pl.pallas_call(
        functools.partial(gram_kernel, steps),
        in_specs=[hbm, hbm, vmem],
        out_specs=[vmem] * 5,
        out_shape=[
            like(leaf_basis),
            like(leaf_transfer),
            shape(leaves, rank, rank),
            shape(rank, rank),
            shape(rank, rank),
        ],
        scratch_shapes=[pltpu.SemaphoreType.DMA((steps,)), pltpu.SemaphoreType.DMA((steps,))],
        compiler_params=params,
        cost_estimate=cost(10**9, 4 * 10**6),
        name="gram",
    )(leaf_basis, leaf_transfer, device_transfer)
    row_lifts = swaps(own_lift, "rows")
    factors = pl.pallas_call(
        factor_kernel,
        in_specs=[vmem],
        out_specs=vmem,
        out_shape=shape(leaves, rank, 2 * rank),
        scratch_shapes=scratch(leaves // SET),
        compiler_params=params,
        cost_estimate=cost(5 * 10**9, 8 * 10**6),
        name="factor",
    )(grams)
    sent, path = pl.pallas_call(
        functools.partial(branch_kernel, n_rows, n_leaf),
        in_specs=[vmem] * (n_rows + 2),
        out_specs=[vmem, vmem],
        out_shape=[shape(n_leaf, rank, 2 * rank), shape(row_bits, rank, rank)],
        compiler_params=params,
        name="branch",
    )(own_gram, own_lift, *row_lifts, upper_transfer)
    others = lax.all_to_all(sent, "leaf", split_axis=0, concat_axis=0, tiled=True)
    leaf_orth, moved, split = pl.pallas_call(
        functools.partial(leaf_kernel, steps),
        in_specs=[vmem] * 4,
        out_specs=[hbm, vmem, vmem],
        out_shape=[
            like(leaf_basis),
            shape(leaves, rank, 2 * rank, kind=B16),
            shape(blocks, rank, 2 * rank, kind=B16),
        ],
        scratch_shapes=[pltpu.VMEM(leaf_basis.shape, F32), pltpu.SemaphoreType.DMA((steps,))],
        compiler_params=params,
        cost_estimate=cost(5 * 10**9, 8 * 10**6),
        name="leaf",
    )(basis, trans, couplings, factors)
    sets = -(-(levels + n_leaf) // SET)
    new_transfers, leaf_bridge, coupled = pl.pallas_call(
        functools.partial(top_kernel, n_rows, n_leaf, steps),
        in_specs=[vmem] * 6 + [smem],
        out_specs=[vmem, hbm, hbm],
        out_shape=[
            shape(1, levels, rank, rank),
            like(leaf_transfer),
            like(couplings),
        ],
        scratch_shapes=[
            pltpu.VMEM((sets * SET, rank, rank), F32),
            pltpu.VMEM((sets * SET, rank, 2 * rank), F32),
            pltpu.VMEM((n_leaf, rank, 4 * rank), B16),
            pltpu.VMEM(leaf_transfer.shape, F32),
            pltpu.VMEM(couplings.shape, F32),
            pltpu.SemaphoreType.DMA((steps,)),
            pltpu.SemaphoreType.DMA((steps,)),
        ]
        + scratch(sets),
        compiler_params=params,
        name="top",
    )(others, upper_transfer, device_transfer, path, moved, split, couple_offset)
    return (leaf_orth, leaf_bridge, new_transfers, coupled)


def solution(mesh):
    in_specs = (
        P(("leaf", "rows"), None, None),
        P(("leaf", "rows"), None, None),
        P(("leaf", "rows"), None, None),
        P(),
        P(("leaf", "rows"), None, None),
        P(("leaf", "rows")),
    )
    out_specs = (
        P(("leaf", "rows"), None, None),
        P(("leaf", "rows"), None, None),
        P(("leaf", "rows"), None, None, None),
        P(("leaf", "rows"), None, None),
    )
    return jax.shard_map(
        per_device, mesh=mesh, in_specs=in_specs, out_specs=out_specs, check_vma=False
    )
```

```python
import functools

import jax
import jax.numpy as jnp
from jax import lax
from jax.experimental import pallas as pl
from jax.experimental.pallas import tpu as pltpu
from jax.sharding import PartitionSpec as P

HIGH = lax.Precision.HIGHEST
SUB = 8
LANES = 128
SET = LANES // SUB
F32 = jnp.float32
B16 = jnp.bfloat16


def mm(a, b, dims=((1,), (0,)), precision=None):
    return lax.dot_general(
        a, b, (dims, ((), ())), precision=precision, preferred_element_type=F32
    )


def mm_nt(a, b, precision=None):
    return mm(a, b, ((1,), (1,)), precision)


def mm_tn(a, b, precision=None):
    return mm(a, b, ((0,), (0,)), precision)


def lift(gram, trans):
    return mm_tn(trans, mm(gram, trans, precision=HIGH), HIGH)


def halves(x):
    high = x.astype(B16).astype(F32)
    return high, x - high


def pair(x):
    return jnp.concatenate(halves(x), axis=1).astype(B16)


def twice(x):
    return jnp.concatenate([x, x], axis=1)


def tall(x):
    high, low = halves(x)
    high, low = high.astype(B16), low.astype(B16)
    return jnp.concatenate([high, high, low, low], axis=0)


def broad(x):
    high, low = halves(x)
    return jnp.concatenate([high, high, low, low], axis=1).astype(B16)


def fold(x):
    half = x.shape[1] // 2
    return x[:, :half] + x[:, half:]


def spread(value, at):
    return jnp.broadcast_to(value[at : at + 1, :], (SUB, LANES))


def load_sets(flat, w_ref):
    sets, groups, rank = w_ref.shape[0], w_ref.shape[1], w_ref.shape[2]
    for t in range(sets):
        for ib in range(groups):
            rows = [
                flat[pl.ds(t * SET * rank + ib * SUB + s, SET, stride=rank), :]
                for s in range(SUB)
            ]
            w_ref[t, ib] = jnp.concatenate(rows, axis=0).T


def eliminate(w_ref, g_ref, out):
    sets, groups, rank = w_ref.shape[0], w_ref.shape[1], w_ref.shape[2]
    place = lax.broadcasted_iota(jnp.int32, (SUB, LANES), 0)
    lane = lax.broadcasted_iota(jnp.int32, (SUB, LANES), 1)
    group = lane // SET
    picks = [p * SET + lane % SET for p in range(SUB)]

    def tile(t, ib, jv):
        return w_ref[t, ib, pl.ds(jv * SUB, SUB), :]

    def picked(value, p):
        return jnp.take_along_axis(value, picks[p], axis=1, mode="promise_in_bounds")

    def corner(t, kb):
        diagonal = tile(t, kb, kb)
        rows = [picked(diagonal, p) for p in range(SUB)]
        inverses, roots = [], []
        for q in range(SUB):
            pivot = spread(rows[q], q)
            inverse = 1.0 / pivot
            root = lax.rsqrt(pivot)
            roots.append(root * (1.5 - 0.5 * pivot * root * root))
            inverses.append(inverse)
            scaled = rows[q] * inverse
            unit = jnp.where(place == q, 1.0, rows[q])
            for p in range(q + 1, SUB):
                kept = jnp.where(place == q, 0.0, rows[p])
                rows[p] = kept - spread(scaled, p) * unit
        return rows, inverses, roots

    def merged(parts):
        value = parts[0]
        for p in range(1, SUB):
            value = jnp.where(group == p, parts[p], value)
        return value

    def panel(t, kb, rows, inverses, roots):
        mult = {(p, q): spread(rows[p], q) for p in range(SUB) for q in range(p)}
        root = merged(roots)
        upper, lower = [], []
        for jv in range(groups):
            if jv == kb:
                for p in range(SUB):
                    unit = jnp.where(place == p, 1.0, 0.0)
                    g_ref[t, p, pl.ds(jv * SUB, SUB), :] = jnp.where(place < p, rows[p], unit)
                final = merged(rows) * root
                upper.append(jnp.where(place >= group, final, 0.0))
                unit = jnp.where(place == group, root, 0.0)
                lower.append(jnp.where(place < group, final, unit))
                continue
            value = tile(t, kb, jv)
            old = [picked(value, p) for p in range(SUB)]
            new = []
            for p in range(SUB):
                term = old[p]
                for q in range(p):
                    term = term + mult[p, q] * old[q]
                g_ref[t, p, pl.ds(jv * SUB, SUB), :] = term
                new.append(term)
            final = merged(new) * root
            zero = jnp.zeros((SUB, LANES), F32)
            upper.append(final if jv > kb else zero)
            lower.append(final if jv < kb else zero)
        return mult, jnp.concatenate(upper + lower, axis=0)

    def store(t, kb, factors):
        turned = factors.T
        for s in range(SUB):
            out[pl.ds(t * SET * rank + kb * SUB + s, SET, stride=rank), :] = turned[
                s * SET : (s + 1) * SET
            ]

    def weights(t, kb, ib, mult, inverses):
        value = tile(t, ib, kb)
        columns = [spread(value, q) for q in range(SUB)]
        found = []
        for q in range(SUB):
            term = columns[q]
            for r in range(q):
                term = term + mult[q, r] * columns[r]
            found.append(term * inverses[q])
        return found

    def trail(t, kb, ib, jv, found):
        acc = None if jv == kb else tile(t, ib, jv)
        for q in range(SUB):
            term = found[q] * g_ref[t, q, pl.ds(jv * SUB, SUB), :]
            acc = -term if acc is None else acc - term
        w_ref[t, ib, pl.ds(jv * SUB, SUB), :] = acc

    corners = [corner(t, 0) for t in range(sets)]
    for kb in range(groups):
        panels = [panel(t, kb, *corners[t]) for t in range(sets)]
        ahead = []
        if kb + 1 < groups:
            for t in range(sets):
                found = weights(t, kb, kb + 1, panels[t][0], corners[t][1])
                for jv in [kb + 1] + [jv for jv in range(groups) if jv != kb + 1]:
                    trail(t, kb, kb + 1, jv, found)
            ahead = [corner(t, kb + 1) for t in range(sets)]
        for t in range(sets):
            for ib in range(kb + 2, groups):
                found = weights(t, kb, ib, panels[t][0], corners[t][1])
                for jv in range(groups):
                    trail(t, kb, ib, jv, found)
            store(t, kb, panels[t][1])
        corners = ahead


def pack(x):
    half = x.shape[0] // 2
    return jnp.concatenate([x[:half], x[half:]], axis=1)


def unpack(x):
    half = x.shape[1] // 2
    return jnp.concatenate([x[:, :half], x[:, half:]], axis=0)


def gram_kernel(steps, sets, basis_hbm, trans_hbm, dev_ref, *refs):
    grams_refs = refs[:sets]
    own_ref, lift_ref, basis_ref, trans_ref, basis_sem, trans_sem = refs[sets:]
    leaves, rank = basis_ref.shape[0], basis_ref.shape[1]
    chunk = leaves // steps
    copies = []
    for step in range(steps):
        span = pl.ds(step * chunk, chunk)
        copies.append(
            (
                pltpu.make_async_copy(basis_hbm.at[span], basis_ref.at[span], basis_sem.at[step]),
                pltpu.make_async_copy(trans_hbm.at[span], trans_ref.at[span], trans_sem.at[step]),
            )
        )
        for copy in copies[-1]:
            copy.start()
    total = jnp.zeros((2 * rank, 2 * rank), F32)
    for step in range(steps):
        for copy in copies[step]:
            copy.wait()
        left, right = [], []
        for n in range(step * chunk, (step + 1) * chunk):
            basis = basis_ref[n]
            high, rest = halves(basis)
            middle, low = halves(rest)
            three = jnp.concatenate([high, middle, low], axis=0).astype(B16)
            product = mm_nt(three, three)
            rows = product[:rank] + product[rank : 2 * rank] + product[2 * rank :]
            gram = fold(rows[:, : 2 * rank]) + rows[:, 2 * rank :]
            grams_refs[n // SET][n % SET] = gram
            trans = pair(trans_ref[n])
            high, low = halves(gram)
            parts = mm(jnp.concatenate([high, low], axis=0).astype(B16), trans)
            left.append(trans)
            right.append(pair(fold(parts[:rank] + parts[rank:])))
        total = total + mm_tn(jnp.concatenate(left, axis=0), jnp.concatenate(right, axis=0))
    gram = fold(total[:rank] + total[rank:])
    own_ref[...] = pack(gram)
    lift_ref[...] = pack(lift(gram, dev_ref[0]))


def factor_kernel(grams_ref, after_ref, out_ref, token_ref, w_ref, g_ref):
    del after_ref
    count, rank = grams_ref.shape[0], grams_ref.shape[1]
    load_sets(grams_ref.reshape(count * rank, rank), w_ref)
    eliminate(w_ref, g_ref, out_ref.reshape(count * rank, 2 * rank))
    token_ref[...] = jnp.zeros(token_ref.shape, F32)


def row_hop_kernel(bit, last, mine_ref, got_ref, own_ref, upper_ref, path_ref, next_ref):
    n_rows, n_leaf = lax.axis_size("rows"), lax.axis_size("leaf")
    level = (n_rows * n_leaf).bit_length() - 2 - bit
    myself = lax.axis_index("leaf") * n_rows + lax.axis_index("rows")
    packed = mine_ref[...] + got_ref[...]
    path_ref[...] = packed
    lifted = pack(lift(unpack(packed), upper_ref[2**level - 2 + (myself >> (bit + 1))]))
    if last:
        next_ref[0] = lifted
        next_ref[1] = own_ref[...]
    else:
        next_ref[...] = lifted


def leaf_hop_kernel(bit, mine_ref, got_ref, upper_ref, after_ref, path_ref, next_ref):
    del after_ref
    level = lax.axis_size("leaf").bit_length() - 2 - bit
    packed = mine_ref[0] + got_ref[0]
    path_ref[...] = packed
    node = lax.axis_index("leaf") >> (bit + 1)
    next_ref[0] = pack(lift(unpack(packed), upper_ref[2**level - 2 + node]))
    count = 2**bit
    next_ref[1 : 1 + count] = mine_ref[1:]
    next_ref[1 + count :] = got_ref[1:]


def leaf_kernel(steps, sets, basis_ref, trans_ref, coup_ref, after_ref, *refs):
    del after_ref
    factor_refs = refs[:sets]
    orth_hbm, moved_ref, split_ref, orth_ref, orth_sem = refs[sets:]
    leaves, rank = basis_ref.shape[0], basis_ref.shape[1]
    chunk = leaves // steps
    lane = lax.broadcasted_iota(jnp.int32, (rank, 2 * rank), 1)
    copies = []
    for step in range(steps):
        for n in range(step * chunk, (step + 1) * chunk):
            high, low = halves(factor_refs[n // SET][n % SET])
            low = jnp.concatenate([low[:, rank:], low[:, :rank]], axis=1)
            upper = jnp.where(lane < rank, high, low).astype(B16)
            inverse = jnp.where(lane < rank, low, high).astype(B16)
            orth_ref[n] = mm(twice(inverse), tall(basis_ref[n]))
            moved_ref[n] = pair(mm(twice(upper), tall(trans_ref[n])))
            split_ref[n] = pair(coup_ref[n])
        span = pl.ds(step * chunk, chunk)
        copy = pltpu.make_async_copy(orth_ref.at[span], orth_hbm.at[span], orth_sem.at[step])
        copy.start()
        copies.append(copy)
    for copy in copies:
        copy.wait()


def top_kernel(n_rows, n_leaf, steps, mine_ref, got_ref, *refs):
    levels = (n_rows * n_leaf).bit_length() - 1
    path_refs = refs[: levels - 1]
    (
        upper_ref,
        dev_ref,
        moved_ref,
        split_ref,
        offset_ref,
        fresh_ref,
        bridge_hbm,
        coupled_hbm,
        grams_ref,
        factor_ref,
        cols_ref,
        bridge_ref,
        coupled_ref,
        bridge_sem,
        coupled_sem,
        w_ref,
        g_ref,
    ) = refs[levels - 1 :]
    rank = grams_ref.shape[1]
    branch, row = lax.axis_index("leaf"), lax.axis_index("rows")
    myself = branch * n_rows + row
    for n in range(levels - 1):
        grams_ref[n] = unpack(path_refs[n][...])
    grams_ref[levels - 1] = unpack(mine_ref[0] + got_ref[0])
    for n in range(n_leaf // 2):
        grams_ref[levels + n] = unpack(mine_ref[1 + n])
        grams_ref[levels + n_leaf // 2 + n] = unpack(got_ref[1 + n])
    count = grams_ref.shape[0]
    load_sets(grams_ref.reshape(count * rank, rank), w_ref)
    eliminate(w_ref, g_ref, factor_ref.reshape(count * rank, 2 * rank))
    own = factor_ref[levels]
    own_upper = twice(pair(own[:, :rank]))
    own_inverse = broad(own[:, rank:])
    for n in range(n_leaf):
        cols_ref[n] = broad(factor_ref[levels + n, :, :rank])
    copies = []
    leaves = moved_ref.shape[0]
    chunk = leaves // steps
    for step in range(steps):
        span = pl.ds(step * chunk, chunk)
        moved = twice(moved_ref[span].reshape(chunk * rank, 2 * rank))
        bridge_ref[span] = mm_nt(moved, own_inverse).reshape(chunk, rank, rank)
        copy = pltpu.make_async_copy(
            bridge_ref.at[span], bridge_hbm.at[span], bridge_sem.at[step]
        )
        copy.start()
        copies.append(copy)
    blocks = split_ref.shape[0]
    chunk = blocks // steps
    for step in range(steps):
        for b in range(step * chunk, (step + 1) * chunk):
            target = lax.rem(myself + offset_ref[b], n_rows * n_leaf)
            inner = mm_nt(twice(split_ref[b]), cols_ref[(target // n_rows) ^ branch])
            coupled_ref[b] = mm(own_upper, tall(inner))
        span = pl.ds(step * chunk, chunk)
        copy = pltpu.make_async_copy(
            coupled_ref.at[span], coupled_hbm.at[span], coupled_sem.at[step]
        )
        copy.start()
        copies.append(copy)
    for k in range(levels):
        if k == 0:
            edge, low = dev_ref[0], own[:, :rank]
        else:
            edge = upper_ref[2 ** (levels - k) - 2 + (myself >> k)]
            low = factor_ref[k - 1, :, :rank]
        inner = mm(low, edge, precision=HIGH)
        fresh_ref[0, k] = mm_nt(inner, factor_ref[k, :, rank:], HIGH)
    for copy in copies:
        copy.wait()


def swap(value, axis, bit):
    pairs = [(source, source ^ 2**bit) for source in range(lax.axis_size(axis))]
    return lax.ppermute(value, axis, pairs)


def cost(flops, moved):
    return pl.CostEstimate(flops=flops, bytes_accessed=moved, transcendentals=0)


def per_device(
    leaf_basis, leaf_transfer, device_transfer, upper_transfer, couplings, couple_offset
):
    n_rows = lax.axis_size("rows")
    n_leaf = lax.axis_size("leaf")
    row_bits = n_rows.bit_length() - 1
    leaf_bits = n_leaf.bit_length() - 1
    levels = row_bits + leaf_bits
    leaves, rank, _ = leaf_basis.shape
    blocks = couplings.shape[0]
    groups = rank // SUB
    params = pltpu.CompilerParams(vmem_limit_bytes=40 * 1024 * 1024)
    vmem = pl.BlockSpec(memory_space=pltpu.VMEM)
    smem = pl.BlockSpec(memory_space=pltpu.SMEM)
    hbm = pl.BlockSpec(memory_space=pltpu.HBM)
    steps = 4

    def like(array, kind=F32):
        return jax.ShapeDtypeStruct(array.shape, kind)

    def shape(*sizes, kind=F32):
        return jax.ShapeDtypeStruct(sizes, kind)

    def scratch(sets):
        return [
            pltpu.VMEM((sets, groups, rank, LANES), F32),
            pltpu.VMEM((sets, SUB, rank, LANES), F32),
        ]

    sets = leaves // SET
    half = rank // 2
    any_place = pl.BlockSpec(memory_space=pl.ANY)
    *grams, own_gram, own_lift = pl.pallas_call(
        functools.partial(gram_kernel, steps, sets),
        in_specs=[hbm, hbm, vmem],
        out_specs=[vmem] * (sets + 2),
        out_shape=[shape(SET, rank, rank)] * sets + [shape(half, 2 * rank)] * 2,
        scratch_shapes=[
            pltpu.VMEM(leaf_basis.shape, F32),
            pltpu.VMEM(leaf_transfer.shape, F32),
            pltpu.SemaphoreType.DMA((steps,)),
            pltpu.SemaphoreType.DMA((steps,)),
        ],
        compiler_params=pltpu.CompilerParams(vmem_limit_bytes=52 * 1024 * 1024),
        cost_estimate=cost(10**9, 4 * 10**6),
        name="gram",
    )(leaf_basis, leaf_transfer, device_transfer)
    path = []
    carry = own_lift
    for bit in range(row_bits):
        got = swap(carry, "rows", bit)
        last = bit == row_bits - 1
        gram, carry = pl.pallas_call(
            functools.partial(row_hop_kernel, bit, last),
            in_specs=[vmem] * 4,
            out_specs=[vmem, vmem],
            out_shape=[shape(half, 2 * rank), shape(*((2,) if last else ()), half, 2 * rank)],
            compiler_params=params,
            name="row_hop",
        )(carry, got, own_gram, upper_transfer)
        path.append(gram)
    factors = []
    for bit in range(leaf_bits - 1):
        got = swap(carry, "leaf", bit)
        if len(factors) < sets:
            factor, token = pl.pallas_call(
                factor_kernel,
                in_specs=[vmem, any_place],
                out_specs=[vmem, vmem],
                out_shape=[shape(SET, rank, 2 * rank), shape(SUB, LANES)],
                scratch_shapes=scratch(1),
                compiler_params=params,
                cost_estimate=cost(5 * 10**9, 8 * 10**6),
                name="factor",
            )(grams[len(factors)], carry)
            factors.append(factor)
        gram, carry = pl.pallas_call(
            functools.partial(leaf_hop_kernel, bit),
            in_specs=[vmem] * 3 + [any_place],
            out_specs=[vmem, vmem],
            out_shape=[shape(half, 2 * rank), shape(1 + 2 ** (bit + 1), half, 2 * rank)],
            compiler_params=params,
            name="leaf_hop",
        )(carry, got, upper_transfer, token)
        path.append(gram)
    got = swap(carry, "leaf", leaf_bits - 1)
    leaf_orth, moved, split = pl.pallas_call(
        functools.partial(leaf_kernel, steps, sets),
        in_specs=[vmem] * 3 + [any_place] + [vmem] * sets,
        out_specs=[hbm, vmem, vmem],
        out_shape=[
            like(leaf_basis),
            shape(leaves, rank, 2 * rank, kind=B16),
            shape(blocks, rank, 2 * rank, kind=B16),
        ],
        scratch_shapes=[pltpu.VMEM(leaf_basis.shape, F32), pltpu.SemaphoreType.DMA((steps,))],
        compiler_params=params,
        cost_estimate=cost(5 * 10**9, 8 * 10**6),
        name="leaf",
    )(leaf_basis, leaf_transfer, couplings, carry, *factors)
    sets = -(-(levels + n_leaf) // SET)
    new_transfers, leaf_bridge, coupled = pl.pallas_call(
        functools.partial(top_kernel, n_rows, n_leaf, steps),
        in_specs=[vmem] * (levels + 5) + [smem],
        out_specs=[vmem, hbm, hbm],
        out_shape=[
            shape(1, levels, rank, rank),
            like(leaf_transfer),
            like(couplings),
        ],
        scratch_shapes=[
            pltpu.VMEM((sets * SET, rank, rank), F32),
            pltpu.VMEM((sets * SET, rank, 2 * rank), F32),
            pltpu.VMEM((n_leaf, rank, 4 * rank), B16),
            pltpu.VMEM(leaf_transfer.shape, F32),
            pltpu.VMEM(couplings.shape, F32),
            pltpu.SemaphoreType.DMA((steps,)),
            pltpu.SemaphoreType.DMA((steps,)),
        ]
        + scratch(sets),
        compiler_params=params,
        name="top",
    )(carry, got, *path, upper_transfer, device_transfer, moved, split, couple_offset)
    return (leaf_orth, leaf_bridge, new_transfers, coupled)


def solution(mesh):
    in_specs = (
        P(("leaf", "rows"), None, None),
        P(("leaf", "rows"), None, None),
        P(("leaf", "rows"), None, None),
        P(),
        P(("leaf", "rows"), None, None),
        P(("leaf", "rows")),
    )
    out_specs = (
        P(("leaf", "rows"), None, None),
        P(("leaf", "rows"), None, None),
        P(("leaf", "rows"), None, None, None),
        P(("leaf", "rows"), None, None),
    )
    return jax.shard_map(
        per_device, mesh=mesh, in_specs=in_specs, out_specs=out_specs, check_vma=False
    )
```

```python
import functools

import jax
import jax.numpy as jnp
from jax import lax
from jax.experimental import pallas as pl
from jax.experimental.pallas import tpu as pltpu
from jax.sharding import PartitionSpec as P

HIGH = lax.Precision.HIGHEST
SUB = 8
LANES = 128
SET = LANES // SUB
GROUP = 4
F32 = jnp.float32
B16 = jnp.bfloat16


def mm(a, b, dims=((1,), (0,)), precision=None):
    return lax.dot_general(
        a, b, (dims, ((), ())), precision=precision, preferred_element_type=F32
    )


def mm_nt(a, b, precision=None):
    return mm(a, b, ((1,), (1,)), precision)


def mm_tn(a, b, precision=None):
    return mm(a, b, ((0,), (0,)), precision)


def lift(gram, trans):
    return mm_tn(trans, mm(gram, trans, precision=HIGH), HIGH)


def halves(x):
    high = x.astype(B16).astype(F32)
    return high, x - high


def pair(x):
    return jnp.concatenate(halves(x), axis=1).astype(B16)


def twice(x):
    return jnp.concatenate([x, x], axis=1)


def tall(x):
    high, low = halves(x)
    high, low = high.astype(B16), low.astype(B16)
    return jnp.concatenate([high, high, low, low], axis=0)


def broad(x):
    high, low = halves(x)
    return jnp.concatenate([high, high, low, low], axis=1).astype(B16)


def fold(x):
    half = x.shape[1] // 2
    return x[:, :half] + x[:, half:]


def spread(value, at):
    return jnp.broadcast_to(value[at : at + 1, :], (SUB, LANES))


def load_sets(flat, w_ref):
    sets, groups, rank = w_ref.shape[0], w_ref.shape[1], w_ref.shape[2]
    for t in range(sets):
        for ib in range(groups):
            rows = [
                flat[pl.ds(t * SET * rank + ib * SUB + s, SET, stride=rank), :]
                for s in range(SUB)
            ]
            w_ref[t, ib] = jnp.concatenate(rows, axis=0).T


def eliminate(w_ref, g_ref, out):
    sets, groups, rank = w_ref.shape[0], w_ref.shape[1], w_ref.shape[2]
    place = lax.broadcasted_iota(jnp.int32, (SUB, LANES), 0)
    lane = lax.broadcasted_iota(jnp.int32, (SUB, LANES), 1)
    group = lane // SET
    picks = [p * SET + lane % SET for p in range(SUB)]

    def tile(t, ib, jv):
        return w_ref[t, ib, pl.ds(jv * SUB, SUB), :]

    def picked(value, p):
        return jnp.take_along_axis(value, picks[p], axis=1, mode="promise_in_bounds")

    def corner(t, kb):
        diagonal = tile(t, kb, kb)
        rows = [picked(diagonal, p) for p in range(SUB)]
        inverses, roots = [], []
        for q in range(SUB):
            pivot = spread(rows[q], q)
            inverse = 1.0 / pivot
            root = lax.rsqrt(pivot)
            roots.append(root * (1.5 - 0.5 * pivot * root * root))
            inverses.append(inverse)
            scaled = rows[q] * inverse
            unit = jnp.where(place == q, 1.0, rows[q])
            for p in range(q + 1, SUB):
                kept = jnp.where(place == q, 0.0, rows[p])
                rows[p] = kept - spread(scaled, p) * unit
        return rows, inverses, roots

    def merged(parts):
        value = parts[0]
        for p in range(1, SUB):
            value = jnp.where(group == p, parts[p], value)
        return value

    def panel(t, kb, rows, inverses, roots):
        mult = {(p, q): spread(rows[p], q) for p in range(SUB) for q in range(p)}
        root = merged(roots)
        upper, lower = [], []
        for jv in range(groups):
            if jv == kb:
                for p in range(SUB):
                    unit = jnp.where(place == p, 1.0, 0.0)
                    g_ref[t, p, pl.ds(jv * SUB, SUB), :] = jnp.where(place < p, rows[p], unit)
                final = merged(rows) * root
                upper.append(jnp.where(place >= group, final, 0.0))
                unit = jnp.where(place == group, root, 0.0)
                lower.append(jnp.where(place < group, final, unit))
                continue
            value = tile(t, kb, jv)
            old = [picked(value, p) for p in range(SUB)]
            new = []
            for p in range(SUB):
                term = old[p]
                for q in range(p):
                    term = term + mult[p, q] * old[q]
                g_ref[t, p, pl.ds(jv * SUB, SUB), :] = term
                new.append(term)
            final = merged(new) * root
            zero = jnp.zeros((SUB, LANES), F32)
            upper.append(final if jv > kb else zero)
            lower.append(final if jv < kb else zero)
        return mult, jnp.concatenate(upper + lower, axis=0)

    def store(t, kb, factors):
        turned = factors.T
        for s in range(SUB):
            out[pl.ds(t * SET * rank + kb * SUB + s, SET, stride=rank), :] = turned[
                s * SET : (s + 1) * SET
            ]

    def weights(t, kb, ib, mult, inverses):
        value = tile(t, ib, kb)
        columns = [spread(value, q) for q in range(SUB)]
        found = []
        for q in range(SUB):
            term = columns[q]
            for r in range(q):
                term = term + mult[q, r] * columns[r]
            found.append(term * inverses[q])
        return found

    def trail(t, kb, ib, jv, found):
        acc = None if jv == kb else tile(t, ib, jv)
        for q in range(SUB):
            term = found[q] * g_ref[t, q, pl.ds(jv * SUB, SUB), :]
            acc = -term if acc is None else acc - term
        w_ref[t, ib, pl.ds(jv * SUB, SUB), :] = acc

    corners = [corner(t, 0) for t in range(sets)]
    for kb in range(groups):
        panels = [panel(t, kb, *corners[t]) for t in range(sets)]
        ahead = []
        if kb + 1 < groups:
            for t in range(sets):
                found = weights(t, kb, kb + 1, panels[t][0], corners[t][1])
                for jv in [kb + 1] + [jv for jv in range(groups) if jv != kb + 1]:
                    trail(t, kb, kb + 1, jv, found)
            ahead = [corner(t, kb + 1) for t in range(sets)]
        for t in range(sets):
            for ib in range(kb + 2, groups):
                found = weights(t, kb, ib, panels[t][0], corners[t][1])
                for jv in range(groups):
                    trail(t, kb, ib, jv, found)
            store(t, kb, panels[t][1])
        corners = ahead


def pack(x):
    half = x.shape[0] // 2
    return jnp.concatenate([x[:half], x[half:]], axis=1)


def unpack(x):
    half = x.shape[1] // 2
    return jnp.concatenate([x[:, :half], x[:, half:]], axis=0)


def gram_kernel(steps, sets, basis_hbm, trans_hbm, dev_ref, *refs):
    grams_refs = refs[:sets]
    own_ref, lift_ref, basis_ref, trans_ref, basis_sem, trans_sem = refs[sets:]
    leaves, rank = basis_ref.shape[0], basis_ref.shape[1]
    chunk = leaves // steps
    copies = []
    for step in range(steps):
        span = pl.ds(step * chunk, chunk)
        copies.append(
            (
                pltpu.make_async_copy(basis_hbm.at[span], basis_ref.at[span], basis_sem.at[step]),
                pltpu.make_async_copy(trans_hbm.at[span], trans_ref.at[span], trans_sem.at[step]),
            )
        )
        for copy in copies[-1]:
            copy.start()
    total = jnp.zeros((2 * rank, 2 * rank), F32)
    for step in range(steps):
        for copy in copies[step]:
            copy.wait()
        left, right = [], []
        for first in range(step * chunk, (step + 1) * chunk, GROUP):
            span = range(first, first + GROUP)
            threes = []
            for n in span:
                high, rest = halves(basis_ref[n])
                middle, low = halves(rest)
                threes.append(jnp.concatenate([high, middle, low], axis=0).astype(B16))
            products = [mm_nt(three, three) for three in threes]
            grams = []
            for n, product in zip(span, products):
                rows = product[:rank] + product[rank : 2 * rank] + product[2 * rank :]
                gram = fold(rows[:, : 2 * rank]) + rows[:, 2 * rank :]
                grams_refs[n // SET][n % SET] = gram
                grams.append(jnp.concatenate(halves(gram), axis=0).astype(B16))
            trans = [pair(trans_ref[n]) for n in span]
            parts = [mm(gram, edge) for gram, edge in zip(grams, trans)]
            left += trans
            right += [pair(fold(part[:rank] + part[rank:])) for part in parts]
        total = total + mm_tn(jnp.concatenate(left, axis=0), jnp.concatenate(right, axis=0))
    gram = fold(total[:rank] + total[rank:])
    own_ref[...] = pack(gram)
    lift_ref[...] = pack(lift(gram, dev_ref[0]))


def factor_kernel(grams_ref, after_ref, out_ref, token_ref, w_ref, g_ref):
    del after_ref
    count, rank = grams_ref.shape[0], grams_ref.shape[1]
    load_sets(grams_ref.reshape(count * rank, rank), w_ref)
    eliminate(w_ref, g_ref, out_ref.reshape(count * rank, 2 * rank))
    token_ref[...] = jnp.zeros(token_ref.shape, F32)


def row_hop_kernel(bit, last, mine_ref, got_ref, own_ref, upper_ref, path_ref, next_ref):
    n_rows, n_leaf = lax.axis_size("rows"), lax.axis_size("leaf")
    level = (n_rows * n_leaf).bit_length() - 2 - bit
    myself = lax.axis_index("leaf") * n_rows + lax.axis_index("rows")
    packed = mine_ref[...] + got_ref[...]
    path_ref[...] = packed
    lifted = pack(lift(unpack(packed), upper_ref[2**level - 2 + (myself >> (bit + 1))]))
    if last:
        half = lifted.shape[0]
        next_ref[:half] = lifted
        next_ref[half:] = own_ref[...]
    else:
        next_ref[...] = lifted


def packed_places(half):
    row = lax.broadcasted_iota(jnp.int32, (half, 4 * half), 0)
    lane = lax.broadcasted_iota(jnp.int32, (half, 4 * half), 1)
    return jnp.where(lane < 2 * half, row, row + half), lane % (2 * half)


def join(a, b):
    half = a.shape[0]
    row, column = packed_places(half)
    diagonal = jnp.sum(jnp.where(row == column, a, 0.0), axis=0, keepdims=True)
    joint = jnp.where(row > column, a, b)
    return jnp.concatenate([joint, jnp.broadcast_to(diagonal, (SUB, 4 * half))], axis=0)


def part(x):
    half = x.shape[0] - SUB
    joint = unpack(x[:half])
    turned = joint.T
    row = lax.broadcasted_iota(jnp.int32, joint.shape, 0)
    column = lax.broadcasted_iota(jnp.int32, joint.shape, 1)
    diagonal = jnp.broadcast_to(fold(x[half : half + 1]), joint.shape)
    first = jnp.where(row > column, joint, jnp.where(row == column, diagonal, turned))
    return first, jnp.where(row <= column, joint, turned)


def leaf_hop_kernel(bit, mine_ref, got_ref, upper_ref, after_ref, path_ref, next_ref):
    del after_ref
    half = path_ref.shape[0]
    level = lax.axis_size("leaf").bit_length() - 2 - bit
    packed = mine_ref[:half] + got_ref[:half]
    path_ref[...] = packed
    node = lax.axis_index("leaf") >> (bit + 1)
    next_ref[:half] = pack(lift(unpack(packed), upper_ref[2**level - 2 + node]))
    if bit == 0:
        next_ref[half:] = join(mine_ref[half:], got_ref[half:])
    else:
        size = mine_ref.shape[0] - half
        next_ref[half : half + size] = mine_ref[half:]
        next_ref[half + size :] = got_ref[half:]


def leaf_kernel(steps, sets, basis_ref, trans_ref, coup_ref, after_ref, *refs):
    del after_ref
    factor_refs = refs[:sets]
    orth_hbm, moved_ref, split_ref, orth_ref, orth_sem = refs[sets:]
    leaves, rank = basis_ref.shape[0], basis_ref.shape[1]
    chunk = leaves // steps
    lane = lax.broadcasted_iota(jnp.int32, (rank, 2 * rank), 1)
    copies = []
    for step in range(steps):
        for n in range(step * chunk, (step + 1) * chunk):
            high, low = halves(factor_refs[n // SET][n % SET])
            low = jnp.concatenate([low[:, rank:], low[:, :rank]], axis=1)
            upper = jnp.where(lane < rank, high, low).astype(B16)
            inverse = jnp.where(lane < rank, low, high).astype(B16)
            orth_ref[n] = mm(twice(inverse), tall(basis_ref[n]))
            moved_ref[n] = pair(mm(twice(upper), tall(trans_ref[n])))
            split_ref[n] = pair(coup_ref[n])
        span = pl.ds(step * chunk, chunk)
        copy = pltpu.make_async_copy(orth_ref.at[span], orth_hbm.at[span], orth_sem.at[step])
        copy.start()
        copies.append(copy)
    for copy in copies:
        copy.wait()


def top_kernel(n_rows, n_leaf, steps, mine_ref, got_ref, *refs):
    levels = (n_rows * n_leaf).bit_length() - 1
    path_refs = refs[: levels - 1]
    (
        upper_ref,
        dev_ref,
        moved_ref,
        split_ref,
        offset_ref,
        fresh_hbm,
        bridge_hbm,
        coupled_hbm,
        grams_ref,
        factor_ref,
        cols_ref,
        fresh_ref,
        bridge_ref,
        coupled_ref,
        fresh_sem,
        bridge_sem,
        coupled_sem,
        w_ref,
        g_ref,
    ) = refs[levels - 1 :]
    rank = grams_ref.shape[1]
    branch, row = lax.axis_index("leaf"), lax.axis_index("rows")
    myself = branch * n_rows + row
    for n in range(levels - 1):
        grams_ref[n] = unpack(path_refs[n][...])
    half = rank // 2
    grams_ref[levels - 1] = unpack(mine_ref[:half] + got_ref[:half])
    pairs = n_leaf // 4
    for n in range(pairs):
        for place, ref in ((0, mine_ref), (pairs, got_ref)):
            joint = ref[pl.ds(half + n * (half + SUB), half + SUB), :]
            at = levels + 2 * (place + n)
            grams_ref[at], grams_ref[at + 1] = part(joint)
    count = grams_ref.shape[0]
    load_sets(grams_ref.reshape(count * rank, rank), w_ref)
    eliminate(w_ref, g_ref, factor_ref.reshape(count * rank, 2 * rank))
    own = factor_ref[levels]
    own_upper = twice(pair(own[:, :rank]))
    own_inverse = broad(own[:, rank:])
    for n in range(n_leaf):
        cols_ref[n] = broad(factor_ref[levels + n, :, :rank])
    copies = []

    def send(source, target, sem):
        copies.append(pltpu.make_async_copy(source, target, sem))
        copies[-1].start()

    lows, edges, inverses = [own_upper], [tall(dev_ref[0])], []
    for k in range(levels):
        inverses.append(broad(factor_ref[k, :, rank:]))
        if k:
            lows.append(twice(pair(factor_ref[k - 1, :, :rank])))
            edges.append(tall(upper_ref[2 ** (levels - k) - 2 + (myself >> k)]))
    inner = [mm(low, edge) for low, edge in zip(lows, edges)]
    inner = [twice(pair(value)) for value in inner]
    for k in range(levels):
        fresh_ref[0, k] = mm_nt(inner[k], inverses[k])
    send(fresh_ref, fresh_hbm, fresh_sem)
    leaves = moved_ref.shape[0]
    chunk = leaves // steps
    for step in range(steps):
        span = pl.ds(step * chunk, chunk)
        moved = twice(moved_ref[span].reshape(chunk * rank, 2 * rank))
        bridge_ref[span] = mm_nt(moved, own_inverse).reshape(chunk, rank, rank)
        send(bridge_ref.at[span], bridge_hbm.at[span], bridge_sem.at[step])
    blocks = split_ref.shape[0]
    chunk = blocks // steps
    for step in range(steps):
        inner = []
        for b in range(step * chunk, (step + 1) * chunk):
            target = lax.rem(myself + offset_ref[b], n_rows * n_leaf)
            column = cols_ref[(target // n_rows) ^ branch]
            inner.append(mm_nt(twice(split_ref[b]), column))
        inner = [tall(value) for value in inner]
        for n in range(chunk):
            coupled_ref[step * chunk + n] = mm(own_upper, inner[n])
        span = pl.ds(step * chunk, chunk)
        send(coupled_ref.at[span], coupled_hbm.at[span], coupled_sem.at[step])
    for copy in copies:
        copy.wait()


def swap(value, axis, bit):
    pairs = [(source, source ^ 2**bit) for source in range(lax.axis_size(axis))]
    return lax.ppermute(value, axis, pairs)


def cost(flops, moved):
    return pl.CostEstimate(flops=flops, bytes_accessed=moved, transcendentals=0)


def per_device(
    leaf_basis, leaf_transfer, device_transfer, upper_transfer, couplings, couple_offset
):
    n_rows = lax.axis_size("rows")
    n_leaf = lax.axis_size("leaf")
    row_bits = n_rows.bit_length() - 1
    leaf_bits = n_leaf.bit_length() - 1
    levels = row_bits + leaf_bits
    leaves, rank, _ = leaf_basis.shape
    blocks = couplings.shape[0]
    groups = rank // SUB
    params = pltpu.CompilerParams(vmem_limit_bytes=40 * 1024 * 1024)
    vmem = pl.BlockSpec(memory_space=pltpu.VMEM)
    smem = pl.BlockSpec(memory_space=pltpu.SMEM)
    hbm = pl.BlockSpec(memory_space=pltpu.HBM)
    steps = 4

    def like(array, kind=F32):
        return jax.ShapeDtypeStruct(array.shape, kind)

    def shape(*sizes, kind=F32):
        return jax.ShapeDtypeStruct(sizes, kind)

    def scratch(sets):
        return [
            pltpu.VMEM((sets, groups, rank, LANES), F32),
            pltpu.VMEM((sets, SUB, rank, LANES), F32),
        ]

    sets = leaves // SET
    half = rank // 2
    any_place = pl.BlockSpec(memory_space=pl.ANY)
    *grams, own_gram, own_lift = pl.pallas_call(
        functools.partial(gram_kernel, steps, sets),
        in_specs=[hbm, hbm, vmem],
        out_specs=[vmem] * (sets + 2),
        out_shape=[shape(SET, rank, rank)] * sets + [shape(half, 2 * rank)] * 2,
        scratch_shapes=[
            pltpu.VMEM(leaf_basis.shape, F32),
            pltpu.VMEM(leaf_transfer.shape, F32),
            pltpu.SemaphoreType.DMA((steps,)),
            pltpu.SemaphoreType.DMA((steps,)),
        ],
        compiler_params=pltpu.CompilerParams(vmem_limit_bytes=52 * 1024 * 1024),
        cost_estimate=cost(10**9, 4 * 10**6),
        name="gram",
    )(leaf_basis, leaf_transfer, device_transfer)
    path = []
    carry = own_lift
    for bit in range(row_bits):
        got = swap(carry, "rows", bit)
        last = bit == row_bits - 1
        gram, carry = pl.pallas_call(
            functools.partial(row_hop_kernel, bit, last),
            in_specs=[vmem] * 4,
            out_specs=[vmem, vmem],
            out_shape=[shape(half, 2 * rank), shape(rank if last else half, 2 * rank)],
            compiler_params=params,
            name="row_hop",
        )(carry, got, own_gram, upper_transfer)
        path.append(gram)
    factors = []
    for bit in range(leaf_bits - 1):
        got = swap(carry, "leaf", bit)
        if len(factors) < sets:
            factor, token = pl.pallas_call(
                factor_kernel,
                in_specs=[vmem, any_place],
                out_specs=[vmem, vmem],
                out_shape=[shape(SET, rank, 2 * rank), shape(SUB, LANES)],
                scratch_shapes=scratch(1),
                compiler_params=params,
                cost_estimate=cost(5 * 10**9, 8 * 10**6),
                name="factor",
            )(grams[len(factors)], carry)
            factors.append(factor)
        gram, carry = pl.pallas_call(
            functools.partial(leaf_hop_kernel, bit),
            in_specs=[vmem] * 3 + [any_place],
            out_specs=[vmem, vmem],
            out_shape=[shape(half, 2 * rank), shape(half + (half + SUB) * 2**bit, 2 * rank)],
            compiler_params=params,
            name="leaf_hop",
        )(carry, got, upper_transfer, token)
        path.append(gram)
    got = swap(carry, "leaf", leaf_bits - 1)
    leaf_orth, moved, split = pl.pallas_call(
        functools.partial(leaf_kernel, steps, sets),
        in_specs=[vmem] * 3 + [any_place] + [vmem] * sets,
        out_specs=[hbm, vmem, vmem],
        out_shape=[
            like(leaf_basis),
            shape(leaves, rank, 2 * rank, kind=B16),
            shape(blocks, rank, 2 * rank, kind=B16),
        ],
        scratch_shapes=[pltpu.VMEM(leaf_basis.shape, F32), pltpu.SemaphoreType.DMA((steps,))],
        compiler_params=params,
        cost_estimate=cost(5 * 10**9, 8 * 10**6),
        name="leaf",
    )(leaf_basis, leaf_transfer, couplings, carry, *factors)
    sets = -(-(levels + n_leaf) // SET)
    new_transfers, leaf_bridge, coupled = pl.pallas_call(
        functools.partial(top_kernel, n_rows, n_leaf, steps),
        in_specs=[vmem] * (levels + 5) + [smem],
        out_specs=[hbm, hbm, hbm],
        out_shape=[
            shape(1, levels, rank, rank),
            like(leaf_transfer),
            like(couplings),
        ],
        scratch_shapes=[
            pltpu.VMEM((sets * SET, rank, rank), F32),
            pltpu.VMEM((sets * SET, rank, 2 * rank), F32),
            pltpu.VMEM((n_leaf, rank, 4 * rank), B16),
            pltpu.VMEM((1, levels, rank, rank), F32),
            pltpu.VMEM(leaf_transfer.shape, F32),
            pltpu.VMEM(couplings.shape, F32),
            pltpu.SemaphoreType.DMA(()),
            pltpu.SemaphoreType.DMA((steps,)),
            pltpu.SemaphoreType.DMA((steps,)),
        ]
        + scratch(sets),
        compiler_params=params,
        name="top",
    )(carry, got, *path, upper_transfer, device_transfer, moved, split, couple_offset)
    return (leaf_orth, leaf_bridge, new_transfers, coupled)


def solution(mesh):
    in_specs = (
        P(("leaf", "rows"), None, None),
        P(("leaf", "rows"), None, None),
        P(("leaf", "rows"), None, None),
        P(),
        P(("leaf", "rows"), None, None),
        P(("leaf", "rows")),
    )
    out_specs = (
        P(("leaf", "rows"), None, None),
        P(("leaf", "rows"), None, None),
        P(("leaf", "rows"), None, None, None),
        P(("leaf", "rows"), None, None),
    )
    return jax.shard_map(
        per_device, mesh=mesh, in_specs=in_specs, out_specs=out_specs, check_vma=False
    )
```

```python
import functools

import jax
import jax.numpy as jnp
from jax import lax
from jax.experimental import pallas as pl
from jax.experimental.pallas import tpu as pltpu
from jax.sharding import PartitionSpec as P

HIGH = lax.Precision.HIGHEST
SUB = 8
LANES = 128
SET = LANES // SUB
GROUP = 4
F32 = jnp.float32
B16 = jnp.bfloat16


def mm(a, b, dims=((1,), (0,)), precision=None):
    return lax.dot_general(
        a, b, (dims, ((), ())), precision=precision, preferred_element_type=F32
    )


def mm_nt(a, b, precision=None):
    return mm(a, b, ((1,), (1,)), precision)


def mm_tn(a, b, precision=None):
    return mm(a, b, ((0,), (0,)), precision)


def lift(gram, trans):
    return mm_tn(trans, mm(gram, trans, precision=HIGH), HIGH)


def halves(x):
    high = x.astype(B16).astype(F32)
    return high, x - high


def pair(x):
    return jnp.concatenate(halves(x), axis=1).astype(B16)


def twice(x):
    return jnp.concatenate([x, x], axis=1)


def tall(x):
    high, low = halves(x)
    high, low = high.astype(B16), low.astype(B16)
    return jnp.concatenate([high, high, low, low], axis=0)


def broad(x):
    high, low = halves(x)
    return jnp.concatenate([high, high, low, low], axis=1).astype(B16)


def fold(x):
    half = x.shape[1] // 2
    return x[:, :half] + x[:, half:]


def spread(value, at):
    return jnp.broadcast_to(value[at : at + 1, :], (SUB, LANES))


def added(terms):
    while len(terms) > 1:
        terms = [sum(terms[n : n + 2][1:], terms[n]) for n in range(0, len(terms), 2)]
    return terms[0]


def load_sets(flat, w_ref):
    sets, groups, rank = w_ref.shape[0], w_ref.shape[1], w_ref.shape[2]
    for t in range(sets):
        for ib in range(groups):
            rows = [
                flat[pl.ds(t * SET * rank + ib * SUB + s, SET, stride=rank), :]
                for s in range(SUB)
            ]
            w_ref[t, ib] = jnp.concatenate(rows, axis=0).T


def eliminate(w_ref, g_ref, out):
    sets, groups, rank = w_ref.shape[0], w_ref.shape[1], w_ref.shape[2]
    place = lax.broadcasted_iota(jnp.int32, (SUB, LANES), 0)
    lane = lax.broadcasted_iota(jnp.int32, (SUB, LANES), 1)
    group = lane // SET
    picks = [p * SET + lane % SET for p in range(SUB)]

    def tile(t, ib, jv):
        return w_ref[t, ib, pl.ds(jv * SUB, SUB), :]

    def picked(value, p):
        return jnp.take_along_axis(value, picks[p], axis=1, mode="promise_in_bounds")

    def corner(t, kb):
        diagonal = tile(t, kb, kb)
        rows = [picked(diagonal, p) for p in range(SUB)]
        pivot = spread(rows[0], 0)
        inverses, roots = [], []
        for q in range(SUB):
            unit = jnp.where(place == q, 1.0, rows[q])
            sides = {p: spread(rows[q], p) for p in range(q + 1, SUB)}
            inverse = pl.reciprocal(pivot, approx=True)
            inverses.append(inverse)
            roots.append(lax.rsqrt(pivot))
            if q + 1 < SUB:
                pivot = spread(rows[q + 1], q + 1) - sides[q + 1] * sides[q + 1] * inverse
            for p in range(q + 1, SUB):
                kept = jnp.where(place == q, 0.0, rows[p])
                rows[p] = kept - (sides[p] * unit) * inverse
        return rows, inverses, roots

    def merged(parts):
        value = parts[0]
        for p in range(1, SUB):
            value = jnp.where(group == p, parts[p], value)
        return value

    def panel(t, kb, rows, inverses, roots):
        mult = {(p, q): spread(rows[p], q) for p in range(SUB) for q in range(p)}
        root = merged(roots)
        upper, lower = [], []
        for jv in range(groups):
            if jv == kb:
                for p in range(SUB):
                    unit = jnp.where(place == p, 1.0, 0.0)
                    g_ref[t, p, pl.ds(jv * SUB, SUB), :] = jnp.where(place < p, rows[p], unit)
                final = merged(rows) * root
                upper.append(jnp.where(place >= group, final, 0.0))
                unit = jnp.where(place == group, root, 0.0)
                lower.append(jnp.where(place < group, final, unit))
                continue
            value = tile(t, kb, jv)
            old = [picked(value, p) for p in range(SUB)]
            new = []
            for p in range(SUB):
                term = added([old[p]] + [mult[p, q] * old[q] for q in range(p)])
                g_ref[t, p, pl.ds(jv * SUB, SUB), :] = term
                new.append(term)
            final = merged(new) * root
            zero = jnp.zeros((SUB, LANES), F32)
            upper.append(final if jv > kb else zero)
            lower.append(final if jv < kb else zero)
        return mult, jnp.concatenate(upper + lower, axis=0)

    def store(t, kb, factors):
        turned = factors.T
        for s in range(SUB):
            out[pl.ds(t * SET * rank + kb * SUB + s, SET, stride=rank), :] = turned[
                s * SET : (s + 1) * SET
            ]

    def weights(t, kb, ib, mult, inverses):
        value = tile(t, ib, kb)
        columns = [spread(value, q) for q in range(SUB)]
        found = []
        for q in range(SUB):
            term = added([columns[q]] + [mult[q, r] * columns[r] for r in range(q)])
            found.append(term * inverses[q])
        return found

    def trail(t, kb, ib, jv, found):
        terms = [found[q] * g_ref[t, q, pl.ds(jv * SUB, SUB), :] for q in range(SUB)]
        acc = -added(terms) if jv == kb else tile(t, ib, jv) - added(terms)
        w_ref[t, ib, pl.ds(jv * SUB, SUB), :] = acc

    corners = [corner(t, 0) for t in range(sets)]
    for kb in range(groups):
        panels = [panel(t, kb, *corners[t]) for t in range(sets)]
        ahead = []
        if kb + 1 < groups:
            for t in range(sets):
                found = weights(t, kb, kb + 1, panels[t][0], corners[t][1])
                for jv in [kb + 1] + [jv for jv in range(groups) if jv != kb + 1]:
                    trail(t, kb, kb + 1, jv, found)
            ahead = [corner(t, kb + 1) for t in range(sets)]
        for t in range(sets):
            for ib in range(kb + 2, groups):
                found = weights(t, kb, ib, panels[t][0], corners[t][1])
                for jv in range(groups):
                    trail(t, kb, ib, jv, found)
            store(t, kb, panels[t][1])
        corners = ahead


def pack(x):
    half = x.shape[0] // 2
    return jnp.concatenate([x[:half], x[half:]], axis=1)


def unpack(x):
    half = x.shape[1] // 2
    return jnp.concatenate([x[:, :half], x[:, half:]], axis=0)


def gram_kernel(steps, sets, basis_hbm, trans_hbm, dev_ref, *refs):
    grams_refs = refs[:sets]
    own_ref, lift_ref, basis_ref, trans_ref, basis_sem, trans_sem = refs[sets:]
    leaves, rank = basis_ref.shape[0], basis_ref.shape[1]
    chunk = leaves // steps
    copies = []
    for step in range(steps):
        span = pl.ds(step * chunk, chunk)
        copies.append(
            (
                pltpu.make_async_copy(basis_hbm.at[span], basis_ref.at[span], basis_sem.at[step]),
                pltpu.make_async_copy(trans_hbm.at[span], trans_ref.at[span], trans_sem.at[step]),
            )
        )
        for copy in copies[-1]:
            copy.start()
    groups = leaves // GROUP
    products, parts, edges, rights = {}, {}, {}, {}
    total = None
    for stage in range(groups + 3):
        if stage < groups:
            if stage * GROUP % chunk == 0:
                for copy in copies[stage * GROUP // chunk]:
                    copy.wait()
            threes = []
            for n in range(stage * GROUP, (stage + 1) * GROUP):
                high, rest = halves(basis_ref[n])
                middle, low = halves(rest)
                threes.append(jnp.concatenate([high, middle, low], axis=0).astype(B16))
            products[stage] = [mm_nt(three, three) for three in threes]
        group = stage - 1
        if 0 <= group < groups:
            edges[group] = [
                pair(trans_ref[n]) for n in range(group * GROUP, (group + 1) * GROUP)
            ]
            parts[group] = []
            for n, product in enumerate(products.pop(group)):
                rows = product[:rank] + product[rank : 2 * rank] + product[2 * rank :]
                gram = fold(rows[:, : 2 * rank]) + rows[:, 2 * rank :]
                at = group * GROUP + n
                grams_refs[at // SET][at % SET] = gram
                both = jnp.concatenate(halves(gram), axis=0).astype(B16)
                parts[group].append(mm(both, edges[group][n]))
        group = stage - 2
        if 0 <= group < groups:
            rights[group] = [pair(fold(part[:rank] + part[rank:])) for part in parts.pop(group)]
        group = stage - 3
        if 0 <= group < groups and group % 2:
            left = jnp.concatenate(edges.pop(group - 1) + edges.pop(group), axis=0)
            right = jnp.concatenate(rights.pop(group - 1) + rights.pop(group), axis=0)
            term = mm_tn(left, right)
            total = term if total is None else total + term
    gram = fold(total[:rank] + total[rank:])
    own_ref[...] = pack(gram)
    lift_ref[...] = pack(lift(gram, dev_ref[0]))


def factor_kernel(grams_ref, after_ref, out_ref, token_ref, w_ref, g_ref):
    del after_ref
    count, rank = grams_ref.shape[0], grams_ref.shape[1]
    load_sets(grams_ref.reshape(count * rank, rank), w_ref)
    eliminate(w_ref, g_ref, out_ref.reshape(count * rank, 2 * rank))
    token_ref[...] = jnp.zeros(token_ref.shape, F32)


def row_hop_kernel(bit, last, mine_ref, got_ref, own_ref, upper_ref, path_ref, next_ref):
    n_rows, n_leaf = lax.axis_size("rows"), lax.axis_size("leaf")
    level = (n_rows * n_leaf).bit_length() - 2 - bit
    myself = lax.axis_index("leaf") * n_rows + lax.axis_index("rows")
    packed = mine_ref[...] + got_ref[...]
    path_ref[...] = packed
    lifted = pack(lift(unpack(packed), upper_ref[2**level - 2 + (myself >> (bit + 1))]))
    if last:
        half = lifted.shape[0]
        next_ref[:half] = lifted
        next_ref[half:] = own_ref[...]
    else:
        next_ref[...] = lifted


def packed_places(half):
    row = lax.broadcasted_iota(jnp.int32, (half, 4 * half), 0)
    lane = lax.broadcasted_iota(jnp.int32, (half, 4 * half), 1)
    return jnp.where(lane < 2 * half, row, row + half), lane % (2 * half)


def join(a, b):
    half = a.shape[0]
    row, column = packed_places(half)
    diagonal = jnp.sum(jnp.where(row == column, a, 0.0), axis=0, keepdims=True)
    joint = jnp.where(row > column, a, b)
    return jnp.concatenate([joint, jnp.broadcast_to(diagonal, (SUB, 4 * half))], axis=0)


def part(x):
    half = x.shape[0] - SUB
    joint = unpack(x[:half])
    turned = joint.T
    row = lax.broadcasted_iota(jnp.int32, joint.shape, 0)
    column = lax.broadcasted_iota(jnp.int32, joint.shape, 1)
    diagonal = jnp.broadcast_to(fold(x[half : half + 1]), joint.shape)
    first = jnp.where(row > column, joint, jnp.where(row == column, diagonal, turned))
    return first, jnp.where(row <= column, joint, turned)


def leaf_hop_kernel(bit, mine_ref, got_ref, upper_ref, after_ref, path_ref, next_ref):
    del after_ref
    half = path_ref.shape[0]
    level = lax.axis_size("leaf").bit_length() - 2 - bit
    packed = mine_ref[:half] + got_ref[:half]
    path_ref[...] = packed
    node = lax.axis_index("leaf") >> (bit + 1)
    next_ref[:half] = pack(lift(unpack(packed), upper_ref[2**level - 2 + node]))
    if bit == 0:
        next_ref[half:] = join(mine_ref[half:], got_ref[half:])
    else:
        size = mine_ref.shape[0] - half
        next_ref[half : half + size] = mine_ref[half:]
        next_ref[half + size :] = got_ref[half:]


def leaf_kernel(steps, sets, basis_ref, trans_ref, coup_ref, after_ref, *refs):
    del after_ref
    factor_refs = refs[:sets]
    orth_hbm, moved_ref, split_ref, orth_ref, orth_sem = refs[sets:]
    leaves, rank = basis_ref.shape[0], basis_ref.shape[1]
    chunk = leaves // steps
    lane = lax.broadcasted_iota(jnp.int32, (rank, 2 * rank), 1)
    copies = []
    for step in range(steps):
        for n in range(step * chunk, (step + 1) * chunk):
            high, low = halves(factor_refs[n // SET][n % SET])
            low = jnp.concatenate([low[:, rank:], low[:, :rank]], axis=1)
            upper = jnp.where(lane < rank, high, low).astype(B16)
            inverse = jnp.where(lane < rank, low, high).astype(B16)
            orth_ref[n] = mm(twice(inverse), tall(basis_ref[n]))
            moved_ref[n] = pair(mm(twice(upper), tall(trans_ref[n])))
            split_ref[n] = pair(coup_ref[n])
        span = pl.ds(step * chunk, chunk)
        copy = pltpu.make_async_copy(orth_ref.at[span], orth_hbm.at[span], orth_sem.at[step])
        copy.start()
        copies.append(copy)
    for copy in copies:
        copy.wait()


def top_kernel(n_rows, n_leaf, steps, mine_ref, got_ref, *refs):
    levels = (n_rows * n_leaf).bit_length() - 1
    path_refs = refs[: levels - 1]
    (
        upper_ref,
        dev_ref,
        moved_ref,
        split_ref,
        offset_ref,
        fresh_hbm,
        bridge_hbm,
        coupled_hbm,
        grams_ref,
        factor_ref,
        cols_ref,
        fresh_ref,
        bridge_ref,
        coupled_ref,
        fresh_sem,
        bridge_sem,
        coupled_sem,
        w_ref,
        g_ref,
    ) = refs[levels - 1 :]
    rank = grams_ref.shape[1]
    branch, row = lax.axis_index("leaf"), lax.axis_index("rows")
    myself = branch * n_rows + row
    for n in range(levels - 1):
        grams_ref[n] = unpack(path_refs[n][...])
    half = rank // 2
    grams_ref[levels - 1] = unpack(mine_ref[:half] + got_ref[:half])
    pairs = n_leaf // 4
    for n in range(pairs):
        for place, ref in ((0, mine_ref), (pairs, got_ref)):
            joint = ref[pl.ds(half + n * (half + SUB), half + SUB), :]
            at = levels + 2 * (place + n)
            grams_ref[at], grams_ref[at + 1] = part(joint)
    count = grams_ref.shape[0]
    load_sets(grams_ref.reshape(count * rank, rank), w_ref)
    eliminate(w_ref, g_ref, factor_ref.reshape(count * rank, 2 * rank))
    own = factor_ref[levels]
    own_upper = twice(pair(own[:, :rank]))
    own_inverse = broad(own[:, rank:])
    for n in range(n_leaf):
        cols_ref[n] = broad(factor_ref[levels + n, :, :rank])
    copies = []

    def send(source, target, sem):
        copies.append(pltpu.make_async_copy(source, target, sem))
        copies[-1].start()

    lows, edges, inverses = [own_upper], [tall(dev_ref[0])], []
    for k in range(levels):
        inverses.append(broad(factor_ref[k, :, rank:]))
        if k:
            lows.append(twice(pair(factor_ref[k - 1, :, :rank])))
            edges.append(tall(upper_ref[2 ** (levels - k) - 2 + (myself >> k)]))
    inner = [mm(low, edge) for low, edge in zip(lows, edges)]
    inner = [twice(pair(value)) for value in inner]
    for k in range(levels):
        fresh_ref[0, k] = mm_nt(inner[k], inverses[k])
    send(fresh_ref, fresh_hbm, fresh_sem)
    leaves = moved_ref.shape[0]
    chunk = leaves // steps
    for step in range(steps):
        span = pl.ds(step * chunk, chunk)
        moved = twice(moved_ref[span].reshape(chunk * rank, 2 * rank))
        bridge_ref[span] = mm_nt(moved, own_inverse).reshape(chunk, rank, rank)
        send(bridge_ref.at[span], bridge_hbm.at[span], bridge_sem.at[step])
    blocks = split_ref.shape[0]
    chunk = blocks // steps
    for step in range(steps):
        inner = []
        for b in range(step * chunk, (step + 1) * chunk):
            target = lax.rem(myself + offset_ref[b], n_rows * n_leaf)
            column = cols_ref[(target // n_rows) ^ branch]
            inner.append(mm_nt(twice(split_ref[b]), column))
        inner = [tall(value) for value in inner]
        for n in range(chunk):
            coupled_ref[step * chunk + n] = mm(own_upper, inner[n])
        span = pl.ds(step * chunk, chunk)
        send(coupled_ref.at[span], coupled_hbm.at[span], coupled_sem.at[step])
    for copy in copies:
        copy.wait()


def swap(value, axis, bit):
    pairs = [(source, source ^ 2**bit) for source in range(lax.axis_size(axis))]
    return lax.ppermute(value, axis, pairs)


def cost(flops, moved):
    return pl.CostEstimate(flops=flops, bytes_accessed=moved, transcendentals=0)


def per_device(
    leaf_basis, leaf_transfer, device_transfer, upper_transfer, couplings, couple_offset
):
    n_rows = lax.axis_size("rows")
    n_leaf = lax.axis_size("leaf")
    row_bits = n_rows.bit_length() - 1
    leaf_bits = n_leaf.bit_length() - 1
    levels = row_bits + leaf_bits
    leaves, rank, _ = leaf_basis.shape
    blocks = couplings.shape[0]
    groups = rank // SUB
    params = pltpu.CompilerParams(vmem_limit_bytes=40 * 1024 * 1024)
    vmem = pl.BlockSpec(memory_space=pltpu.VMEM)
    smem = pl.BlockSpec(memory_space=pltpu.SMEM)
    hbm = pl.BlockSpec(memory_space=pltpu.HBM)
    steps = 4

    def like(array, kind=F32):
        return jax.ShapeDtypeStruct(array.shape, kind)

    def shape(*sizes, kind=F32):
        return jax.ShapeDtypeStruct(sizes, kind)

    def scratch(sets):
        return [
            pltpu.VMEM((sets, groups, rank, LANES), F32),
            pltpu.VMEM((sets, SUB, rank, LANES), F32),
        ]

    sets = leaves // SET
    half = rank // 2
    any_place = pl.BlockSpec(memory_space=pl.ANY)
    *grams, own_gram, own_lift = pl.pallas_call(
        functools.partial(gram_kernel, steps, sets),
        in_specs=[hbm, hbm, vmem],
        out_specs=[vmem] * (sets + 2),
        out_shape=[shape(SET, rank, rank)] * sets + [shape(half, 2 * rank)] * 2,
        scratch_shapes=[
            pltpu.VMEM(leaf_basis.shape, F32),
            pltpu.VMEM(leaf_transfer.shape, F32),
            pltpu.SemaphoreType.DMA((steps,)),
            pltpu.SemaphoreType.DMA((steps,)),
        ],
        compiler_params=pltpu.CompilerParams(vmem_limit_bytes=52 * 1024 * 1024),
        cost_estimate=cost(10**9, 4 * 10**6),
        name="gram",
    )(leaf_basis, leaf_transfer, device_transfer)
    path = []
    carry = own_lift
    for bit in range(row_bits):
        got = swap(carry, "rows", bit)
        last = bit == row_bits - 1
        gram, carry = pl.pallas_call(
            functools.partial(row_hop_kernel, bit, last),
            in_specs=[vmem] * 4,
            out_specs=[vmem, vmem],
            out_shape=[shape(half, 2 * rank), shape(rank if last else half, 2 * rank)],
            compiler_params=params,
            name="row_hop",
        )(carry, got, own_gram, upper_transfer)
        path.append(gram)
    factors = []
    for bit in range(leaf_bits - 1):
        got = swap(carry, "leaf", bit)
        if len(factors) < sets:
            factor, token = pl.pallas_call(
                factor_kernel,
                in_specs=[vmem, any_place],
                out_specs=[vmem, vmem],
                out_shape=[shape(SET, rank, 2 * rank), shape(SUB, LANES)],
                scratch_shapes=scratch(1),
                compiler_params=params,
                cost_estimate=cost(5 * 10**9, 8 * 10**6),
                name="factor",
            )(grams[len(factors)], carry)
            factors.append(factor)
        gram, carry = pl.pallas_call(
            functools.partial(leaf_hop_kernel, bit),
            in_specs=[vmem] * 3 + [any_place],
            out_specs=[vmem, vmem],
            out_shape=[shape(half, 2 * rank), shape(half + (half + SUB) * 2**bit, 2 * rank)],
            compiler_params=params,
            name="leaf_hop",
        )(carry, got, upper_transfer, token)
        path.append(gram)
    got = swap(carry, "leaf", leaf_bits - 1)
    leaf_orth, moved, split = pl.pallas_call(
        functools.partial(leaf_kernel, steps, sets),
        in_specs=[vmem] * 3 + [any_place] + [vmem] * sets,
        out_specs=[hbm, vmem, vmem],
        out_shape=[
            like(leaf_basis),
            shape(leaves, rank, 2 * rank, kind=B16),
            shape(blocks, rank, 2 * rank, kind=B16),
        ],
        scratch_shapes=[pltpu.VMEM(leaf_basis.shape, F32), pltpu.SemaphoreType.DMA((steps,))],
        compiler_params=params,
        cost_estimate=cost(5 * 10**9, 8 * 10**6),
        name="leaf",
    )(leaf_basis, leaf_transfer, couplings, carry, *factors)
    sets = -(-(levels + n_leaf) // SET)
    new_transfers, leaf_bridge, coupled = pl.pallas_call(
        functools.partial(top_kernel, n_rows, n_leaf, steps),
        in_specs=[vmem] * (levels + 5) + [smem],
        out_specs=[hbm, hbm, hbm],
        out_shape=[
            shape(1, levels, rank, rank),
            like(leaf_transfer),
            like(couplings),
        ],
        scratch_shapes=[
            pltpu.VMEM((sets * SET, rank, rank), F32),
            pltpu.VMEM((sets * SET, rank, 2 * rank), F32),
            pltpu.VMEM((n_leaf, rank, 4 * rank), B16),
            pltpu.VMEM((1, levels, rank, rank), F32),
            pltpu.VMEM(leaf_transfer.shape, F32),
            pltpu.VMEM(couplings.shape, F32),
            pltpu.SemaphoreType.DMA(()),
            pltpu.SemaphoreType.DMA((steps,)),
            pltpu.SemaphoreType.DMA((steps,)),
        ]
        + scratch(sets),
        compiler_params=params,
        name="top",
    )(carry, got, *path, upper_transfer, device_transfer, moved, split, couple_offset)
    return (leaf_orth, leaf_bridge, new_transfers, coupled)


def solution(mesh):
    in_specs = (
        P(("leaf", "rows"), None, None),
        P(("leaf", "rows"), None, None),
        P(("leaf", "rows"), None, None),
        P(),
        P(("leaf", "rows"), None, None),
        P(("leaf", "rows")),
    )
    out_specs = (
        P(("leaf", "rows"), None, None),
        P(("leaf", "rows"), None, None),
        P(("leaf", "rows"), None, None, None),
        P(("leaf", "rows"), None, None),
    )
    return jax.shard_map(
        per_device, mesh=mesh, in_specs=in_specs, out_specs=out_specs, check_vma=False
    )
```

```python
import functools

import jax
import jax.numpy as jnp
from jax import lax
from jax.experimental import pallas as pl
from jax.experimental.pallas import tpu as pltpu
from jax.sharding import PartitionSpec as P

HIGH = lax.Precision.HIGHEST
SUB = 8
LANES = 128
SET = LANES // SUB
GROUP = 4
F32 = jnp.float32
B16 = jnp.bfloat16


def mm(a, b, dims=((1,), (0,)), precision=None):
    return lax.dot_general(
        a, b, (dims, ((), ())), precision=precision, preferred_element_type=F32
    )


def mm_nt(a, b, precision=None):
    return mm(a, b, ((1,), (1,)), precision)


def mm_tn(a, b, precision=None):
    return mm(a, b, ((0,), (0,)), precision)


def lift(gram, trans):
    return mm_tn(trans, mm(gram, trans, precision=HIGH), HIGH)


def halves(x):
    high = x.astype(B16).astype(F32)
    return high, x - high


def pair(x):
    return jnp.concatenate(halves(x), axis=1).astype(B16)


def twice(x):
    return jnp.concatenate([x, x], axis=1)


def tall(x):
    high, low = halves(x)
    high, low = high.astype(B16), low.astype(B16)
    return jnp.concatenate([high, high, low, low], axis=0)


def broad(x):
    high, low = halves(x)
    return jnp.concatenate([high, high, low, low], axis=1).astype(B16)


def fold(x):
    half = x.shape[1] // 2
    return x[:, :half] + x[:, half:]


def spread(value, at):
    return jnp.broadcast_to(value[at : at + 1, :], (SUB, LANES))


def added(terms):
    while len(terms) > 1:
        terms = [sum(terms[n : n + 2][1:], terms[n]) for n in range(0, len(terms), 2)]
    return terms[0]


def load_sets(flat, w_ref, alone=False):
    sets, groups, rank = w_ref.shape[0], w_ref.shape[1], w_ref.shape[2]
    for t in range(sets):
        for ib in range(groups):
            rows = [
                flat[pl.ds(t * SET * rank + ib * SUB + s, SET, stride=0 if alone else rank), :]
                for s in range(SUB)
            ]
            w_ref[t, ib] = jnp.concatenate(rows, axis=0).T


def eliminate(w_ref, g_ref, out, alone=False):
    sets, groups, rank = w_ref.shape[0], w_ref.shape[1], w_ref.shape[2]
    place = lax.broadcasted_iota(jnp.int32, (SUB, LANES), 0)
    lane = lax.broadcasted_iota(jnp.int32, (SUB, LANES), 1)
    group = lane // SET
    picks = [p * SET + lane % SET for p in range(SUB)]

    def tile(t, ib, jv):
        return w_ref[t, ib, pl.ds(jv * SUB, SUB), :]

    def picked(value, p):
        return jnp.take_along_axis(value, picks[p], axis=1, mode="promise_in_bounds")

    def corner(t, kb):
        diagonal = tile(t, kb, kb)
        rows = [picked(diagonal, p) for p in range(SUB)]
        pivot = spread(rows[0], 0)
        inverses, roots = [], []
        for q in range(SUB):
            unit = jnp.where(place == q, 1.0, rows[q])
            sides = {p: spread(rows[q], p) for p in range(q + 1, SUB)}
            inverse = pl.reciprocal(pivot, approx=True)
            inverses.append(inverse)
            roots.append(lax.rsqrt(pivot))
            if q + 1 < SUB:
                pivot = spread(rows[q + 1], q + 1) - sides[q + 1] * sides[q + 1] * inverse
            for p in range(q + 1, SUB):
                kept = jnp.where(place == q, 0.0, rows[p])
                rows[p] = kept - (sides[p] * unit) * inverse
        return rows, inverses, roots

    def merged(parts):
        value = parts[0]
        for p in range(1, SUB):
            value = jnp.where(group == p, parts[p], value)
        return value

    def copied(ref, row):
        return ref[pl.ds(row, SUB, stride=0), :]

    def panel(t, kb, rows):
        for p in range(SUB):
            g_ref[t, p, pl.ds(kb * SUB, SUB), :] = rows[p]
        for jv in [kb + 1 + n for n in range(groups - 1 - kb)] + list(range(kb)):
            value = tile(t, kb, jv)
            for p in range(SUB):
                g_ref[t, p, pl.ds(jv * SUB, SUB), :] = picked(value, p)
        return {
            (p, q): copied(g_ref.at[t, p], kb * SUB + q) for p in range(SUB) for q in range(p)
        }

    def store(t, kb, mult, rows, roots):
        root = merged(roots)
        zero = jnp.zeros((SUB, LANES), F32)
        lanes = [
            merged([mult[p, q] if p > q else zero for p in range(SUB)]) for q in range(SUB - 1)
        ]
        upper, lower = [], []
        for jv in range(groups):
            if jv == kb:
                final = merged(rows) * root
                upper.append(jnp.where(place >= group, final, 0.0))
                unit = jnp.where(place == group, root, 0.0)
                lower.append(jnp.where(place < group, final, unit))
                continue
            terms = [lanes[q] * g_ref[t, q, pl.ds(jv * SUB, SUB), :] for q in range(SUB - 1)]
            final = added([tile(t, kb, jv)] + terms) * root
            upper.append(final if jv > kb else zero)
            lower.append(final if jv < kb else zero)
        turned = jnp.concatenate(upper + lower, axis=0).T
        for s in range(SUB):
            if alone:
                out[pl.ds(kb * SUB + s, 1), :] = turned[s * SET : s * SET + 1]
            else:
                out[pl.ds(t * SET * rank + kb * SUB + s, SET, stride=rank), :] = turned[
                    s * SET : (s + 1) * SET
                ]

    def weights(t, kb, ib, mult, inverses):
        columns = [copied(w_ref.at[t, ib], kb * SUB + q) for q in range(SUB)]
        found = []
        for q in range(SUB):
            term = added([columns[q]] + [mult[q, r] * columns[r] for r in range(q)])
            found.append(term * inverses[q])
        return [
            added([found[r]] + [found[q] * mult[q, r] for q in range(r + 1, SUB)])
            for r in range(SUB)
        ]

    def trail(t, kb, ib, jv, found):
        if jv == kb:
            value = -found[0]
            for r in range(1, SUB):
                value = jnp.where(place == r, -found[r], value)
        else:
            terms = [found[r] * g_ref[t, r, pl.ds(jv * SUB, SUB), :] for r in range(SUB)]
            value = tile(t, ib, jv) - added(terms)
        w_ref[t, ib, pl.ds(jv * SUB, SUB), :] = value

    corners = [corner(t, 0) for t in range(sets)]
    for kb in range(groups):
        mults = [panel(t, kb, corners[t][0]) for t in range(sets)]
        ahead = []
        if kb + 1 < groups:
            for t in range(sets):
                found = weights(t, kb, kb + 1, mults[t], corners[t][1])
                for jv in [kb + 1] + [jv for jv in range(groups) if jv != kb + 1]:
                    trail(t, kb, kb + 1, jv, found)
            ahead = [corner(t, kb + 1) for t in range(sets)]
        for t in range(sets):
            for ib in range(kb + 2, groups):
                found = weights(t, kb, ib, mults[t], corners[t][1])
                for jv in range(groups):
                    trail(t, kb, ib, jv, found)
            store(t, kb, mults[t], corners[t][0], corners[t][2])
        corners = ahead


def pack(x):
    half = x.shape[0] // 2
    return jnp.concatenate([x[:half], x[half:]], axis=1)


def unpack(x):
    half = x.shape[1] // 2
    return jnp.concatenate([x[:, :half], x[:, half:]], axis=0)


def gram_kernel(steps, sets, basis_hbm, trans_hbm, dev_ref, *refs):
    grams_refs = refs[:sets]
    own_ref, lift_ref, basis_ref, trans_ref, basis_sem, trans_sem = refs[sets:]
    leaves, rank = basis_ref.shape[0], basis_ref.shape[1]
    chunk = leaves // steps
    copies = []
    for step in range(steps):
        span = pl.ds(step * chunk, chunk)
        copies.append(
            (
                pltpu.make_async_copy(basis_hbm.at[span], basis_ref.at[span], basis_sem.at[step]),
                pltpu.make_async_copy(trans_hbm.at[span], trans_ref.at[span], trans_sem.at[step]),
            )
        )
        for copy in copies[-1]:
            copy.start()
    groups = leaves // GROUP
    products, parts, edges, rights = {}, {}, {}, {}
    total = None
    for stage in range(groups + 3):
        if stage < groups:
            if stage * GROUP % chunk == 0:
                for copy in copies[stage * GROUP // chunk]:
                    copy.wait()
            threes = []
            for n in range(stage * GROUP, (stage + 1) * GROUP):
                high, rest = halves(basis_ref[n])
                middle, low = halves(rest)
                threes.append(jnp.concatenate([high, middle, low], axis=0).astype(B16))
            products[stage] = [mm_nt(three, three) for three in threes]
        group = stage - 1
        if 0 <= group < groups:
            edges[group] = [
                pair(trans_ref[n]) for n in range(group * GROUP, (group + 1) * GROUP)
            ]
            parts[group] = []
            for n, product in enumerate(products.pop(group)):
                rows = product[:rank] + product[rank : 2 * rank] + product[2 * rank :]
                gram = fold(rows[:, : 2 * rank]) + rows[:, 2 * rank :]
                at = group * GROUP + n
                grams_refs[at // SET][at % SET] = gram
                both = jnp.concatenate(halves(gram), axis=0).astype(B16)
                parts[group].append(mm(both, edges[group][n]))
        group = stage - 2
        if 0 <= group < groups:
            rights[group] = [pair(fold(part[:rank] + part[rank:])) for part in parts.pop(group)]
        group = stage - 3
        if 0 <= group < groups and group % 2:
            left = jnp.concatenate(edges.pop(group - 1) + edges.pop(group), axis=0)
            right = jnp.concatenate(rights.pop(group - 1) + rights.pop(group), axis=0)
            term = mm_tn(left, right)
            total = term if total is None else total + term
    gram = fold(total[:rank] + total[rank:])
    own_ref[...] = pack(gram)
    lift_ref[...] = pack(lift(gram, dev_ref[0]))


def factor_kernel(grams_ref, after_ref, out_ref, token_ref, w_ref, g_ref):
    del after_ref
    count, rank = grams_ref.shape[0], grams_ref.shape[1]
    load_sets(grams_ref.reshape(count * rank, rank), w_ref)
    eliminate(w_ref, g_ref, out_ref.reshape(count * rank, 2 * rank))
    token_ref[...] = jnp.zeros(token_ref.shape, F32)


def own_kernel(own_ref, after_ref, out_ref, token_ref, full_ref, w_ref, g_ref):
    del after_ref
    full_ref[...] = unpack(own_ref[...])
    load_sets(full_ref, w_ref, alone=True)
    eliminate(w_ref, g_ref, out_ref, alone=True)
    token_ref[...] = jnp.zeros(token_ref.shape, F32)


def row_hop_kernel(
    bit, last, mine_ref, got_ref, own_ref, upper_ref, after_ref, path_ref, next_ref
):
    del after_ref
    n_rows, n_leaf = lax.axis_size("rows"), lax.axis_size("leaf")
    level = (n_rows * n_leaf).bit_length() - 2 - bit
    myself = lax.axis_index("leaf") * n_rows + lax.axis_index("rows")
    packed = mine_ref[...] + got_ref[...]
    path_ref[...] = packed
    lifted = pack(lift(unpack(packed), upper_ref[2**level - 2 + (myself >> (bit + 1))]))
    if last:
        half = lifted.shape[0]
        next_ref[:half] = lifted
        next_ref[half:] = own_ref[...]
    else:
        next_ref[...] = lifted


def packed_places(half):
    row = lax.broadcasted_iota(jnp.int32, (half, 4 * half), 0)
    lane = lax.broadcasted_iota(jnp.int32, (half, 4 * half), 1)
    return jnp.where(lane < 2 * half, row, row + half), lane % (2 * half)


def join(a, b):
    half = a.shape[0]
    row, column = packed_places(half)
    diagonal = jnp.sum(jnp.where(row == column, a, 0.0), axis=0, keepdims=True)
    joint = jnp.where(row > column, a, b)
    return jnp.concatenate([joint, jnp.broadcast_to(diagonal, (SUB, 4 * half))], axis=0)


def part(x):
    half = x.shape[0] - SUB
    joint = unpack(x[:half])
    turned = joint.T
    row = lax.broadcasted_iota(jnp.int32, joint.shape, 0)
    column = lax.broadcasted_iota(jnp.int32, joint.shape, 1)
    diagonal = jnp.broadcast_to(fold(x[half : half + 1]), joint.shape)
    first = jnp.where(row > column, joint, jnp.where(row == column, diagonal, turned))
    return first, jnp.where(row <= column, joint, turned)


def leaf_hop_kernel(bit, mine_ref, got_ref, upper_ref, after_ref, path_ref, next_ref):
    del after_ref
    half = path_ref.shape[0]
    level = lax.axis_size("leaf").bit_length() - 2 - bit
    packed = mine_ref[:half] + got_ref[:half]
    path_ref[...] = packed
    node = lax.axis_index("leaf") >> (bit + 1)
    next_ref[:half] = pack(lift(unpack(packed), upper_ref[2**level - 2 + node]))
    if bit == 0:
        next_ref[half:] = join(mine_ref[half:], got_ref[half:])
    else:
        size = mine_ref.shape[0] - half
        next_ref[half : half + size] = mine_ref[half:]
        next_ref[half + size :] = got_ref[half:]


def leaf_kernel(steps, sets, basis_ref, trans_ref, coup_ref, own_ref, after_ref, *refs):
    del after_ref
    factor_refs = refs[:sets]
    (
        orth_hbm,
        bridge_hbm,
        split_ref,
        orth_ref,
        bridge_ref,
        orth_sem,
        bridge_sem,
    ) = refs[sets:]
    leaves, rank = basis_ref.shape[0], basis_ref.shape[1]
    chunk = leaves // steps
    lane = lax.broadcasted_iota(jnp.int32, (rank, 2 * rank), 1)
    own_upper = twice(pair(own_ref[:, :rank]))
    own_inverse = broad(own_ref[:, rank:])
    copies = []

    def send(source, target, sem):
        copies.append(pltpu.make_async_copy(source, target, sem))
        copies[-1].start()

    for step in range(steps):
        moved = []
        for n in range(step * chunk, (step + 1) * chunk):
            high, low = halves(factor_refs[n // SET][n % SET])
            low = jnp.concatenate([low[:, rank:], low[:, :rank]], axis=1)
            upper = jnp.where(lane < rank, high, low).astype(B16)
            inverse = jnp.where(lane < rank, low, high).astype(B16)
            moved.append(mm(twice(upper), tall(trans_ref[n])))
            orth_ref[n] = mm(twice(inverse), tall(basis_ref[n]))
        span = pl.ds(step * chunk, chunk)
        send(orth_ref.at[span], orth_hbm.at[span], orth_sem.at[step])
        moved = twice(pair(jnp.concatenate(moved, axis=0)))
        bridge_ref[span] = mm_nt(moved, own_inverse).reshape(chunk, rank, rank)
        send(bridge_ref.at[span], bridge_hbm.at[span], bridge_sem.at[step])
    for b in range(coup_ref.shape[0]):
        split_ref[b] = pair(mm(own_upper, tall(coup_ref[b])))
    for copy in copies:
        copy.wait()


def top_kernel(n_rows, n_leaf, steps, mine_ref, got_ref, *refs):
    levels = (n_rows * n_leaf).bit_length() - 1
    path_refs = refs[: levels - 1]
    (
        upper_ref,
        dev_ref,
        own_ref,
        split_ref,
        offset_ref,
        fresh_hbm,
        coupled_hbm,
        grams_ref,
        factor_ref,
        cols_ref,
        fresh_ref,
        coupled_ref,
        fresh_sem,
        coupled_sem,
        w_ref,
        g_ref,
    ) = refs[levels - 1 :]
    rank = grams_ref.shape[1]
    branch, row = lax.axis_index("leaf"), lax.axis_index("rows")
    myself = branch * n_rows + row
    for n in range(levels - 1):
        grams_ref[n] = unpack(path_refs[n][...])
    half = rank // 2
    grams_ref[levels - 1] = unpack(mine_ref[:half] + got_ref[:half])
    pairs = n_leaf // 4
    for n in range(pairs):
        for place, ref in ((0, mine_ref), (pairs, got_ref)):
            joint = ref[pl.ds(half + n * (half + SUB), half + SUB), :]
            at = levels + 2 * (place + n)
            grams_ref[at], grams_ref[at + 1] = part(joint)
    count = grams_ref.shape[0]
    load_sets(grams_ref.reshape(count * rank, rank), w_ref)
    eliminate(w_ref, g_ref, factor_ref.reshape(count * rank, 2 * rank))
    for n in range(n_leaf):
        cols_ref[n] = broad(factor_ref[levels + n, :, :rank])
    copies = []

    def send(source, target, sem):
        copies.append(pltpu.make_async_copy(source, target, sem))
        copies[-1].start()

    lows, edges, inverses = [twice(pair(own_ref[:, :rank]))], [tall(dev_ref[0])], []
    for k in range(levels):
        inverses.append(broad(factor_ref[k, :, rank:]))
        if k:
            lows.append(twice(pair(factor_ref[k - 1, :, :rank])))
            edges.append(tall(upper_ref[2 ** (levels - k) - 2 + (myself >> k)]))
    inner = [mm(low, edge) for low, edge in zip(lows, edges)]
    inner = [twice(pair(value)) for value in inner]
    for k in range(levels):
        fresh_ref[0, k] = mm_nt(inner[k], inverses[k])
    send(fresh_ref, fresh_hbm, fresh_sem)
    blocks = split_ref.shape[0]
    chunk = blocks // steps
    for step in range(steps):
        for b in range(step * chunk, (step + 1) * chunk):
            target = lax.rem(myself + offset_ref[b], n_rows * n_leaf)
            column = cols_ref[(target // n_rows) ^ branch]
            coupled_ref[b] = mm_nt(twice(split_ref[b]), column)
        span = pl.ds(step * chunk, chunk)
        send(coupled_ref.at[span], coupled_hbm.at[span], coupled_sem.at[step])
    for copy in copies:
        copy.wait()


def swap(value, axis, bit):
    pairs = [(source, source ^ 2**bit) for source in range(lax.axis_size(axis))]
    return lax.ppermute(value, axis, pairs)


def cost(flops, moved):
    return pl.CostEstimate(flops=flops, bytes_accessed=moved, transcendentals=0)


def per_device(
    leaf_basis, leaf_transfer, device_transfer, upper_transfer, couplings, couple_offset
):
    n_rows = lax.axis_size("rows")
    n_leaf = lax.axis_size("leaf")
    row_bits = n_rows.bit_length() - 1
    leaf_bits = n_leaf.bit_length() - 1
    levels = row_bits + leaf_bits
    leaves, rank, _ = leaf_basis.shape
    blocks = couplings.shape[0]
    groups = rank // SUB
    params = pltpu.CompilerParams(vmem_limit_bytes=40 * 1024 * 1024)
    vmem = pl.BlockSpec(memory_space=pltpu.VMEM)
    smem = pl.BlockSpec(memory_space=pltpu.SMEM)
    hbm = pl.BlockSpec(memory_space=pltpu.HBM)
    steps = 4

    def like(array, kind=F32):
        return jax.ShapeDtypeStruct(array.shape, kind)

    def shape(*sizes, kind=F32):
        return jax.ShapeDtypeStruct(sizes, kind)

    def scratch(sets):
        return [
            pltpu.VMEM((sets, groups, rank, LANES), F32),
            pltpu.VMEM((sets, SUB, rank, LANES), F32),
        ]

    sets = leaves // SET
    half = rank // 2
    any_place = pl.BlockSpec(memory_space=pl.ANY)
    *grams, own_gram, own_lift = pl.pallas_call(
        functools.partial(gram_kernel, steps, sets),
        in_specs=[hbm, hbm, vmem],
        out_specs=[vmem] * (sets + 2),
        out_shape=[shape(SET, rank, rank)] * sets + [shape(half, 2 * rank)] * 2,
        scratch_shapes=[
            pltpu.VMEM(leaf_basis.shape, F32),
            pltpu.VMEM(leaf_transfer.shape, F32),
            pltpu.SemaphoreType.DMA((steps,)),
            pltpu.SemaphoreType.DMA((steps,)),
        ],
        compiler_params=pltpu.CompilerParams(vmem_limit_bytes=52 * 1024 * 1024),
        cost_estimate=cost(10**9, 4 * 10**6),
        name="gram",
    )(leaf_basis, leaf_transfer, device_transfer)
    path = []
    carry = own_lift
    for bit in range(row_bits):
        got = swap(carry, "rows", bit)
        last = bit == row_bits - 1
        if bit == 1:
            own_factor, token = pl.pallas_call(
                own_kernel,
                in_specs=[vmem, any_place],
                out_specs=[vmem, vmem],
                out_shape=[shape(rank, 2 * rank), shape(SUB, LANES)],
                scratch_shapes=[pltpu.VMEM((rank, rank), F32)] + scratch(1),
                compiler_params=params,
                cost_estimate=cost(5 * 10**9, 8 * 10**6),
                name="own",
            )(own_gram, carry)
        gram, carry = pl.pallas_call(
            functools.partial(row_hop_kernel, bit, last),
            in_specs=[vmem] * 4 + [any_place],
            out_specs=[vmem, vmem],
            out_shape=[shape(half, 2 * rank), shape(rank if last else half, 2 * rank)],
            compiler_params=params,
            name="row_hop",
        )(carry, got, own_gram, upper_transfer, token if bit == 1 else own_gram)
        path.append(gram)
    factors = []
    for bit in range(leaf_bits - 1):
        got = swap(carry, "leaf", bit)
        if len(factors) < sets:
            factor, token = pl.pallas_call(
                factor_kernel,
                in_specs=[vmem, any_place],
                out_specs=[vmem, vmem],
                out_shape=[shape(SET, rank, 2 * rank), shape(SUB, LANES)],
                scratch_shapes=scratch(1),
                compiler_params=params,
                cost_estimate=cost(5 * 10**9, 8 * 10**6),
                name="factor",
            )(grams[len(factors)], carry)
            factors.append(factor)
        gram, carry = pl.pallas_call(
            functools.partial(leaf_hop_kernel, bit),
            in_specs=[vmem] * 3 + [any_place],
            out_specs=[vmem, vmem],
            out_shape=[shape(half, 2 * rank), shape(half + (half + SUB) * 2**bit, 2 * rank)],
            compiler_params=params,
            name="leaf_hop",
        )(carry, got, upper_transfer, token)
        path.append(gram)
    got = swap(carry, "leaf", leaf_bits - 1)
    leaf_orth, leaf_bridge, split = pl.pallas_call(
        functools.partial(leaf_kernel, steps, sets),
        in_specs=[vmem] * 4 + [any_place] + [vmem] * sets,
        out_specs=[hbm, hbm, vmem],
        out_shape=[
            like(leaf_basis),
            like(leaf_transfer),
            shape(blocks, rank, 2 * rank, kind=B16),
        ],
        scratch_shapes=[
            pltpu.VMEM(leaf_basis.shape, F32),
            pltpu.VMEM(leaf_transfer.shape, F32),
            pltpu.SemaphoreType.DMA((steps,)),
            pltpu.SemaphoreType.DMA((steps,)),
        ],
        compiler_params=params,
        cost_estimate=cost(5 * 10**9, 8 * 10**6),
        name="leaf",
    )(leaf_basis, leaf_transfer, couplings, own_factor, carry, *factors)
    sets = -(-(levels + n_leaf) // SET)
    new_transfers, coupled = pl.pallas_call(
        functools.partial(top_kernel, n_rows, n_leaf, steps),
        in_specs=[vmem] * (levels + 5) + [smem],
        out_specs=[hbm, hbm],
        out_shape=[shape(1, levels, rank, rank), like(couplings)],
        scratch_shapes=[
            pltpu.VMEM((sets * SET, rank, rank), F32),
            pltpu.VMEM((sets * SET, rank, 2 * rank), F32),
            pltpu.VMEM((n_leaf, rank, 4 * rank), B16),
            pltpu.VMEM((1, levels, rank, rank), F32),
            pltpu.VMEM(couplings.shape, F32),
            pltpu.SemaphoreType.DMA(()),
            pltpu.SemaphoreType.DMA((steps,)),
        ]
        + scratch(sets),
        compiler_params=params,
        name="top",
    )(carry, got, *path, upper_transfer, device_transfer, own_factor, split, couple_offset)
    return (leaf_orth, leaf_bridge, new_transfers, coupled)


def solution(mesh):
    in_specs = (
        P(("leaf", "rows"), None, None),
        P(("leaf", "rows"), None, None),
        P(("leaf", "rows"), None, None),
        P(),
        P(("leaf", "rows"), None, None),
        P(("leaf", "rows")),
    )
    out_specs = (
        P(("leaf", "rows"), None, None),
        P(("leaf", "rows"), None, None),
        P(("leaf", "rows"), None, None, None),
        P(("leaf", "rows"), None, None),
    )
    return jax.shard_map(
        per_device, mesh=mesh, in_specs=in_specs, out_specs=out_specs, check_vma=False
    )
```

```python
import functools

import jax
import jax.numpy as jnp
from jax import lax
from jax.experimental import pallas as pl
from jax.experimental.pallas import tpu as pltpu
from jax.sharding import PartitionSpec as P

HIGH = lax.Precision.HIGHEST
SUB = 8
LANES = 128
SET = LANES // SUB
GROUP = 4
F32 = jnp.float32
B16 = jnp.bfloat16


def mm(a, b, dims=((1,), (0,)), precision=None):
    return lax.dot_general(
        a, b, (dims, ((), ())), precision=precision, preferred_element_type=F32
    )


def mm_nt(a, b, precision=None):
    return mm(a, b, ((1,), (1,)), precision)


def mm_tn(a, b, precision=None):
    return mm(a, b, ((0,), (0,)), precision)


def lift(gram, trans):
    return mm_tn(trans, mm(gram, trans, precision=HIGH), HIGH)


def halves(x):
    high = x.astype(B16).astype(F32)
    return high, x - high


def pair(x):
    return jnp.concatenate(halves(x), axis=1).astype(B16)


def twice(x):
    return jnp.concatenate([x, x], axis=1)


def tall(x):
    high, low = halves(x)
    high, low = high.astype(B16), low.astype(B16)
    return jnp.concatenate([high, high, low, low], axis=0)


def broad(x):
    high, low = halves(x)
    return jnp.concatenate([high, high, low, low], axis=1).astype(B16)


def fold(x):
    half = x.shape[1] // 2
    return x[:, :half] + x[:, half:]


def spread(value, at):
    return jnp.broadcast_to(value[at : at + 1, :], (SUB, LANES))


def added(terms):
    while len(terms) > 1:
        terms = [sum(terms[n : n + 2][1:], terms[n]) for n in range(0, len(terms), 2)]
    return terms[0]


def load_sets(flat, w_ref, alone=False):
    sets, groups, rank = w_ref.shape[0], w_ref.shape[1], w_ref.shape[2]
    for t in range(sets):
        for ib in range(groups):
            rows = [
                flat[pl.ds(t * SET * rank + ib * SUB + s, SET, stride=0 if alone else rank), :]
                for s in range(SUB)
            ]
            w_ref[t, ib] = jnp.concatenate(rows, axis=0).T


def eliminate(w_ref, g_ref, c_ref, out, alone=False):
    sets, groups, rank = w_ref.shape[0], w_ref.shape[1], w_ref.shape[2]
    place = lax.broadcasted_iota(jnp.int32, (SUB, LANES), 0)
    lane = lax.broadcasted_iota(jnp.int32, (SUB, LANES), 1)
    group = lane // SET
    picks = [p * SET + lane % SET for p in range(SUB)]

    def tile(t, ib, jv):
        return w_ref[t, ib, pl.ds(jv * SUB, SUB), :]

    def picked(value, p):
        return jnp.take_along_axis(value, picks[p], axis=1, mode="promise_in_bounds")

    def copied(ref, row):
        return ref[pl.ds(row, SUB, stride=0), :]

    def corner(t, kb):
        diagonal = tile(t, kb, kb)
        for p in range(SUB):
            c_ref[t, p] = picked(diagonal, p)
        a = {(p, q): copied(c_ref.at[t, p], q) for p in range(SUB) for q in range(p + 1)}
        low, inverses, roots = {}, [], []
        for q in range(SUB):
            squares = {p: a[p, q] * a[q + 1, q] for p in range(q + 1, SUB)}
            inverse = pl.reciprocal(a[q, q], approx=True)
            inverses.append(inverse)
            roots.append(lax.rsqrt(a[q, q]))
            for p in range(q + 1, SUB):
                a[p, q + 1] = a[p, q + 1] - squares[p] * inverse
            for p in range(q + 1, SUB):
                low[p, q] = a[p, q] * inverse
            for p in range(q + 2, SUB):
                for r in range(q + 2, p + 1):
                    a[p, r] = a[p, r] - low[p, q] * a[r, q]
        mult = {}
        for p in range(1, SUB):
            for q in range(p):
                terms = [low[p, q]] + [low[p, r] * mult[r, q] for r in range(q + 1, p)]
                mult[p, q] = -added(terms)
        return a, mult, inverses, roots

    def merged(parts):
        value = parts[0]
        for p in range(1, SUB):
            value = jnp.where(group == p, parts[p], value)
        return value

    def panel(t, kb):
        for jv in [kb + 1 + n for n in range(groups - 1 - kb)] + list(range(kb)):
            value = tile(t, kb, jv)
            for p in range(SUB):
                g_ref[t, p, pl.ds(jv * SUB, SUB), :] = picked(value, p)

    def store(t, kb, a, mult, inverses, roots):
        del inverses
        root = merged(roots)
        zero = jnp.zeros((SUB, LANES), F32)
        lanes = [
            merged([mult[p, q] if p > q else zero for p in range(SUB)]) for q in range(SUB - 1)
        ]
        pivots = merged([a[p, p] for p in range(SUB)])
        upper, lower = [], []
        for jv in range(groups):
            if jv == kb:
                value = zero
                for r in range(SUB):
                    row = lanes[r] if r < SUB - 1 else zero
                    for p in range(r):
                        row = jnp.where(group == p, a[r, p], row)
                    value = jnp.where(place == r, row, value)
                final = value * root
                middle = jnp.where(place == group, pivots * root, 0.0)
                upper.append(jnp.where(place > group, final, middle))
                middle = jnp.where(place == group, root, 0.0)
                lower.append(jnp.where(place < group, final, middle))
                continue
            terms = [lanes[q] * g_ref[t, q, pl.ds(jv * SUB, SUB), :] for q in range(SUB - 1)]
            final = added([tile(t, kb, jv)] + terms) * root
            upper.append(final if jv > kb else zero)
            lower.append(final if jv < kb else zero)
        turned = jnp.concatenate(upper + lower, axis=0).T
        for s in range(SUB):
            if alone:
                out[pl.ds(kb * SUB + s, 1), :] = turned[s * SET : s * SET + 1]
            else:
                out[pl.ds(t * SET * rank + kb * SUB + s, SET, stride=rank), :] = turned[
                    s * SET : (s + 1) * SET
                ]

    def weights(t, kb, ib, mult, inverses):
        columns = [copied(w_ref.at[t, ib], kb * SUB + q) for q in range(SUB)]
        found = []
        for q in range(SUB):
            term = added([columns[q]] + [mult[q, r] * columns[r] for r in range(q)])
            found.append(term * inverses[q])
        return [
            added([found[r]] + [found[q] * mult[q, r] for q in range(r + 1, SUB)])
            for r in range(SUB)
        ]

    def trail(t, kb, ib, jv, found):
        if jv == kb:
            value = -found[0]
            for r in range(1, SUB):
                value = jnp.where(place == r, -found[r], value)
        else:
            terms = [found[r] * g_ref[t, r, pl.ds(jv * SUB, SUB), :] for r in range(SUB)]
            value = tile(t, ib, jv) - added(terms)
        w_ref[t, ib, pl.ds(jv * SUB, SUB), :] = value

    corners = [corner(t, 0) for t in range(sets)]
    for kb in range(groups):
        for t in range(sets):
            panel(t, kb)
        ahead = []
        if kb + 1 < groups:
            for t in range(sets):
                found = weights(t, kb, kb + 1, *corners[t][1:3])
                for jv in [kb + 1] + [jv for jv in range(groups) if jv != kb + 1]:
                    trail(t, kb, kb + 1, jv, found)
            ahead = [corner(t, kb + 1) for t in range(sets)]
        for t in range(sets):
            for ib in range(kb + 2, groups):
                found = weights(t, kb, ib, *corners[t][1:3])
                for jv in range(groups):
                    trail(t, kb, ib, jv, found)
            store(t, kb, *corners[t])
        corners = ahead


def pack(x):
    half = x.shape[0] // 2
    return jnp.concatenate([x[:half], x[half:]], axis=1)


def unpack(x):
    half = x.shape[1] // 2
    return jnp.concatenate([x[:, :half], x[:, half:]], axis=0)


def gram_kernel(steps, sets, basis_hbm, trans_hbm, dev_ref, *refs):
    grams_refs = refs[:sets]
    own_ref, lift_ref, basis_ref, trans_ref, basis_sem, trans_sem = refs[sets:]
    leaves, rank = basis_ref.shape[0], basis_ref.shape[1]
    chunk = leaves // steps
    copies = []
    for step in range(steps):
        span = pl.ds(step * chunk, chunk)
        copies.append(
            (
                pltpu.make_async_copy(basis_hbm.at[span], basis_ref.at[span], basis_sem.at[step]),
                pltpu.make_async_copy(trans_hbm.at[span], trans_ref.at[span], trans_sem.at[step]),
            )
        )
        for copy in copies[-1]:
            copy.start()
    groups = leaves // GROUP
    products, parts, edges, rights = {}, {}, {}, {}
    total = None
    for stage in range(groups + 3):
        if stage < groups:
            if stage * GROUP % chunk == 0:
                for copy in copies[stage * GROUP // chunk]:
                    copy.wait()
            twos = []
            for n in range(stage * GROUP, (stage + 1) * GROUP):
                twos.append(jnp.concatenate(halves(basis_ref[n]), axis=0).astype(B16))
            products[stage] = [mm_nt(two, two) for two in twos]
        group = stage - 1
        if 0 <= group < groups:
            edges[group] = [
                pair(trans_ref[n]) for n in range(group * GROUP, (group + 1) * GROUP)
            ]
            parts[group] = []
            for n, product in enumerate(products.pop(group)):
                gram = fold(product[:rank] + product[rank:])
                at = group * GROUP + n
                grams_refs[at // SET][at % SET] = gram
                both = jnp.concatenate(halves(gram), axis=0).astype(B16)
                parts[group].append(mm(both, edges[group][n]))
        group = stage - 2
        if 0 <= group < groups:
            rights[group] = [pair(fold(part[:rank] + part[rank:])) for part in parts.pop(group)]
        group = stage - 3
        if 0 <= group < groups and group % 2:
            left = jnp.concatenate(edges.pop(group - 1) + edges.pop(group), axis=0)
            right = jnp.concatenate(rights.pop(group - 1) + rights.pop(group), axis=0)
            term = mm_tn(left, right)
            total = term if total is None else total + term
    gram = fold(total[:rank] + total[rank:])
    own_ref[...] = pack(gram)
    lift_ref[...] = pack(lift(gram, dev_ref[0]))


def factor_kernel(grams_ref, after_ref, out_ref, token_ref, w_ref, g_ref, c_ref):
    del after_ref
    count, rank = grams_ref.shape[0], grams_ref.shape[1]
    load_sets(grams_ref.reshape(count * rank, rank), w_ref)
    eliminate(w_ref, g_ref, c_ref, out_ref.reshape(count * rank, 2 * rank))
    token_ref[...] = jnp.zeros(token_ref.shape, F32)


def own_kernel(own_ref, after_ref, out_ref, token_ref, full_ref, w_ref, g_ref, c_ref):
    del after_ref
    full_ref[...] = unpack(own_ref[...])
    load_sets(full_ref, w_ref, alone=True)
    eliminate(w_ref, g_ref, c_ref, out_ref, alone=True)
    token_ref[...] = jnp.zeros(token_ref.shape, F32)


def row_hop_kernel(
    bit, last, mine_ref, got_ref, own_ref, upper_ref, after_ref, path_ref, next_ref
):
    del after_ref
    n_rows, n_leaf = lax.axis_size("rows"), lax.axis_size("leaf")
    level = (n_rows * n_leaf).bit_length() - 2 - bit
    myself = lax.axis_index("leaf") * n_rows + lax.axis_index("rows")
    packed = mine_ref[...] + got_ref[...]
    path_ref[...] = packed
    lifted = pack(lift(unpack(packed), upper_ref[2**level - 2 + (myself >> (bit + 1))]))
    if last:
        half = lifted.shape[0]
        next_ref[:half] = lifted
        next_ref[half:] = own_ref[...]
    else:
        next_ref[...] = lifted


def packed_places(half):
    row = lax.broadcasted_iota(jnp.int32, (half, 4 * half), 0)
    lane = lax.broadcasted_iota(jnp.int32, (half, 4 * half), 1)
    return jnp.where(lane < 2 * half, row, row + half), lane % (2 * half)


def join(a, b):
    half = a.shape[0]
    row, column = packed_places(half)
    diagonal = jnp.sum(jnp.where(row == column, a, 0.0), axis=0, keepdims=True)
    joint = jnp.where(row > column, a, b)
    return jnp.concatenate([joint, jnp.broadcast_to(diagonal, (SUB, 4 * half))], axis=0)


def part(x):
    half = x.shape[0] - SUB
    joint = unpack(x[:half])
    turned = joint.T
    row = lax.broadcasted_iota(jnp.int32, joint.shape, 0)
    column = lax.broadcasted_iota(jnp.int32, joint.shape, 1)
    diagonal = jnp.broadcast_to(fold(x[half : half + 1]), joint.shape)
    first = jnp.where(row > column, joint, jnp.where(row == column, diagonal, turned))
    return first, jnp.where(row <= column, joint, turned)


def leaf_hop_kernel(bit, mine_ref, got_ref, upper_ref, after_ref, path_ref, next_ref):
    del after_ref
    half = path_ref.shape[0]
    level = lax.axis_size("leaf").bit_length() - 2 - bit
    packed = mine_ref[:half] + got_ref[:half]
    path_ref[...] = packed
    node = lax.axis_index("leaf") >> (bit + 1)
    next_ref[:half] = pack(lift(unpack(packed), upper_ref[2**level - 2 + node]))
    if bit == 0:
        next_ref[half:] = join(mine_ref[half:], got_ref[half:])
    else:
        size = mine_ref.shape[0] - half
        next_ref[half : half + size] = mine_ref[half:]
        next_ref[half + size :] = got_ref[half:]


def leaf_kernel(steps, sets, basis_ref, trans_ref, coup_ref, own_ref, after_ref, *refs):
    del after_ref
    factor_refs = refs[:sets]
    (
        orth_hbm,
        bridge_hbm,
        split_ref,
        orth_ref,
        bridge_ref,
        orth_sem,
        bridge_sem,
    ) = refs[sets:]
    leaves, rank = basis_ref.shape[0], basis_ref.shape[1]
    chunk = leaves // steps
    lane = lax.broadcasted_iota(jnp.int32, (rank, 2 * rank), 1)
    own_upper = twice(pair(own_ref[:, :rank]))
    own_inverse = broad(own_ref[:, rank:])
    copies = []

    def send(source, target, sem):
        copies.append(pltpu.make_async_copy(source, target, sem))
        copies[-1].start()

    for step in range(steps):
        moved = []
        for n in range(step * chunk, (step + 1) * chunk):
            high, low = halves(factor_refs[n // SET][n % SET])
            low = jnp.concatenate([low[:, rank:], low[:, :rank]], axis=1)
            upper = jnp.where(lane < rank, high, low).astype(B16)
            inverse = jnp.where(lane < rank, low, high).astype(B16)
            moved.append(mm(twice(upper), tall(trans_ref[n])))
            orth_ref[n] = mm(twice(inverse), tall(basis_ref[n]))
        span = pl.ds(step * chunk, chunk)
        send(orth_ref.at[span], orth_hbm.at[span], orth_sem.at[step])
        moved = twice(pair(jnp.concatenate(moved, axis=0)))
        bridge_ref[span] = mm_nt(moved, own_inverse).reshape(chunk, rank, rank)
        send(bridge_ref.at[span], bridge_hbm.at[span], bridge_sem.at[step])
    for b in range(coup_ref.shape[0]):
        split_ref[b] = pair(mm(own_upper, tall(coup_ref[b])))
    for copy in copies:
        copy.wait()


def top_kernel(n_rows, n_leaf, steps, mine_ref, got_ref, *refs):
    levels = (n_rows * n_leaf).bit_length() - 1
    path_refs = refs[: levels - 1]
    (
        upper_ref,
        dev_ref,
        own_ref,
        split_ref,
        offset_ref,
        fresh_hbm,
        coupled_hbm,
        grams_ref,
        factor_ref,
        cols_ref,
        fresh_ref,
        coupled_ref,
        fresh_sem,
        coupled_sem,
        w_ref,
        g_ref,
        c_ref,
    ) = refs[levels - 1 :]
    rank = grams_ref.shape[1]
    branch, row = lax.axis_index("leaf"), lax.axis_index("rows")
    myself = branch * n_rows + row
    for n in range(levels - 1):
        grams_ref[n] = unpack(path_refs[n][...])
    half = rank // 2
    grams_ref[levels - 1] = unpack(mine_ref[:half] + got_ref[:half])
    pairs = n_leaf // 4
    for n in range(pairs):
        for place, ref in ((0, mine_ref), (pairs, got_ref)):
            joint = ref[pl.ds(half + n * (half + SUB), half + SUB), :]
            at = levels + 2 * (place + n)
            grams_ref[at], grams_ref[at + 1] = part(joint)
    count = grams_ref.shape[0]
    load_sets(grams_ref.reshape(count * rank, rank), w_ref)
    eliminate(w_ref, g_ref, c_ref, factor_ref.reshape(count * rank, 2 * rank))
    for n in range(n_leaf):
        cols_ref[n] = broad(factor_ref[levels + n, :, :rank])
    copies = []

    def send(source, target, sem):
        copies.append(pltpu.make_async_copy(source, target, sem))
        copies[-1].start()

    lows, edges, inverses = [twice(pair(own_ref[:, :rank]))], [tall(dev_ref[0])], []
    for k in range(levels):
        inverses.append(broad(factor_ref[k, :, rank:]))
        if k:
            lows.append(twice(pair(factor_ref[k - 1, :, :rank])))
            edges.append(tall(upper_ref[2 ** (levels - k) - 2 + (myself >> k)]))
    inner = [mm(low, edge) for low, edge in zip(lows, edges)]
    inner = [twice(pair(value)) for value in inner]
    for k in range(levels):
        fresh_ref[0, k] = mm_nt(inner[k], inverses[k])
    send(fresh_ref, fresh_hbm, fresh_sem)
    blocks = split_ref.shape[0]
    chunk = blocks // steps
    for step in range(steps):
        for b in range(step * chunk, (step + 1) * chunk):
            target = lax.rem(myself + offset_ref[b], n_rows * n_leaf)
            column = cols_ref[(target // n_rows) ^ branch]
            coupled_ref[b] = mm_nt(twice(split_ref[b]), column)
        span = pl.ds(step * chunk, chunk)
        send(coupled_ref.at[span], coupled_hbm.at[span], coupled_sem.at[step])
    for copy in copies:
        copy.wait()


def swap(value, axis, bit):
    pairs = [(source, source ^ 2**bit) for source in range(lax.axis_size(axis))]
    return lax.ppermute(value, axis, pairs)


def cost(flops, moved):
    return pl.CostEstimate(flops=flops, bytes_accessed=moved, transcendentals=0)


def per_device(
    leaf_basis, leaf_transfer, device_transfer, upper_transfer, couplings, couple_offset
):
    n_rows = lax.axis_size("rows")
    n_leaf = lax.axis_size("leaf")
    row_bits = n_rows.bit_length() - 1
    leaf_bits = n_leaf.bit_length() - 1
    levels = row_bits + leaf_bits
    leaves, rank, _ = leaf_basis.shape
    blocks = couplings.shape[0]
    groups = rank // SUB
    params = pltpu.CompilerParams(vmem_limit_bytes=40 * 1024 * 1024)
    vmem = pl.BlockSpec(memory_space=pltpu.VMEM)
    smem = pl.BlockSpec(memory_space=pltpu.SMEM)
    hbm = pl.BlockSpec(memory_space=pltpu.HBM)
    steps = 4

    def like(array, kind=F32):
        return jax.ShapeDtypeStruct(array.shape, kind)

    def shape(*sizes, kind=F32):
        return jax.ShapeDtypeStruct(sizes, kind)

    def scratch(sets):
        return [
            pltpu.VMEM((sets, groups, rank, LANES), F32),
            pltpu.VMEM((sets, SUB, rank, LANES), F32),
            pltpu.VMEM((sets, SUB, SUB, LANES), F32),
        ]

    sets = leaves // SET
    half = rank // 2
    any_place = pl.BlockSpec(memory_space=pl.ANY)
    *grams, own_gram, own_lift = pl.pallas_call(
        functools.partial(gram_kernel, steps, sets),
        in_specs=[hbm, hbm, vmem],
        out_specs=[vmem] * (sets + 2),
        out_shape=[shape(SET, rank, rank)] * sets + [shape(half, 2 * rank)] * 2,
        scratch_shapes=[
            pltpu.VMEM(leaf_basis.shape, F32),
            pltpu.VMEM(leaf_transfer.shape, F32),
            pltpu.SemaphoreType.DMA((steps,)),
            pltpu.SemaphoreType.DMA((steps,)),
        ],
        compiler_params=pltpu.CompilerParams(vmem_limit_bytes=52 * 1024 * 1024),
        cost_estimate=cost(10**9, 4 * 10**6),
        name="gram",
    )(leaf_basis, leaf_transfer, device_transfer)
    path = []
    carry = own_lift
    for bit in range(row_bits):
        got = swap(carry, "rows", bit)
        last = bit == row_bits - 1
        if bit == 1:
            own_factor, token = pl.pallas_call(
                own_kernel,
                in_specs=[vmem, any_place],
                out_specs=[vmem, vmem],
                out_shape=[shape(rank, 2 * rank), shape(SUB, LANES)],
                scratch_shapes=[pltpu.VMEM((rank, rank), F32)] + scratch(1),
                compiler_params=params,
                cost_estimate=cost(5 * 10**9, 8 * 10**6),
                name="own",
            )(own_gram, carry)
        gram, carry = pl.pallas_call(
            functools.partial(row_hop_kernel, bit, last),
            in_specs=[vmem] * 4 + [any_place],
            out_specs=[vmem, vmem],
            out_shape=[shape(half, 2 * rank), shape(rank if last else half, 2 * rank)],
            compiler_params=params,
            name="row_hop",
        )(carry, got, own_gram, upper_transfer, token if bit == 1 else own_gram)
        path.append(gram)
    factors = []
    for bit in range(leaf_bits - 1):
        got = swap(carry, "leaf", bit)
        if len(factors) < sets:
            factor, token = pl.pallas_call(
                factor_kernel,
                in_specs=[vmem, any_place],
                out_specs=[vmem, vmem],
                out_shape=[shape(SET, rank, 2 * rank), shape(SUB, LANES)],
                scratch_shapes=scratch(1),
                compiler_params=params,
                cost_estimate=cost(5 * 10**9, 8 * 10**6),
                name="factor",
            )(grams[len(factors)], carry)
            factors.append(factor)
        gram, carry = pl.pallas_call(
            functools.partial(leaf_hop_kernel, bit),
            in_specs=[vmem] * 3 + [any_place],
            out_specs=[vmem, vmem],
            out_shape=[shape(half, 2 * rank), shape(half + (half + SUB) * 2**bit, 2 * rank)],
            compiler_params=params,
            name="leaf_hop",
        )(carry, got, upper_transfer, token)
        path.append(gram)
    got = swap(carry, "leaf", leaf_bits - 1)
    leaf_orth, leaf_bridge, split = pl.pallas_call(
        functools.partial(leaf_kernel, steps, sets),
        in_specs=[vmem] * 4 + [any_place] + [vmem] * sets,
        out_specs=[hbm, hbm, vmem],
        out_shape=[
            like(leaf_basis),
            like(leaf_transfer),
            shape(blocks, rank, 2 * rank, kind=B16),
        ],
        scratch_shapes=[
            pltpu.VMEM(leaf_basis.shape, F32),
            pltpu.VMEM(leaf_transfer.shape, F32),
            pltpu.SemaphoreType.DMA((steps,)),
            pltpu.SemaphoreType.DMA((steps,)),
        ],
        compiler_params=params,
        cost_estimate=cost(5 * 10**9, 8 * 10**6),
        name="leaf",
    )(leaf_basis, leaf_transfer, couplings, own_factor, carry, *factors)
    sets = -(-(levels + n_leaf) // SET)
    new_transfers, coupled = pl.pallas_call(
        functools.partial(top_kernel, n_rows, n_leaf, steps),
        in_specs=[vmem] * (levels + 5) + [smem],
        out_specs=[hbm, hbm],
        out_shape=[shape(1, levels, rank, rank), like(couplings)],
        scratch_shapes=[
            pltpu.VMEM((sets * SET, rank, rank), F32),
            pltpu.VMEM((sets * SET, rank, 2 * rank), F32),
            pltpu.VMEM((n_leaf, rank, 4 * rank), B16),
            pltpu.VMEM((1, levels, rank, rank), F32),
            pltpu.VMEM(couplings.shape, F32),
            pltpu.SemaphoreType.DMA(()),
            pltpu.SemaphoreType.DMA((steps,)),
        ]
        + scratch(sets),
        compiler_params=params,
        name="top",
    )(carry, got, *path, upper_transfer, device_transfer, own_factor, split, couple_offset)
    return (leaf_orth, leaf_bridge, new_transfers, coupled)


def solution(mesh):
    in_specs = (
        P(("leaf", "rows"), None, None),
        P(("leaf", "rows"), None, None),
        P(("leaf", "rows"), None, None),
        P(),
        P(("leaf", "rows"), None, None),
        P(("leaf", "rows")),
    )
    out_specs = (
        P(("leaf", "rows"), None, None),
        P(("leaf", "rows"), None, None),
        P(("leaf", "rows"), None, None, None),
        P(("leaf", "rows"), None, None),
    )
    return jax.shard_map(
        per_device, mesh=mesh, in_specs=in_specs, out_specs=out_specs, check_vma=False
    )
```

```python
import functools

import jax
import jax.numpy as jnp
from jax import lax
from jax.experimental import pallas as pl
from jax.experimental.pallas import tpu as pltpu
from jax.sharding import PartitionSpec as P

HIGH = lax.Precision.HIGHEST
SUB = 8
LANES = 128
SET = LANES // SUB
GROUP = 4
F32 = jnp.float32
B16 = jnp.bfloat16


def mm(a, b, dims=((1,), (0,)), precision=None):
    return lax.dot_general(
        a, b, (dims, ((), ())), precision=precision, preferred_element_type=F32
    )


def mm_nt(a, b, precision=None):
    return mm(a, b, ((1,), (1,)), precision)


def mm_tn(a, b, precision=None):
    return mm(a, b, ((0,), (0,)), precision)


def lift(gram, trans):
    return mm_tn(trans, mm(gram, trans, precision=HIGH), HIGH)


def halves(x):
    high = x.astype(B16).astype(F32)
    return high, x - high


def pair(x):
    return jnp.concatenate(halves(x), axis=1).astype(B16)


def twice(x):
    return jnp.concatenate([x, x], axis=1)


def tall(x):
    high, low = halves(x)
    high, low = high.astype(B16), low.astype(B16)
    return jnp.concatenate([high, high, low, low], axis=0)


def broad(x):
    high, low = halves(x)
    return jnp.concatenate([high, high, low, low], axis=1).astype(B16)


def fold(x):
    half = x.shape[1] // 2
    return x[:, :half] + x[:, half:]


def spread(value, at):
    return jnp.broadcast_to(value[at : at + 1, :], (SUB, LANES))


def added(terms):
    while len(terms) > 1:
        terms = [sum(terms[n : n + 2][1:], terms[n]) for n in range(0, len(terms), 2)]
    return terms[0]


def load_sets(flat, w_ref, alone=False):
    sets, groups, rank = w_ref.shape[0], w_ref.shape[1], w_ref.shape[2]
    for t in range(sets):
        for ib in range(groups):
            rows = [
                flat[pl.ds(t * SET * rank + ib * SUB + s, SET, stride=0 if alone else rank), :]
                for s in range(SUB)
            ]
            w_ref[t, ib] = jnp.concatenate(rows, axis=0).T


def eliminate(w_ref, g_ref, c_ref, out, alone=False):
    sets, groups, rank = w_ref.shape[0], w_ref.shape[1], w_ref.shape[2]
    place = lax.broadcasted_iota(jnp.int32, (SUB, LANES), 0)
    lane = lax.broadcasted_iota(jnp.int32, (SUB, LANES), 1)
    group = lane // SET

    def tile(t, ib, jv):
        return w_ref[t, ib, pl.ds(jv * SUB, SUB), :]

    def replicated(value):
        found = [value]
        for width in (LANES // 2, LANES // 4, LANES // 8):
            first = lane % (2 * width) < width
            split = []
            for part in found:
                rolled = pltpu.roll(part, width, 1)
                split.append(jnp.where(first, part, rolled))
                split.append(jnp.where(first, rolled, part))
            found = split
        return found

    def copied(ref, row):
        return ref[pl.ds(row, SUB, stride=0), :]

    def corner(t, kb):
        diagonal = tile(t, kb, kb)
        for p, row in enumerate(replicated(diagonal)):
            c_ref[t, p] = row
        a = {(p, q): copied(c_ref.at[t, p], q) for p in range(SUB) for q in range(p + 1)}
        low, inverses, roots = {}, [], []
        for q in range(SUB):
            squares = {p: a[p, q] * a[q + 1, q] for p in range(q + 1, SUB)}
            inverse = pl.reciprocal(a[q, q], approx=True)
            inverses.append(inverse)
            roots.append(lax.rsqrt(a[q, q]))
            for p in range(q + 1, SUB):
                a[p, q + 1] = a[p, q + 1] - squares[p] * inverse
            for p in range(q + 1, SUB):
                low[p, q] = a[p, q] * inverse
            for p in range(q + 2, SUB):
                for r in range(q + 2, p + 1):
                    a[p, r] = a[p, r] - low[p, q] * a[r, q]
        mult = {}
        for p in range(1, SUB):
            for q in range(p):
                terms = [low[p, q]] + [low[p, r] * mult[r, q] for r in range(q + 1, p)]
                mult[p, q] = -added(terms)
        return a, mult, inverses, roots

    def merged(parts):
        value = parts[0]
        for p in range(1, SUB):
            value = jnp.where(group == p, parts[p], value)
        return value

    def panel(t, kb):
        for jv in [kb + 1 + n for n in range(groups - 1 - kb)] + list(range(kb)):
            for p, row in enumerate(replicated(tile(t, kb, jv))):
                g_ref[t, p, pl.ds(jv * SUB, SUB), :] = row

    def store(t, kb, a, mult, inverses, roots):
        del inverses
        root = merged(roots)
        zero = jnp.zeros((SUB, LANES), F32)
        lanes = [
            merged([mult[p, q] if p > q else zero for p in range(SUB)]) for q in range(SUB - 1)
        ]
        pivots = merged([a[p, p] for p in range(SUB)])
        upper, lower = [], []
        for jv in range(groups):
            if jv == kb:
                value = zero
                for r in range(SUB):
                    row = lanes[r] if r < SUB - 1 else zero
                    for p in range(r):
                        row = jnp.where(group == p, a[r, p], row)
                    value = jnp.where(place == r, row, value)
                final = value * root
                middle = jnp.where(place == group, pivots * root, 0.0)
                upper.append(jnp.where(place > group, final, middle))
                middle = jnp.where(place == group, root, 0.0)
                lower.append(jnp.where(place < group, final, middle))
                continue
            terms = [lanes[q] * g_ref[t, q, pl.ds(jv * SUB, SUB), :] for q in range(SUB - 1)]
            final = added([tile(t, kb, jv)] + terms) * root
            upper.append(final if jv > kb else zero)
            lower.append(final if jv < kb else zero)
        turned = jnp.concatenate(upper + lower, axis=0).T
        for s in range(SUB):
            if alone:
                out[pl.ds(kb * SUB + s, 1), :] = turned[s * SET : s * SET + 1]
            else:
                out[pl.ds(t * SET * rank + kb * SUB + s, SET, stride=rank), :] = turned[
                    s * SET : (s + 1) * SET
                ]

    def weights(t, kb, ib, mult, inverses):
        columns = [copied(w_ref.at[t, ib], kb * SUB + q) for q in range(SUB)]
        found = []
        for q in range(SUB):
            term = added([columns[q]] + [mult[q, r] * columns[r] for r in range(q)])
            found.append(term * inverses[q])
        return [
            added([found[r]] + [found[q] * mult[q, r] for q in range(r + 1, SUB)])
            for r in range(SUB)
        ]

    def trail(t, kb, jv, founds):
        if jv == kb:
            values = {}
            for ib, found in founds.items():
                values[ib] = -found[0]
                for r in range(1, SUB):
                    values[ib] = jnp.where(place == r, -found[r], values[ib])
        else:
            source = [g_ref[t, r, pl.ds(jv * SUB, SUB), :] for r in range(SUB)]
            values = {
                ib: tile(t, ib, jv) - added([found[r] * source[r] for r in range(SUB)])
                for ib, found in founds.items()
            }
        for ib, value in values.items():
            w_ref[t, ib, pl.ds(jv * SUB, SUB), :] = value

    corners = [corner(t, 0) for t in range(sets)]
    for kb in range(groups):
        for t in range(sets):
            panel(t, kb)
        ahead = []
        if kb + 1 < groups:
            for t in range(sets):
                founds = {kb + 1: weights(t, kb, kb + 1, *corners[t][1:3])}
                for jv in [kb + 1] + [jv for jv in range(groups) if jv != kb + 1]:
                    trail(t, kb, jv, founds)
            ahead = [corner(t, kb + 1) for t in range(sets)]
        for t in range(sets):
            for ib in range(kb + 2, groups, 2):
                founds = {
                    n: weights(t, kb, n, *corners[t][1:3]) for n in range(ib, min(ib + 2, groups))
                }
                for jv in range(groups):
                    trail(t, kb, jv, founds)
            store(t, kb, *corners[t])
        corners = ahead


def pack(x):
    half = x.shape[0] // 2
    return jnp.concatenate([x[:half], x[half:]], axis=1)


def unpack(x):
    half = x.shape[1] // 2
    return jnp.concatenate([x[:, :half], x[:, half:]], axis=0)


def gram_kernel(steps, sets, basis_hbm, trans_hbm, dev_ref, *refs):
    grams_refs = refs[:sets]
    own_ref, lift_ref, basis_ref, trans_ref, basis_sem, trans_sem = refs[sets:]
    leaves, rank = basis_ref.shape[0], basis_ref.shape[1]
    chunk = leaves // steps
    copies = []
    for step in range(steps):
        span = pl.ds(step * chunk, chunk)
        copies.append(
            (
                pltpu.make_async_copy(basis_hbm.at[span], basis_ref.at[span], basis_sem.at[step]),
                pltpu.make_async_copy(trans_hbm.at[span], trans_ref.at[span], trans_sem.at[step]),
            )
        )
        for copy in copies[-1]:
            copy.start()
    groups = leaves // GROUP
    products, parts, edges, rights = {}, {}, {}, {}
    total = None
    for stage in range(groups + 3):
        if stage < groups:
            if stage * GROUP % chunk == 0:
                for copy in copies[stage * GROUP // chunk]:
                    copy.wait()
            twos = []
            for n in range(stage * GROUP, (stage + 1) * GROUP):
                twos.append(jnp.concatenate(halves(basis_ref[n]), axis=0).astype(B16))
            products[stage] = [mm_nt(two, two) for two in twos]
        group = stage - 1
        if 0 <= group < groups:
            edges[group] = [
                pair(trans_ref[n]) for n in range(group * GROUP, (group + 1) * GROUP)
            ]
            parts[group] = []
            for n, product in enumerate(products.pop(group)):
                gram = fold(product[:rank] + product[rank:])
                at = group * GROUP + n
                grams_refs[at // SET][at % SET] = gram
                both = jnp.concatenate(halves(gram), axis=0).astype(B16)
                parts[group].append(mm(both, edges[group][n]))
        group = stage - 2
        if 0 <= group < groups:
            rights[group] = [pair(fold(part[:rank] + part[rank:])) for part in parts.pop(group)]
        group = stage - 3
        if 0 <= group < groups and group % 2:
            left = jnp.concatenate(edges.pop(group - 1) + edges.pop(group), axis=0)
            right = jnp.concatenate(rights.pop(group - 1) + rights.pop(group), axis=0)
            term = mm_tn(left, right)
            total = term if total is None else total + term
    gram = fold(total[:rank] + total[rank:])
    own_ref[...] = pack(gram)
    lift_ref[...] = pack(lift(gram, dev_ref[0]))


def factor_kernel(grams_ref, after_ref, out_ref, token_ref, w_ref, g_ref, c_ref):
    del after_ref
    count, rank = grams_ref.shape[0], grams_ref.shape[1]
    load_sets(grams_ref.reshape(count * rank, rank), w_ref)
    eliminate(w_ref, g_ref, c_ref, out_ref.reshape(count * rank, 2 * rank))
    token_ref[...] = jnp.zeros(token_ref.shape, F32)


def own_kernel(own_ref, after_ref, out_ref, token_ref, full_ref, w_ref, g_ref, c_ref):
    del after_ref
    full_ref[...] = unpack(own_ref[...])
    load_sets(full_ref, w_ref, alone=True)
    eliminate(w_ref, g_ref, c_ref, out_ref, alone=True)
    token_ref[...] = jnp.zeros(token_ref.shape, F32)


def row_hop_kernel(
    bit, last, mine_ref, got_ref, own_ref, upper_ref, after_ref, path_ref, next_ref
):
    del after_ref
    n_rows, n_leaf = lax.axis_size("rows"), lax.axis_size("leaf")
    level = (n_rows * n_leaf).bit_length() - 2 - bit
    myself = lax.axis_index("leaf") * n_rows + lax.axis_index("rows")
    packed = mine_ref[...] + got_ref[...]
    path_ref[...] = packed
    lifted = pack(lift(unpack(packed), upper_ref[2**level - 2 + (myself >> (bit + 1))]))
    if last:
        half = lifted.shape[0]
        next_ref[:half] = lifted
        next_ref[half:] = own_ref[...]
    else:
        next_ref[...] = lifted


def packed_places(half):
    row = lax.broadcasted_iota(jnp.int32, (half, 4 * half), 0)
    lane = lax.broadcasted_iota(jnp.int32, (half, 4 * half), 1)
    return jnp.where(lane < 2 * half, row, row + half), lane % (2 * half)


def join(a, b):
    half = a.shape[0]
    row, column = packed_places(half)
    diagonal = jnp.sum(jnp.where(row == column, a, 0.0), axis=0, keepdims=True)
    joint = jnp.where(row > column, a, b)
    return jnp.concatenate([joint, jnp.broadcast_to(diagonal, (SUB, 4 * half))], axis=0)


def part(x):
    half = x.shape[0] - SUB
    joint = unpack(x[:half])
    turned = joint.T
    row = lax.broadcasted_iota(jnp.int32, joint.shape, 0)
    column = lax.broadcasted_iota(jnp.int32, joint.shape, 1)
    diagonal = jnp.broadcast_to(fold(x[half : half + 1]), joint.shape)
    first = jnp.where(row > column, joint, jnp.where(row == column, diagonal, turned))
    return first, jnp.where(row <= column, joint, turned)


def leaf_hop_kernel(bit, mine_ref, got_ref, upper_ref, after_ref, path_ref, next_ref):
    del after_ref
    half = path_ref.shape[0]
    level = lax.axis_size("leaf").bit_length() - 2 - bit
    packed = mine_ref[:half] + got_ref[:half]
    path_ref[...] = packed
    node = lax.axis_index("leaf") >> (bit + 1)
    next_ref[:half] = pack(lift(unpack(packed), upper_ref[2**level - 2 + node]))
    if bit == 0:
        next_ref[half:] = join(mine_ref[half:], got_ref[half:])
    else:
        size = mine_ref.shape[0] - half
        next_ref[half : half + size] = mine_ref[half:]
        next_ref[half + size :] = got_ref[half:]


def leaf_kernel(steps, sets, basis_ref, trans_ref, coup_ref, own_ref, after_ref, *refs):
    del after_ref
    factor_refs = refs[:sets]
    (
        orth_hbm,
        bridge_hbm,
        split_ref,
        orth_ref,
        bridge_ref,
        orth_sem,
        bridge_sem,
    ) = refs[sets:]
    leaves, rank = basis_ref.shape[0], basis_ref.shape[1]
    chunk = leaves // steps
    lane = lax.broadcasted_iota(jnp.int32, (rank, 2 * rank), 1)
    own_upper = twice(pair(own_ref[:, :rank]))
    own_inverse = broad(own_ref[:, rank:])
    copies = []

    def send(source, target, sem):
        copies.append(pltpu.make_async_copy(source, target, sem))
        copies[-1].start()

    for step in range(steps):
        moved = []
        for n in range(step * chunk, (step + 1) * chunk):
            high, low = halves(factor_refs[n // SET][n % SET])
            low = jnp.concatenate([low[:, rank:], low[:, :rank]], axis=1)
            upper = jnp.where(lane < rank, high, low).astype(B16)
            inverse = jnp.where(lane < rank, low, high).astype(B16)
            moved.append(mm(twice(upper), tall(trans_ref[n])))
            orth_ref[n] = mm(twice(inverse), tall(basis_ref[n]))
        span = pl.ds(step * chunk, chunk)
        send(orth_ref.at[span], orth_hbm.at[span], orth_sem.at[step])
        moved = twice(pair(jnp.concatenate(moved, axis=0)))
        bridge_ref[span] = mm_nt(moved, own_inverse).reshape(chunk, rank, rank)
        send(bridge_ref.at[span], bridge_hbm.at[span], bridge_sem.at[step])
    for b in range(coup_ref.shape[0]):
        split_ref[b] = pair(mm(own_upper, tall(coup_ref[b])))
    for copy in copies:
        copy.wait()


def top_kernel(n_rows, n_leaf, steps, mine_ref, got_ref, *refs):
    levels = (n_rows * n_leaf).bit_length() - 1
    path_refs = refs[: levels - 1]
    (
        upper_ref,
        dev_ref,
        own_ref,
        split_ref,
        offset_ref,
        fresh_hbm,
        coupled_hbm,
        grams_ref,
        factor_ref,
        cols_ref,
        fresh_ref,
        coupled_ref,
        fresh_sem,
        coupled_sem,
        w_ref,
        g_ref,
        c_ref,
    ) = refs[levels - 1 :]
    rank = grams_ref.shape[1]
    branch, row = lax.axis_index("leaf"), lax.axis_index("rows")
    myself = branch * n_rows + row
    for n in range(levels - 1):
        grams_ref[n] = unpack(path_refs[n][...])
    half = rank // 2
    grams_ref[levels - 1] = unpack(mine_ref[:half] + got_ref[:half])
    pairs = n_leaf // 4
    for n in range(pairs):
        for place, ref in ((0, mine_ref), (pairs, got_ref)):
            joint = ref[pl.ds(half + n * (half + SUB), half + SUB), :]
            at = levels + 2 * (place + n)
            grams_ref[at], grams_ref[at + 1] = part(joint)
    count = grams_ref.shape[0]
    load_sets(grams_ref.reshape(count * rank, rank), w_ref)
    eliminate(w_ref, g_ref, c_ref, factor_ref.reshape(count * rank, 2 * rank))
    for n in range(n_leaf):
        cols_ref[n] = broad(factor_ref[levels + n, :, :rank])
    copies = []

    def send(source, target, sem):
        copies.append(pltpu.make_async_copy(source, target, sem))
        copies[-1].start()

    lows, edges, inverses = [twice(pair(own_ref[:, :rank]))], [tall(dev_ref[0])], []
    for k in range(levels):
        inverses.append(broad(factor_ref[k, :, rank:]))
        if k:
            lows.append(twice(pair(factor_ref[k - 1, :, :rank])))
            edges.append(tall(upper_ref[2 ** (levels - k) - 2 + (myself >> k)]))
    inner = [mm(low, edge) for low, edge in zip(lows, edges)]
    inner = [twice(pair(value)) for value in inner]
    for k in range(levels):
        fresh_ref[0, k] = mm_nt(inner[k], inverses[k])
    send(fresh_ref, fresh_hbm, fresh_sem)
    blocks = split_ref.shape[0]
    chunk = blocks // steps
    for step in range(steps):
        for b in range(step * chunk, (step + 1) * chunk):
            target = lax.rem(myself + offset_ref[b], n_rows * n_leaf)
            column = cols_ref[(target // n_rows) ^ branch]
            coupled_ref[b] = mm_nt(twice(split_ref[b]), column)
        span = pl.ds(step * chunk, chunk)
        send(coupled_ref.at[span], coupled_hbm.at[span], coupled_sem.at[step])
    for copy in copies:
        copy.wait()


def swap(value, axis, bit):
    pairs = [(source, source ^ 2**bit) for source in range(lax.axis_size(axis))]
    return lax.ppermute(value, axis, pairs)


def cost(flops, moved):
    return pl.CostEstimate(flops=flops, bytes_accessed=moved, transcendentals=0)


def per_device(
    leaf_basis, leaf_transfer, device_transfer, upper_transfer, couplings, couple_offset
):
    n_rows = lax.axis_size("rows")
    n_leaf = lax.axis_size("leaf")
    row_bits = n_rows.bit_length() - 1
    leaf_bits = n_leaf.bit_length() - 1
    levels = row_bits + leaf_bits
    leaves, rank, _ = leaf_basis.shape
    blocks = couplings.shape[0]
    groups = rank // SUB
    params = pltpu.CompilerParams(vmem_limit_bytes=40 * 1024 * 1024)
    vmem = pl.BlockSpec(memory_space=pltpu.VMEM)
    smem = pl.BlockSpec(memory_space=pltpu.SMEM)
    hbm = pl.BlockSpec(memory_space=pltpu.HBM)
    steps = 4

    def like(array, kind=F32):
        return jax.ShapeDtypeStruct(array.shape, kind)

    def shape(*sizes, kind=F32):
        return jax.ShapeDtypeStruct(sizes, kind)

    def scratch(sets):
        return [
            pltpu.VMEM((sets, groups, rank, LANES), F32),
            pltpu.VMEM((sets, SUB, rank, LANES), F32),
            pltpu.VMEM((sets, SUB, SUB, LANES), F32),
        ]

    sets = leaves // SET
    half = rank // 2
    any_place = pl.BlockSpec(memory_space=pl.ANY)
    *grams, own_gram, own_lift = pl.pallas_call(
        functools.partial(gram_kernel, steps, sets),
        in_specs=[hbm, hbm, vmem],
        out_specs=[vmem] * (sets + 2),
        out_shape=[shape(SET, rank, rank)] * sets + [shape(half, 2 * rank)] * 2,
        scratch_shapes=[
            pltpu.VMEM(leaf_basis.shape, F32),
            pltpu.VMEM(leaf_transfer.shape, F32),
            pltpu.SemaphoreType.DMA((steps,)),
            pltpu.SemaphoreType.DMA((steps,)),
        ],
        compiler_params=pltpu.CompilerParams(vmem_limit_bytes=52 * 1024 * 1024),
        cost_estimate=cost(10**9, 4 * 10**6),
        name="gram",
    )(leaf_basis, leaf_transfer, device_transfer)
    path = []
    carry = own_lift
    for bit in range(row_bits):
        got = swap(carry, "rows", bit)
        last = bit == row_bits - 1
        if bit == 1:
            own_factor, token = pl.pallas_call(
                own_kernel,
                in_specs=[vmem, any_place],
                out_specs=[vmem, vmem],
                out_shape=[shape(rank, 2 * rank), shape(SUB, LANES)],
                scratch_shapes=[pltpu.VMEM((rank, rank), F32)] + scratch(1),
                compiler_params=params,
                cost_estimate=cost(5 * 10**9, 8 * 10**6),
                name="own",
            )(own_gram, carry)
        gram, carry = pl.pallas_call(
            functools.partial(row_hop_kernel, bit, last),
            in_specs=[vmem] * 4 + [any_place],
            out_specs=[vmem, vmem],
            out_shape=[shape(half, 2 * rank), shape(rank if last else half, 2 * rank)],
            compiler_params=params,
            name="row_hop",
        )(carry, got, own_gram, upper_transfer, token if bit == 1 else own_gram)
        path.append(gram)
    factors = []
    for bit in range(leaf_bits - 1):
        got = swap(carry, "leaf", bit)
        if len(factors) < sets:
            factor, token = pl.pallas_call(
                factor_kernel,
                in_specs=[vmem, any_place],
                out_specs=[vmem, vmem],
                out_shape=[shape(SET, rank, 2 * rank), shape(SUB, LANES)],
                scratch_shapes=scratch(1),
                compiler_params=params,
                cost_estimate=cost(5 * 10**9, 8 * 10**6),
                name="factor",
            )(grams[len(factors)], carry)
            factors.append(factor)
        gram, carry = pl.pallas_call(
            functools.partial(leaf_hop_kernel, bit),
            in_specs=[vmem] * 3 + [any_place],
            out_specs=[vmem, vmem],
            out_shape=[shape(half, 2 * rank), shape(half + (half + SUB) * 2**bit, 2 * rank)],
            compiler_params=params,
            name="leaf_hop",
        )(carry, got, upper_transfer, token)
        path.append(gram)
    got = swap(carry, "leaf", leaf_bits - 1)
    leaf_orth, leaf_bridge, split = pl.pallas_call(
        functools.partial(leaf_kernel, steps, sets),
        in_specs=[vmem] * 4 + [any_place] + [vmem] * sets,
        out_specs=[hbm, hbm, vmem],
        out_shape=[
            like(leaf_basis),
            like(leaf_transfer),
            shape(blocks, rank, 2 * rank, kind=B16),
        ],
        scratch_shapes=[
            pltpu.VMEM(leaf_basis.shape, F32),
            pltpu.VMEM(leaf_transfer.shape, F32),
            pltpu.SemaphoreType.DMA((steps,)),
            pltpu.SemaphoreType.DMA((steps,)),
        ],
        compiler_params=params,
        cost_estimate=cost(5 * 10**9, 8 * 10**6),
        name="leaf",
    )(leaf_basis, leaf_transfer, couplings, own_factor, carry, *factors)
    sets = -(-(levels + n_leaf) // SET)
    new_transfers, coupled = pl.pallas_call(
        functools.partial(top_kernel, n_rows, n_leaf, steps),
        in_specs=[vmem] * (levels + 5) + [smem],
        out_specs=[hbm, hbm],
        out_shape=[shape(1, levels, rank, rank), like(couplings)],
        scratch_shapes=[
            pltpu.VMEM((sets * SET, rank, rank), F32),
            pltpu.VMEM((sets * SET, rank, 2 * rank), F32),
            pltpu.VMEM((n_leaf, rank, 4 * rank), B16),
            pltpu.VMEM((1, levels, rank, rank), F32),
            pltpu.VMEM(couplings.shape, F32),
            pltpu.SemaphoreType.DMA(()),
            pltpu.SemaphoreType.DMA((steps,)),
        ]
        + scratch(sets),
        compiler_params=params,
        name="top",
    )(carry, got, *path, upper_transfer, device_transfer, own_factor, split, couple_offset)
    return (leaf_orth, leaf_bridge, new_transfers, coupled)


def solution(mesh):
    in_specs = (
        P(("leaf", "rows"), None, None),
        P(("leaf", "rows"), None, None),
        P(("leaf", "rows"), None, None),
        P(),
        P(("leaf", "rows"), None, None),
        P(("leaf", "rows")),
    )
    out_specs = (
        P(("leaf", "rows"), None, None),
        P(("leaf", "rows"), None, None),
        P(("leaf", "rows"), None, None, None),
        P(("leaf", "rows"), None, None),
    )
    return jax.shard_map(
        per_device, mesh=mesh, in_specs=in_specs, out_specs=out_specs, check_vma=False
    )
```

```python
import functools

import jax
import jax.numpy as jnp
from jax import lax
from jax.experimental import pallas as pl
from jax.experimental.pallas import tpu as pltpu
from jax.sharding import PartitionSpec as P

HIGH = lax.Precision.HIGHEST
SUB = 8
LANES = 128
SET = LANES // SUB
GROUP = 4
F32 = jnp.float32
B16 = jnp.bfloat16


def mm(a, b, dims=((1,), (0,)), precision=None):
    return lax.dot_general(
        a, b, (dims, ((), ())), precision=precision, preferred_element_type=F32
    )


def mm_nt(a, b, precision=None):
    return mm(a, b, ((1,), (1,)), precision)


def mm_tn(a, b, precision=None):
    return mm(a, b, ((0,), (0,)), precision)


def lift(gram, trans):
    return mm_tn(trans, mm(gram, trans, precision=HIGH), HIGH)


def halves(x):
    high = x.astype(B16).astype(F32)
    return high, x - high


def pair(x):
    return jnp.concatenate(halves(x), axis=1).astype(B16)


def twice(x):
    return jnp.concatenate([x, x], axis=1)


def tall(x):
    high, low = halves(x)
    high, low = high.astype(B16), low.astype(B16)
    return jnp.concatenate([high, high, low, low], axis=0)


def broad(x):
    high, low = halves(x)
    return jnp.concatenate([high, high, low, low], axis=1).astype(B16)


def fold(x):
    half = x.shape[1] // 2
    return x[:, :half] + x[:, half:]


def spread(value, at):
    return jnp.broadcast_to(value[at : at + 1, :], (SUB, LANES))


def added(terms):
    while len(terms) > 1:
        terms = [sum(terms[n : n + 2][1:], terms[n]) for n in range(0, len(terms), 2)]
    return terms[0]


def load_sets(flat, w_ref, alone=False):
    sets, groups, rank = w_ref.shape[0], w_ref.shape[1], w_ref.shape[2]
    for t in range(sets):
        for ib in range(groups):
            rows = [
                flat[pl.ds(t * SET * rank + ib * SUB + s, SET, stride=0 if alone else rank), :]
                for s in range(SUB)
            ]
            w_ref[t, ib] = jnp.concatenate(rows, axis=0).T


def eliminate(w_ref, g_ref, c_ref, out, alone=False):
    sets, groups, rank = w_ref.shape[0], w_ref.shape[1], w_ref.shape[2]
    place = lax.broadcasted_iota(jnp.int32, (SUB, LANES), 0)
    lane = lax.broadcasted_iota(jnp.int32, (SUB, LANES), 1)
    group = lane // SET
    picks = [p * SET + lane % SET for p in range(SUB)]

    def tile(t, ib, jv):
        return w_ref[t, ib, pl.ds(jv * SUB, SUB), :]

    def picked(value, p):
        return jnp.take_along_axis(value, picks[p], axis=1, mode="promise_in_bounds")

    def copied(ref, row):
        return ref[pl.ds(row, SUB, stride=0), :]

    def corner(t, kb):
        diagonal = tile(t, kb, kb)
        for p in range(SUB):
            c_ref[t, p] = picked(diagonal, p)
        a = {(p, q): copied(c_ref.at[t, p], q) for p in range(SUB) for q in range(p + 1)}
        low, inverses, roots = {}, [], []
        yield None
        for q in range(SUB):
            squares = {p: a[p, q] * a[q + 1, q] for p in range(q + 1, SUB)}
            inverse = pl.reciprocal(a[q, q], approx=True)
            inverses.append(inverse)
            roots.append(lax.rsqrt(a[q, q]))
            yield None
            for p in range(q + 1, SUB):
                a[p, q + 1] = a[p, q + 1] - squares[p] * inverse
            for p in range(q + 1, SUB):
                low[p, q] = a[p, q] * inverse
            for p in range(q + 2, SUB):
                for r in range(q + 2, p + 1):
                    a[p, r] = a[p, r] - low[p, q] * a[r, q]
        mult = {}
        for p in range(1, SUB):
            if p % 2 == 0:
                yield None
            for q in range(p):
                terms = [low[p, q]] + [low[p, r] * mult[r, q] for r in range(q + 1, p)]
                mult[p, q] = -added(terms)
        yield a, mult, inverses, roots

    def merged(parts):
        value = parts[0]
        for p in range(1, SUB):
            value = jnp.where(group == p, parts[p], value)
        return value

    def panel(t, kb, jv):
        value = tile(t, kb, jv)
        for p in range(SUB):
            g_ref[kb % 2, t, p, pl.ds(jv * SUB, SUB), :] = picked(value, p)

    def store(t, kb, a, mult, inverses, roots):
        del inverses
        root = merged(roots)
        zero = jnp.zeros((SUB, LANES), F32)
        lanes = [
            merged([mult[p, q] if p > q else zero for p in range(SUB)]) for q in range(SUB - 1)
        ]
        pivots = merged([a[p, p] for p in range(SUB)])
        upper, lower = [], []
        for jv in range(groups):
            if jv == kb:
                value = zero
                for r in range(SUB):
                    row = lanes[r] if r < SUB - 1 else zero
                    for p in range(r):
                        row = jnp.where(group == p, a[r, p], row)
                    value = jnp.where(place == r, row, value)
                final = value * root
                middle = jnp.where(place == group, pivots * root, 0.0)
                upper.append(jnp.where(place > group, final, middle))
                middle = jnp.where(place == group, root, 0.0)
                lower.append(jnp.where(place < group, final, middle))
                continue
            terms = [lanes[q] * g_ref[kb % 2, t, q, pl.ds(jv * SUB, SUB), :] for q in range(SUB - 1)]
            final = added([tile(t, kb, jv)] + terms) * root
            upper.append(final if jv > kb else zero)
            lower.append(final if jv < kb else zero)
        turned = jnp.concatenate(upper + lower, axis=0).T
        for s in range(SUB):
            if alone:
                out[pl.ds(kb * SUB + s, 1), :] = turned[s * SET : s * SET + 1]
            else:
                out[pl.ds(t * SET * rank + kb * SUB + s, SET, stride=rank), :] = turned[
                    s * SET : (s + 1) * SET
                ]

    def weights(t, kb, ib, mult, inverses):
        columns = [copied(w_ref.at[t, ib], kb * SUB + q) for q in range(SUB)]
        found = []
        for q in range(SUB):
            term = added([columns[q]] + [mult[q, r] * columns[r] for r in range(q)])
            found.append(term * inverses[q])
        return [
            added([found[r]] + [found[q] * mult[q, r] for q in range(r + 1, SUB)])
            for r in range(SUB)
        ]

    def trail(t, kb, ib, jv, found):
        if jv == kb:
            value = -found[0]
            for r in range(1, SUB):
                value = jnp.where(place == r, -found[r], value)
        else:
            terms = [found[r] * g_ref[kb % 2, t, r, pl.ds(jv * SUB, SUB), :] for r in range(SUB)]
            value = tile(t, ib, jv) - added(terms)
        w_ref[t, ib, pl.ds(jv * SUB, SUB), :] = value

    def woven(chains, work):
        results = [None] * len(chains)
        steps = SUB + 5
        for step in range(steps):
            for n, chain in enumerate(chains):
                results[n] = next(chain)
            done = len(work) * step // steps
            for item in work[done : len(work) * (step + 1) // steps]:
                item()
        return results

    def gathers(kb):
        order = list(range(kb + 1, groups)) + list(range(kb))
        return [functools.partial(panel, t, kb, jv) for jv in order for t in range(sets)]

    def bulk(t, kb, ib, state):
        founds = {}

        def prepare():
            founds[ib] = weights(t, kb, ib, *state[1:3])

        def subtract(jv):
            trail(t, kb, ib, jv, founds[ib])

        return [prepare] + [functools.partial(subtract, jv) for jv in range(groups)]

    states = woven([corner(t, 0) for t in range(sets)], gathers(0))
    for kb in range(groups):
        if kb + 1 == groups:
            for t in range(sets):
                store(t, kb, *states[t])
            break
        for t in range(sets):
            found = weights(t, kb, kb + 1, *states[t][1:3])
            for jv in [kb + 1] + [jv for jv in range(groups) if jv != kb + 1]:
                trail(t, kb, kb + 1, jv, found)
        work = gathers(kb + 1)
        for ib in range(kb + 2, groups):
            for t in range(sets):
                work += bulk(t, kb, ib, states[t])
        work += [functools.partial(store, t, kb, *states[t]) for t in range(sets)]
        states = woven([corner(t, kb + 1) for t in range(sets)], work)


def pack(x):
    half = x.shape[0] // 2
    return jnp.concatenate([x[:half], x[half:]], axis=1)


def unpack(x):
    half = x.shape[1] // 2
    return jnp.concatenate([x[:, :half], x[:, half:]], axis=0)


def gram_kernel(steps, sets, basis_hbm, trans_hbm, dev_ref, *refs):
    grams_refs = refs[:sets]
    own_ref, lift_ref, basis_ref, trans_ref, basis_sem, trans_sem = refs[sets:]
    leaves, rank = basis_ref.shape[0], basis_ref.shape[1]
    chunk = leaves // steps
    copies = []
    for step in range(steps):
        span = pl.ds(step * chunk, chunk)
        copies.append(
            (
                pltpu.make_async_copy(basis_hbm.at[span], basis_ref.at[span], basis_sem.at[step]),
                pltpu.make_async_copy(trans_hbm.at[span], trans_ref.at[span], trans_sem.at[step]),
            )
        )
        for copy in copies[-1]:
            copy.start()
    groups = leaves // GROUP
    products, parts, edges, rights = {}, {}, {}, {}
    total = None
    for stage in range(groups + 3):
        if stage < groups:
            if stage * GROUP % chunk == 0:
                for copy in copies[stage * GROUP // chunk]:
                    copy.wait()
            twos = []
            for n in range(stage * GROUP, (stage + 1) * GROUP):
                twos.append(jnp.concatenate(halves(basis_ref[n]), axis=0).astype(B16))
            products[stage] = [mm_nt(two, two) for two in twos]
        group = stage - 1
        if 0 <= group < groups:
            edges[group] = [
                pair(trans_ref[n]) for n in range(group * GROUP, (group + 1) * GROUP)
            ]
            parts[group] = []
            for n, product in enumerate(products.pop(group)):
                gram = fold(product[:rank] + product[rank:])
                at = group * GROUP + n
                grams_refs[at // SET][at % SET] = gram
                both = jnp.concatenate(halves(gram), axis=0).astype(B16)
                parts[group].append(mm(both, edges[group][n]))
        group = stage - 2
        if 0 <= group < groups:
            rights[group] = [pair(fold(part[:rank] + part[rank:])) for part in parts.pop(group)]
        group = stage - 3
        if 0 <= group < groups and group % 2:
            left = jnp.concatenate(edges.pop(group - 1) + edges.pop(group), axis=0)
            right = jnp.concatenate(rights.pop(group - 1) + rights.pop(group), axis=0)
            term = mm_tn(left, right)
            total = term if total is None else total + term
    gram = fold(total[:rank] + total[rank:])
    own_ref[...] = pack(gram)
    lift_ref[...] = pack(lift(gram, dev_ref[0]))


def factor_kernel(grams_ref, after_ref, out_ref, token_ref, w_ref, g_ref, c_ref):
    del after_ref
    count, rank = grams_ref.shape[0], grams_ref.shape[1]
    load_sets(grams_ref.reshape(count * rank, rank), w_ref)
    eliminate(w_ref, g_ref, c_ref, out_ref.reshape(count * rank, 2 * rank))
    token_ref[...] = jnp.zeros(token_ref.shape, F32)


def own_kernel(own_ref, after_ref, out_ref, token_ref, full_ref, w_ref, g_ref, c_ref):
    del after_ref
    full_ref[...] = unpack(own_ref[...])
    load_sets(full_ref, w_ref, alone=True)
    eliminate(w_ref, g_ref, c_ref, out_ref, alone=True)
    token_ref[...] = jnp.zeros(token_ref.shape, F32)


def row_hop_kernel(
    bit, last, mine_ref, got_ref, own_ref, upper_ref, after_ref, path_ref, next_ref
):
    del after_ref
    n_rows, n_leaf = lax.axis_size("rows"), lax.axis_size("leaf")
    level = (n_rows * n_leaf).bit_length() - 2 - bit
    myself = lax.axis_index("leaf") * n_rows + lax.axis_index("rows")
    packed = mine_ref[...] + got_ref[...]
    path_ref[...] = packed
    lifted = pack(lift(unpack(packed), upper_ref[2**level - 2 + (myself >> (bit + 1))]))
    if last:
        half = lifted.shape[0]
        next_ref[:half] = lifted
        next_ref[half:] = own_ref[...]
    else:
        next_ref[...] = lifted


def packed_places(half):
    row = lax.broadcasted_iota(jnp.int32, (half, 4 * half), 0)
    lane = lax.broadcasted_iota(jnp.int32, (half, 4 * half), 1)
    return jnp.where(lane < 2 * half, row, row + half), lane % (2 * half)


def join(a, b):
    half = a.shape[0]
    row, column = packed_places(half)
    diagonal = jnp.sum(jnp.where(row == column, a, 0.0), axis=0, keepdims=True)
    joint = jnp.where(row > column, a, b)
    return jnp.concatenate([joint, jnp.broadcast_to(diagonal, (SUB, 4 * half))], axis=0)


def part(x):
    half = x.shape[0] - SUB
    joint = unpack(x[:half])
    turned = joint.T
    row = lax.broadcasted_iota(jnp.int32, joint.shape, 0)
    column = lax.broadcasted_iota(jnp.int32, joint.shape, 1)
    diagonal = jnp.broadcast_to(fold(x[half : half + 1]), joint.shape)
    first = jnp.where(row > column, joint, jnp.where(row == column, diagonal, turned))
    return first, jnp.where(row <= column, joint, turned)


def leaf_hop_kernel(bit, mine_ref, got_ref, upper_ref, after_ref, path_ref, next_ref):
    del after_ref
    half = path_ref.shape[0]
    level = lax.axis_size("leaf").bit_length() - 2 - bit
    packed = mine_ref[:half] + got_ref[:half]
    path_ref[...] = packed
    node = lax.axis_index("leaf") >> (bit + 1)
    next_ref[:half] = pack(lift(unpack(packed), upper_ref[2**level - 2 + node]))
    if bit == 0:
        next_ref[half:] = join(mine_ref[half:], got_ref[half:])
    else:
        size = mine_ref.shape[0] - half
        next_ref[half : half + size] = mine_ref[half:]
        next_ref[half + size :] = got_ref[half:]


def leaf_kernel(steps, sets, basis_ref, trans_ref, coup_ref, own_ref, after_ref, *refs):
    del after_ref
    factor_refs = refs[:sets]
    (
        orth_hbm,
        bridge_hbm,
        split_ref,
        orth_ref,
        bridge_ref,
        orth_sem,
        bridge_sem,
    ) = refs[sets:]
    leaves, rank = basis_ref.shape[0], basis_ref.shape[1]
    chunk = leaves // steps
    lane = lax.broadcasted_iota(jnp.int32, (rank, 2 * rank), 1)
    own_upper = twice(pair(own_ref[:, :rank]))
    own_inverse = broad(own_ref[:, rank:])
    copies = []

    def send(source, target, sem):
        copies.append(pltpu.make_async_copy(source, target, sem))
        copies[-1].start()

    for step in range(steps):
        moved = []
        for n in range(step * chunk, (step + 1) * chunk):
            high, low = halves(factor_refs[n // SET][n % SET])
            low = jnp.concatenate([low[:, rank:], low[:, :rank]], axis=1)
            upper = jnp.where(lane < rank, high, low).astype(B16)
            inverse = jnp.where(lane < rank, low, high).astype(B16)
            moved.append(mm(twice(upper), tall(trans_ref[n])))
            orth_ref[n] = mm(twice(inverse), tall(basis_ref[n]))
        span = pl.ds(step * chunk, chunk)
        send(orth_ref.at[span], orth_hbm.at[span], orth_sem.at[step])
        moved = twice(pair(jnp.concatenate(moved, axis=0)))
        bridge_ref[span] = mm_nt(moved, own_inverse).reshape(chunk, rank, rank)
        send(bridge_ref.at[span], bridge_hbm.at[span], bridge_sem.at[step])
    for b in range(coup_ref.shape[0]):
        split_ref[b] = pair(mm(own_upper, tall(coup_ref[b])))
    for copy in copies:
        copy.wait()


def top_kernel(n_rows, n_leaf, steps, mine_ref, got_ref, *refs):
    levels = (n_rows * n_leaf).bit_length() - 1
    path_refs = refs[: levels - 1]
    (
        upper_ref,
        dev_ref,
        own_ref,
        split_ref,
        offset_ref,
        fresh_hbm,
        coupled_hbm,
        grams_ref,
        factor_ref,
        cols_ref,
        fresh_ref,
        coupled_ref,
        fresh_sem,
        coupled_sem,
        w_ref,
        g_ref,
        c_ref,
    ) = refs[levels - 1 :]
    rank = grams_ref.shape[1]
    branch, row = lax.axis_index("leaf"), lax.axis_index("rows")
    myself = branch * n_rows + row
    for n in range(levels - 1):
        grams_ref[n] = unpack(path_refs[n][...])
    half = rank // 2
    grams_ref[levels - 1] = unpack(mine_ref[:half] + got_ref[:half])
    pairs = n_leaf // 4
    for n in range(pairs):
        for place, ref in ((0, mine_ref), (pairs, got_ref)):
            joint = ref[pl.ds(half + n * (half + SUB), half + SUB), :]
            at = levels + 2 * (place + n)
            grams_ref[at], grams_ref[at + 1] = part(joint)
    count = grams_ref.shape[0]
    load_sets(grams_ref.reshape(count * rank, rank), w_ref)
    eliminate(w_ref, g_ref, c_ref, factor_ref.reshape(count * rank, 2 * rank))
    for n in range(n_leaf):
        cols_ref[n] = broad(factor_ref[levels + n, :, :rank])
    copies = []

    def send(source, target, sem):
        copies.append(pltpu.make_async_copy(source, target, sem))
        copies[-1].start()

    lows, edges, inverses = [twice(pair(own_ref[:, :rank]))], [tall(dev_ref[0])], []
    for k in range(levels):
        inverses.append(broad(factor_ref[k, :, rank:]))
        if k:
            lows.append(twice(pair(factor_ref[k - 1, :, :rank])))
            edges.append(tall(upper_ref[2 ** (levels - k) - 2 + (myself >> k)]))
    inner = [mm(low, edge) for low, edge in zip(lows, edges)]
    inner = [twice(pair(value)) for value in inner]
    for k in range(levels):
        fresh_ref[0, k] = mm_nt(inner[k], inverses[k])
    send(fresh_ref, fresh_hbm, fresh_sem)
    blocks = split_ref.shape[0]
    chunk = blocks // steps
    for step in range(steps):
        for b in range(step * chunk, (step + 1) * chunk):
            target = lax.rem(myself + offset_ref[b], n_rows * n_leaf)
            column = cols_ref[(target // n_rows) ^ branch]
            coupled_ref[b] = mm_nt(twice(split_ref[b]), column)
        span = pl.ds(step * chunk, chunk)
        send(coupled_ref.at[span], coupled_hbm.at[span], coupled_sem.at[step])
    for copy in copies:
        copy.wait()


def swap(value, axis, bit):
    pairs = [(source, source ^ 2**bit) for source in range(lax.axis_size(axis))]
    return lax.ppermute(value, axis, pairs)


def cost(flops, moved):
    return pl.CostEstimate(flops=flops, bytes_accessed=moved, transcendentals=0)


def per_device(
    leaf_basis, leaf_transfer, device_transfer, upper_transfer, couplings, couple_offset
):
    n_rows = lax.axis_size("rows")
    n_leaf = lax.axis_size("leaf")
    row_bits = n_rows.bit_length() - 1
    leaf_bits = n_leaf.bit_length() - 1
    levels = row_bits + leaf_bits
    leaves, rank, _ = leaf_basis.shape
    blocks = couplings.shape[0]
    groups = rank // SUB
    params = pltpu.CompilerParams(vmem_limit_bytes=40 * 1024 * 1024)
    vmem = pl.BlockSpec(memory_space=pltpu.VMEM)
    smem = pl.BlockSpec(memory_space=pltpu.SMEM)
    hbm = pl.BlockSpec(memory_space=pltpu.HBM)
    steps = 4

    def like(array, kind=F32):
        return jax.ShapeDtypeStruct(array.shape, kind)

    def shape(*sizes, kind=F32):
        return jax.ShapeDtypeStruct(sizes, kind)

    def scratch(sets):
        return [
            pltpu.VMEM((sets, groups, rank, LANES), F32),
            pltpu.VMEM((2, sets, SUB, rank, LANES), F32),
            pltpu.VMEM((sets, SUB, SUB, LANES), F32),
        ]

    sets = leaves // SET
    half = rank // 2
    any_place = pl.BlockSpec(memory_space=pl.ANY)
    *grams, own_gram, own_lift = pl.pallas_call(
        functools.partial(gram_kernel, steps, sets),
        in_specs=[hbm, hbm, vmem],
        out_specs=[vmem] * (sets + 2),
        out_shape=[shape(SET, rank, rank)] * sets + [shape(half, 2 * rank)] * 2,
        scratch_shapes=[
            pltpu.VMEM(leaf_basis.shape, F32),
            pltpu.VMEM(leaf_transfer.shape, F32),
            pltpu.SemaphoreType.DMA((steps,)),
            pltpu.SemaphoreType.DMA((steps,)),
        ],
        compiler_params=pltpu.CompilerParams(vmem_limit_bytes=52 * 1024 * 1024),
        cost_estimate=cost(10**9, 4 * 10**6),
        name="gram",
    )(leaf_basis, leaf_transfer, device_transfer)
    path = []
    carry = own_lift
    for bit in range(row_bits):
        got = swap(carry, "rows", bit)
        last = bit == row_bits - 1
        if bit == 1:
            own_factor, token = pl.pallas_call(
                own_kernel,
                in_specs=[vmem, any_place],
                out_specs=[vmem, vmem],
                out_shape=[shape(rank, 2 * rank), shape(SUB, LANES)],
                scratch_shapes=[pltpu.VMEM((rank, rank), F32)] + scratch(1),
                compiler_params=params,
                cost_estimate=cost(5 * 10**9, 8 * 10**6),
                name="own",
            )(own_gram, carry)
        gram, carry = pl.pallas_call(
            functools.partial(row_hop_kernel, bit, last),
            in_specs=[vmem] * 4 + [any_place],
            out_specs=[vmem, vmem],
            out_shape=[shape(half, 2 * rank), shape(rank if last else half, 2 * rank)],
            compiler_params=params,
            name="row_hop",
        )(carry, got, own_gram, upper_transfer, token if bit == 1 else own_gram)
        path.append(gram)
    factors = []
    for bit in range(leaf_bits - 1):
        got = swap(carry, "leaf", bit)
        if len(factors) < sets:
            factor, token = pl.pallas_call(
                factor_kernel,
                in_specs=[vmem, any_place],
                out_specs=[vmem, vmem],
                out_shape=[shape(SET, rank, 2 * rank), shape(SUB, LANES)],
                scratch_shapes=scratch(1),
                compiler_params=params,
                cost_estimate=cost(5 * 10**9, 8 * 10**6),
                name="factor",
            )(grams[len(factors)], carry)
            factors.append(factor)
        gram, carry = pl.pallas_call(
            functools.partial(leaf_hop_kernel, bit),
            in_specs=[vmem] * 3 + [any_place],
            out_specs=[vmem, vmem],
            out_shape=[shape(half, 2 * rank), shape(half + (half + SUB) * 2**bit, 2 * rank)],
            compiler_params=params,
            name="leaf_hop",
        )(carry, got, upper_transfer, token)
        path.append(gram)
    got = swap(carry, "leaf", leaf_bits - 1)
    leaf_orth, leaf_bridge, split = pl.pallas_call(
        functools.partial(leaf_kernel, steps, sets),
        in_specs=[vmem] * 4 + [any_place] + [vmem] * sets,
        out_specs=[hbm, hbm, vmem],
        out_shape=[
            like(leaf_basis),
            like(leaf_transfer),
            shape(blocks, rank, 2 * rank, kind=B16),
        ],
        scratch_shapes=[
            pltpu.VMEM(leaf_basis.shape, F32),
            pltpu.VMEM(leaf_transfer.shape, F32),
            pltpu.SemaphoreType.DMA((steps,)),
            pltpu.SemaphoreType.DMA((steps,)),
        ],
        compiler_params=params,
        cost_estimate=cost(5 * 10**9, 8 * 10**6),
        name="leaf",
    )(leaf_basis, leaf_transfer, couplings, own_factor, carry, *factors)
    sets = -(-(levels + n_leaf) // SET)
    new_transfers, coupled = pl.pallas_call(
        functools.partial(top_kernel, n_rows, n_leaf, steps),
        in_specs=[vmem] * (levels + 5) + [smem],
        out_specs=[hbm, hbm],
        out_shape=[shape(1, levels, rank, rank), like(couplings)],
        scratch_shapes=[
            pltpu.VMEM((sets * SET, rank, rank), F32),
            pltpu.VMEM((sets * SET, rank, 2 * rank), F32),
            pltpu.VMEM((n_leaf, rank, 4 * rank), B16),
            pltpu.VMEM((1, levels, rank, rank), F32),
            pltpu.VMEM(couplings.shape, F32),
            pltpu.SemaphoreType.DMA(()),
            pltpu.SemaphoreType.DMA((steps,)),
        ]
        + scratch(sets),
        compiler_params=params,
        name="top",
    )(carry, got, *path, upper_transfer, device_transfer, own_factor, split, couple_offset)
    return (leaf_orth, leaf_bridge, new_transfers, coupled)


def solution(mesh):
    in_specs = (
        P(("leaf", "rows"), None, None),
        P(("leaf", "rows"), None, None),
        P(("leaf", "rows"), None, None),
        P(),
        P(("leaf", "rows"), None, None),
        P(("leaf", "rows")),
    )
    out_specs = (
        P(("leaf", "rows"), None, None),
        P(("leaf", "rows"), None, None),
        P(("leaf", "rows"), None, None, None),
        P(("leaf", "rows"), None, None),
    )
    return jax.shard_map(
        per_device, mesh=mesh, in_specs=in_specs, out_specs=out_specs, check_vma=False
    )
```

```python
import functools

import jax
import jax.numpy as jnp
from jax import lax
from jax.experimental import pallas as pl
from jax.experimental.pallas import tpu as pltpu
from jax.sharding import PartitionSpec as P

HIGH = lax.Precision.HIGHEST
SUB = 8
LANES = 128
SET = LANES // SUB
GROUP = 4
F32 = jnp.float32
B16 = jnp.bfloat16


def mm(a, b, dims=((1,), (0,)), precision=None):
    return lax.dot_general(
        a, b, (dims, ((), ())), precision=precision, preferred_element_type=F32
    )


def mm_nt(a, b, precision=None):
    return mm(a, b, ((1,), (1,)), precision)


def mm_tn(a, b, precision=None):
    return mm(a, b, ((0,), (0,)), precision)


def lift(gram, trans):
    return mm_tn(trans, mm(gram, trans, precision=HIGH), HIGH)


def halves(x):
    high = x.astype(B16).astype(F32)
    return high, x - high


def pair(x):
    return jnp.concatenate(halves(x), axis=1).astype(B16)


def twice(x):
    return jnp.concatenate([x, x], axis=1)


def tall(x):
    high, low = halves(x)
    high, low = high.astype(B16), low.astype(B16)
    return jnp.concatenate([high, high, low, low], axis=0)


def broad(x):
    high, low = halves(x)
    return jnp.concatenate([high, high, low, low], axis=1).astype(B16)


def fold(x):
    half = x.shape[1] // 2
    return x[:, :half] + x[:, half:]


def spread(value, at):
    return jnp.broadcast_to(value[at : at + 1, :], (SUB, LANES))


def added(terms):
    while len(terms) > 1:
        terms = [sum(terms[n : n + 2][1:], terms[n]) for n in range(0, len(terms), 2)]
    return terms[0]


def load_sets(flat, w_ref, alone=False):
    sets, groups, rank = w_ref.shape[0], w_ref.shape[1], w_ref.shape[2]
    for t in range(sets):
        for ib in range(groups):
            rows = [
                flat[pl.ds(t * SET * rank + ib * SUB + s, SET, stride=0 if alone else rank), :]
                for s in range(SUB)
            ]
            w_ref[t, ib] = jnp.concatenate(rows, axis=0).T


def eliminate(w_ref, g_ref, c_ref, pick_ref, out, alone=False):
    sets, groups, rank = w_ref.shape[0], w_ref.shape[1], w_ref.shape[2]
    place = lax.broadcasted_iota(jnp.int32, (SUB, LANES), 0)
    lane = lax.broadcasted_iota(jnp.int32, (SUB, LANES), 1)
    group = lane // SET
    picks = [p * SET + lane % SET for p in range(SUB)]

    def tile(t, ib, jv):
        return w_ref[t, ib, pl.ds(jv * SUB, SUB), :]

    def picked(value, p):
        return jnp.take_along_axis(value, picks[p], axis=1, mode="promise_in_bounds")

    def copied(ref, row):
        return ref[pl.ds(row, SUB, stride=0), :]

    def corner(t, kb):
        diagonal = tile(t, kb, kb)
        for p in range(SUB):
            c_ref[t, p] = picked(diagonal, p)
        a = {(p, q): copied(c_ref.at[t, p], q) for p in range(SUB) for q in range(p + 1)}
        low, inverses, roots = {}, [], []
        yield None
        for q in range(SUB):
            squares = {p: a[p, q] * a[q + 1, q] for p in range(q + 1, SUB)}
            inverse = pl.reciprocal(a[q, q], approx=True)
            inverses.append(inverse)
            roots.append(lax.rsqrt(a[q, q]))
            yield None
            for p in range(q + 1, SUB):
                a[p, q + 1] = a[p, q + 1] - squares[p] * inverse
            for p in range(q + 1, SUB):
                low[p, q] = a[p, q] * inverse
            for p in range(q + 2, SUB):
                for r in range(q + 2, p + 1):
                    a[p, r] = a[p, r] - low[p, q] * a[r, q]
        mult = {}
        for p in range(1, SUB):
            if p % 2 == 0:
                yield None
            for q in range(p):
                terms = [low[p, q]] + [low[p, r] * mult[r, q] for r in range(q + 1, p)]
                mult[p, q] = -added(terms)
        yield a, mult, inverses, roots

    def merged(parts):
        value = parts[0]
        for p in range(1, SUB):
            value = jnp.where(group == p, parts[p], value)
        return value

    def panel(t, kb):
        parts = []

        def prepare():
            high, rest = halves(w_ref[t, kb])
            parts.append(jnp.concatenate([high, *halves(rest)], axis=1).astype(B16))

        def select(p):
            found = mm(parts[0], pick_ref[:, pl.ds(p * LANES, 2 * LANES)])
            g_ref[kb % 2, t, p] = found[:, :LANES]
            g_ref[kb % 2, t, p + 1] = found[:, LANES:]

        return [prepare] + [functools.partial(select, p) for p in range(0, SUB, 2)]

    def store(t, kb, a, mult, inverses, roots):
        del inverses
        root = merged(roots)
        zero = jnp.zeros((SUB, LANES), F32)
        lanes = [
            merged([mult[p, q] if p > q else zero for p in range(SUB)]) for q in range(SUB - 1)
        ]
        pivots = merged([a[p, p] for p in range(SUB)])
        upper, lower = [], []
        for jv in range(groups):
            if jv == kb:
                value = zero
                for r in range(SUB):
                    row = lanes[r] if r < SUB - 1 else zero
                    for p in range(r):
                        row = jnp.where(group == p, a[r, p], row)
                    value = jnp.where(place == r, row, value)
                final = value * root
                middle = jnp.where(place == group, pivots * root, 0.0)
                upper.append(jnp.where(place > group, final, middle))
                middle = jnp.where(place == group, root, 0.0)
                lower.append(jnp.where(place < group, final, middle))
                continue
            terms = [lanes[q] * g_ref[kb % 2, t, q, pl.ds(jv * SUB, SUB), :] for q in range(SUB - 1)]
            final = added([tile(t, kb, jv)] + terms) * root
            upper.append(final if jv > kb else zero)
            lower.append(final if jv < kb else zero)
        turned = jnp.concatenate(upper + lower, axis=0).T
        for s in range(SUB):
            if alone:
                out[pl.ds(kb * SUB + s, 1), :] = turned[s * SET : s * SET + 1]
            else:
                out[pl.ds(t * SET * rank + kb * SUB + s, SET, stride=rank), :] = turned[
                    s * SET : (s + 1) * SET
                ]

    def weights(t, kb, ib, mult, inverses):
        columns = [copied(w_ref.at[t, ib], kb * SUB + q) for q in range(SUB)]
        found = []
        for q in range(SUB):
            term = added([columns[q]] + [mult[q, r] * columns[r] for r in range(q)])
            found.append(term * inverses[q])
        return [
            added([found[r]] + [found[q] * mult[q, r] for q in range(r + 1, SUB)])
            for r in range(SUB)
        ]

    def trail(t, kb, ib, jv, found):
        if jv == kb:
            value = -found[0]
            for r in range(1, SUB):
                value = jnp.where(place == r, -found[r], value)
        else:
            terms = [found[r] * g_ref[kb % 2, t, r, pl.ds(jv * SUB, SUB), :] for r in range(SUB)]
            value = tile(t, ib, jv) - added(terms)
        w_ref[t, ib, pl.ds(jv * SUB, SUB), :] = value

    def woven(chains, work):
        results = [None] * len(chains)
        steps = SUB + 5
        for step in range(steps):
            for n, chain in enumerate(chains):
                results[n] = next(chain)
            done = len(work) * step // steps
            for item in work[done : len(work) * (step + 1) // steps]:
                item()
        return results

    def gathers(kb):
        return [item for t in range(sets) for item in panel(t, kb)]

    def bulk(t, kb, ib, state):
        founds = {}

        def prepare():
            founds[ib] = weights(t, kb, ib, *state[1:3])

        def subtract(jv):
            trail(t, kb, ib, jv, founds[ib])

        return [prepare] + [functools.partial(subtract, jv) for jv in range(groups)]

    row = lax.broadcasted_iota(jnp.int32, (LANES, SUB * LANES), 0)
    column = lax.broadcasted_iota(jnp.int32, (LANES, SUB * LANES), 1)
    wanted = column // LANES * SET + column % SET
    for n in range(3):
        chosen = jnp.where(row == wanted, 1.0, 0.0).astype(B16)
        pick_ref[pl.ds(n * LANES, LANES), :] = chosen
    states = woven([corner(t, 0) for t in range(sets)], gathers(0))
    for kb in range(groups):
        if kb + 1 == groups:
            for t in range(sets):
                store(t, kb, *states[t])
            break
        for t in range(sets):
            found = weights(t, kb, kb + 1, *states[t][1:3])
            for jv in [kb + 1] + [jv for jv in range(groups) if jv != kb + 1]:
                trail(t, kb, kb + 1, jv, found)
        work = gathers(kb + 1)
        for ib in range(kb + 2, groups):
            for t in range(sets):
                work += bulk(t, kb, ib, states[t])
        work += [functools.partial(store, t, kb, *states[t]) for t in range(sets)]
        states = woven([corner(t, kb + 1) for t in range(sets)], work)


def pack(x):
    half = x.shape[0] // 2
    return jnp.concatenate([x[:half], x[half:]], axis=1)


def unpack(x):
    half = x.shape[1] // 2
    return jnp.concatenate([x[:, :half], x[:, half:]], axis=0)


def gram_kernel(steps, sets, basis_hbm, trans_hbm, dev_ref, *refs):
    grams_refs = refs[:sets]
    own_ref, lift_ref, basis_ref, trans_ref, basis_sem, trans_sem = refs[sets:]
    leaves, rank = basis_ref.shape[0], basis_ref.shape[1]
    chunk = leaves // steps
    copies = []
    for step in range(steps):
        span = pl.ds(step * chunk, chunk)
        copies.append(
            (
                pltpu.make_async_copy(basis_hbm.at[span], basis_ref.at[span], basis_sem.at[step]),
                pltpu.make_async_copy(trans_hbm.at[span], trans_ref.at[span], trans_sem.at[step]),
            )
        )
        for copy in copies[-1]:
            copy.start()
    groups = leaves // GROUP
    products, parts, edges, rights = {}, {}, {}, {}
    total = None
    for stage in range(groups + 3):
        if stage < groups:
            if stage * GROUP % chunk == 0:
                for copy in copies[stage * GROUP // chunk]:
                    copy.wait()
            twos = []
            for n in range(stage * GROUP, (stage + 1) * GROUP):
                twos.append(jnp.concatenate(halves(basis_ref[n]), axis=0).astype(B16))
            products[stage] = [mm_nt(two, two) for two in twos]
        group = stage - 1
        if 0 <= group < groups:
            edges[group] = [
                pair(trans_ref[n]) for n in range(group * GROUP, (group + 1) * GROUP)
            ]
            parts[group] = []
            for n, product in enumerate(products.pop(group)):
                gram = fold(product[:rank] + product[rank:])
                at = group * GROUP + n
                grams_refs[at // SET][at % SET] = gram
                both = jnp.concatenate(halves(gram), axis=0).astype(B16)
                parts[group].append(mm(both, edges[group][n]))
        group = stage - 2
        if 0 <= group < groups:
            rights[group] = [pair(fold(part[:rank] + part[rank:])) for part in parts.pop(group)]
        group = stage - 3
        if 0 <= group < groups and group % 2:
            left = jnp.concatenate(edges.pop(group - 1) + edges.pop(group), axis=0)
            right = jnp.concatenate(rights.pop(group - 1) + rights.pop(group), axis=0)
            term = mm_tn(left, right)
            total = term if total is None else total + term
    gram = fold(total[:rank] + total[rank:])
    own_ref[...] = pack(gram)
    lift_ref[...] = pack(lift(gram, dev_ref[0]))


def factor_kernel(grams_ref, after_ref, out_ref, token_ref, w_ref, g_ref, c_ref, pick_ref):
    del after_ref
    count, rank = grams_ref.shape[0], grams_ref.shape[1]
    load_sets(grams_ref.reshape(count * rank, rank), w_ref)
    eliminate(w_ref, g_ref, c_ref, pick_ref, out_ref.reshape(count * rank, 2 * rank))
    token_ref[...] = jnp.zeros(token_ref.shape, F32)


def own_kernel(own_ref, after_ref, out_ref, token_ref, full_ref, w_ref, g_ref, c_ref, pick_ref):
    del after_ref
    full_ref[...] = unpack(own_ref[...])
    load_sets(full_ref, w_ref, alone=True)
    eliminate(w_ref, g_ref, c_ref, pick_ref, out_ref, alone=True)
    token_ref[...] = jnp.zeros(token_ref.shape, F32)


def row_hop_kernel(
    bit, last, mine_ref, got_ref, own_ref, upper_ref, after_ref, path_ref, next_ref
):
    del after_ref
    n_rows, n_leaf = lax.axis_size("rows"), lax.axis_size("leaf")
    level = (n_rows * n_leaf).bit_length() - 2 - bit
    myself = lax.axis_index("leaf") * n_rows + lax.axis_index("rows")
    packed = mine_ref[...] + got_ref[...]
    path_ref[...] = packed
    lifted = pack(lift(unpack(packed), upper_ref[2**level - 2 + (myself >> (bit + 1))]))
    if last:
        half = lifted.shape[0]
        next_ref[:half] = lifted
        next_ref[half:] = own_ref[...]
    else:
        next_ref[...] = lifted


def packed_places(half):
    row = lax.broadcasted_iota(jnp.int32, (half, 4 * half), 0)
    lane = lax.broadcasted_iota(jnp.int32, (half, 4 * half), 1)
    return jnp.where(lane < 2 * half, row, row + half), lane % (2 * half)


def join(a, b):
    half = a.shape[0]
    row, column = packed_places(half)
    diagonal = jnp.sum(jnp.where(row == column, a, 0.0), axis=0, keepdims=True)
    joint = jnp.where(row > column, a, b)
    return jnp.concatenate([joint, jnp.broadcast_to(diagonal, (SUB, 4 * half))], axis=0)


def part(x):
    half = x.shape[0] - SUB
    joint = unpack(x[:half])
    turned = joint.T
    row = lax.broadcasted_iota(jnp.int32, joint.shape, 0)
    column = lax.broadcasted_iota(jnp.int32, joint.shape, 1)
    diagonal = jnp.broadcast_to(fold(x[half : half + 1]), joint.shape)
    first = jnp.where(row > column, joint, jnp.where(row == column, diagonal, turned))
    return first, jnp.where(row <= column, joint, turned)


def leaf_hop_kernel(bit, mine_ref, got_ref, upper_ref, after_ref, path_ref, next_ref):
    del after_ref
    half = path_ref.shape[0]
    level = lax.axis_size("leaf").bit_length() - 2 - bit
    packed = mine_ref[:half] + got_ref[:half]
    path_ref[...] = packed
    node = lax.axis_index("leaf") >> (bit + 1)
    next_ref[:half] = pack(lift(unpack(packed), upper_ref[2**level - 2 + node]))
    if bit == 0:
        next_ref[half:] = join(mine_ref[half:], got_ref[half:])
    else:
        size = mine_ref.shape[0] - half
        next_ref[half : half + size] = mine_ref[half:]
        next_ref[half + size :] = got_ref[half:]


def leaf_kernel(steps, sets, basis_ref, trans_ref, coup_ref, own_ref, after_ref, *refs):
    del after_ref
    factor_refs = refs[:sets]
    (
        orth_hbm,
        bridge_hbm,
        split_ref,
        orth_ref,
        bridge_ref,
        orth_sem,
        bridge_sem,
    ) = refs[sets:]
    leaves, rank = basis_ref.shape[0], basis_ref.shape[1]
    chunk = leaves // steps
    lane = lax.broadcasted_iota(jnp.int32, (rank, 2 * rank), 1)
    own_upper = twice(pair(own_ref[:, :rank]))
    own_inverse = broad(own_ref[:, rank:])
    copies = []

    def send(source, target, sem):
        copies.append(pltpu.make_async_copy(source, target, sem))
        copies[-1].start()

    for step in range(steps):
        moved = []
        for n in range(step * chunk, (step + 1) * chunk):
            high, low = halves(factor_refs[n // SET][n % SET])
            low = jnp.concatenate([low[:, rank:], low[:, :rank]], axis=1)
            upper = jnp.where(lane < rank, high, low).astype(B16)
            inverse = jnp.where(lane < rank, low, high).astype(B16)
            moved.append(mm(twice(upper), tall(trans_ref[n])))
            orth_ref[n] = mm(twice(inverse), tall(basis_ref[n]))
        span = pl.ds(step * chunk, chunk)
        send(orth_ref.at[span], orth_hbm.at[span], orth_sem.at[step])
        moved = twice(pair(jnp.concatenate(moved, axis=0)))
        bridge_ref[span] = mm_nt(moved, own_inverse).reshape(chunk, rank, rank)
        send(bridge_ref.at[span], bridge_hbm.at[span], bridge_sem.at[step])
    for b in range(coup_ref.shape[0]):
        split_ref[b] = pair(mm(own_upper, tall(coup_ref[b])))
    for copy in copies:
        copy.wait()


def top_kernel(n_rows, n_leaf, steps, mine_ref, got_ref, *refs):
    levels = (n_rows * n_leaf).bit_length() - 1
    path_refs = refs[: levels - 1]
    (
        upper_ref,
        dev_ref,
        own_ref,
        split_ref,
        offset_ref,
        fresh_hbm,
        coupled_hbm,
        grams_ref,
        factor_ref,
        cols_ref,
        fresh_ref,
        coupled_ref,
        fresh_sem,
        coupled_sem,
        w_ref,
        g_ref,
        c_ref,
        pick_ref,
    ) = refs[levels - 1 :]
    rank = grams_ref.shape[1]
    branch, row = lax.axis_index("leaf"), lax.axis_index("rows")
    myself = branch * n_rows + row
    for n in range(levels - 1):
        grams_ref[n] = unpack(path_refs[n][...])
    half = rank // 2
    grams_ref[levels - 1] = unpack(mine_ref[:half] + got_ref[:half])
    pairs = n_leaf // 4
    for n in range(pairs):
        for place, ref in ((0, mine_ref), (pairs, got_ref)):
            joint = ref[pl.ds(half + n * (half + SUB), half + SUB), :]
            at = levels + 2 * (place + n)
            grams_ref[at], grams_ref[at + 1] = part(joint)
    count = grams_ref.shape[0]
    for n in range(levels + n_leaf, count):
        grams_ref[n] = grams_ref[levels]
    load_sets(grams_ref.reshape(count * rank, rank), w_ref)
    eliminate(w_ref, g_ref, c_ref, pick_ref, factor_ref.reshape(count * rank, 2 * rank))
    for n in range(n_leaf):
        cols_ref[n] = broad(factor_ref[levels + n, :, :rank])
    copies = []

    def send(source, target, sem):
        copies.append(pltpu.make_async_copy(source, target, sem))
        copies[-1].start()

    lows, edges, inverses = [twice(pair(own_ref[:, :rank]))], [tall(dev_ref[0])], []
    for k in range(levels):
        inverses.append(broad(factor_ref[k, :, rank:]))
        if k:
            lows.append(twice(pair(factor_ref[k - 1, :, :rank])))
            edges.append(tall(upper_ref[2 ** (levels - k) - 2 + (myself >> k)]))
    inner = [mm(low, edge) for low, edge in zip(lows, edges)]
    inner = [twice(pair(value)) for value in inner]
    for k in range(levels):
        fresh_ref[0, k] = mm_nt(inner[k], inverses[k])
    send(fresh_ref, fresh_hbm, fresh_sem)
    blocks = split_ref.shape[0]
    chunk = blocks // steps
    for step in range(steps):
        for b in range(step * chunk, (step + 1) * chunk):
            target = lax.rem(myself + offset_ref[b], n_rows * n_leaf)
            column = cols_ref[(target // n_rows) ^ branch]
            coupled_ref[b] = mm_nt(twice(split_ref[b]), column)
        span = pl.ds(step * chunk, chunk)
        send(coupled_ref.at[span], coupled_hbm.at[span], coupled_sem.at[step])
    for copy in copies:
        copy.wait()


def swap(value, axis, bit):
    pairs = [(source, source ^ 2**bit) for source in range(lax.axis_size(axis))]
    return lax.ppermute(value, axis, pairs)


def cost(flops, moved):
    return pl.CostEstimate(flops=flops, bytes_accessed=moved, transcendentals=0)


def per_device(
    leaf_basis, leaf_transfer, device_transfer, upper_transfer, couplings, couple_offset
):
    n_rows = lax.axis_size("rows")
    n_leaf = lax.axis_size("leaf")
    row_bits = n_rows.bit_length() - 1
    leaf_bits = n_leaf.bit_length() - 1
    levels = row_bits + leaf_bits
    leaves, rank, _ = leaf_basis.shape
    blocks = couplings.shape[0]
    groups = rank // SUB
    params = pltpu.CompilerParams(vmem_limit_bytes=40 * 1024 * 1024)
    vmem = pl.BlockSpec(memory_space=pltpu.VMEM)
    smem = pl.BlockSpec(memory_space=pltpu.SMEM)
    hbm = pl.BlockSpec(memory_space=pltpu.HBM)
    steps = 4

    def like(array, kind=F32):
        return jax.ShapeDtypeStruct(array.shape, kind)

    def shape(*sizes, kind=F32):
        return jax.ShapeDtypeStruct(sizes, kind)

    def scratch(sets):
        return [
            pltpu.VMEM((sets, groups, rank, LANES), F32),
            pltpu.VMEM((2, sets, SUB, rank, LANES), F32),
            pltpu.VMEM((sets, SUB, SUB, LANES), F32),
            pltpu.VMEM((3 * LANES, SUB * LANES), B16),
        ]

    sets = leaves // SET
    half = rank // 2
    any_place = pl.BlockSpec(memory_space=pl.ANY)
    *grams, own_gram, own_lift = pl.pallas_call(
        functools.partial(gram_kernel, steps, sets),
        in_specs=[hbm, hbm, vmem],
        out_specs=[vmem] * (sets + 2),
        out_shape=[shape(SET, rank, rank)] * sets + [shape(half, 2 * rank)] * 2,
        scratch_shapes=[
            pltpu.VMEM(leaf_basis.shape, F32),
            pltpu.VMEM(leaf_transfer.shape, F32),
            pltpu.SemaphoreType.DMA((steps,)),
            pltpu.SemaphoreType.DMA((steps,)),
        ],
        compiler_params=pltpu.CompilerParams(vmem_limit_bytes=52 * 1024 * 1024),
        cost_estimate=cost(10**9, 4 * 10**6),
        name="gram",
    )(leaf_basis, leaf_transfer, device_transfer)
    path = []
    carry = own_lift
    for bit in range(row_bits):
        got = swap(carry, "rows", bit)
        last = bit == row_bits - 1
        if bit == 1:
            own_factor, token = pl.pallas_call(
                own_kernel,
                in_specs=[vmem, any_place],
                out_specs=[vmem, vmem],
                out_shape=[shape(rank, 2 * rank), shape(SUB, LANES)],
                scratch_shapes=[pltpu.VMEM((rank, rank), F32)] + scratch(1),
                compiler_params=params,
                cost_estimate=cost(5 * 10**9, 8 * 10**6),
                name="own",
            )(own_gram, carry)
        gram, carry = pl.pallas_call(
            functools.partial(row_hop_kernel, bit, last),
            in_specs=[vmem] * 4 + [any_place],
            out_specs=[vmem, vmem],
            out_shape=[shape(half, 2 * rank), shape(rank if last else half, 2 * rank)],
            compiler_params=params,
            name="row_hop",
        )(carry, got, own_gram, upper_transfer, token if bit == 1 else own_gram)
        path.append(gram)
    factors = []
    for bit in range(leaf_bits - 1):
        got = swap(carry, "leaf", bit)
        if len(factors) < sets:
            factor, token = pl.pallas_call(
                factor_kernel,
                in_specs=[vmem, any_place],
                out_specs=[vmem, vmem],
                out_shape=[shape(SET, rank, 2 * rank), shape(SUB, LANES)],
                scratch_shapes=scratch(1),
                compiler_params=params,
                cost_estimate=cost(5 * 10**9, 8 * 10**6),
                name="factor",
            )(grams[len(factors)], carry)
            factors.append(factor)
        gram, carry = pl.pallas_call(
            functools.partial(leaf_hop_kernel, bit),
            in_specs=[vmem] * 3 + [any_place],
            out_specs=[vmem, vmem],
            out_shape=[shape(half, 2 * rank), shape(half + (half + SUB) * 2**bit, 2 * rank)],
            compiler_params=params,
            name="leaf_hop",
        )(carry, got, upper_transfer, token)
        path.append(gram)
    got = swap(carry, "leaf", leaf_bits - 1)
    leaf_orth, leaf_bridge, split = pl.pallas_call(
        functools.partial(leaf_kernel, steps, sets),
        in_specs=[vmem] * 4 + [any_place] + [vmem] * sets,
        out_specs=[hbm, hbm, vmem],
        out_shape=[
            like(leaf_basis),
            like(leaf_transfer),
            shape(blocks, rank, 2 * rank, kind=B16),
        ],
        scratch_shapes=[
            pltpu.VMEM(leaf_basis.shape, F32),
            pltpu.VMEM(leaf_transfer.shape, F32),
            pltpu.SemaphoreType.DMA((steps,)),
            pltpu.SemaphoreType.DMA((steps,)),
        ],
        compiler_params=params,
        cost_estimate=cost(5 * 10**9, 8 * 10**6),
        name="leaf",
    )(leaf_basis, leaf_transfer, couplings, own_factor, carry, *factors)
    sets = -(-(levels + n_leaf) // SET)
    new_transfers, coupled = pl.pallas_call(
        functools.partial(top_kernel, n_rows, n_leaf, steps),
        in_specs=[vmem] * (levels + 5) + [smem],
        out_specs=[hbm, hbm],
        out_shape=[shape(1, levels, rank, rank), like(couplings)],
        scratch_shapes=[
            pltpu.VMEM((sets * SET, rank, rank), F32),
            pltpu.VMEM((sets * SET, rank, 2 * rank), F32),
            pltpu.VMEM((n_leaf, rank, 4 * rank), B16),
            pltpu.VMEM((1, levels, rank, rank), F32),
            pltpu.VMEM(couplings.shape, F32),
            pltpu.SemaphoreType.DMA(()),
            pltpu.SemaphoreType.DMA((steps,)),
        ]
        + scratch(sets),
        compiler_params=params,
        name="top",
    )(carry, got, *path, upper_transfer, device_transfer, own_factor, split, couple_offset)
    return (leaf_orth, leaf_bridge, new_transfers, coupled)


def solution(mesh):
    in_specs = (
        P(("leaf", "rows"), None, None),
        P(("leaf", "rows"), None, None),
        P(("leaf", "rows"), None, None),
        P(),
        P(("leaf", "rows"), None, None),
        P(("leaf", "rows")),
    )
    out_specs = (
        P(("leaf", "rows"), None, None),
        P(("leaf", "rows"), None, None),
        P(("leaf", "rows"), None, None, None),
        P(("leaf", "rows"), None, None),
    )
    return jax.shard_map(
        per_device, mesh=mesh, in_specs=in_specs, out_specs=out_specs, check_vma=False
    )
```

```python
import functools

import jax
import jax.numpy as jnp
from jax import lax
from jax.experimental import pallas as pl
from jax.experimental.pallas import tpu as pltpu
from jax.sharding import PartitionSpec as P

HIGH = lax.Precision.HIGHEST
SUB = 8
LANES = 128
SET = LANES // SUB
GROUP = 4
F32 = jnp.float32
B16 = jnp.bfloat16


def mm(a, b, dims=((1,), (0,)), precision=None):
    return lax.dot_general(
        a, b, (dims, ((), ())), precision=precision, preferred_element_type=F32
    )


def mm_nt(a, b, precision=None):
    return mm(a, b, ((1,), (1,)), precision)


def mm_tn(a, b, precision=None):
    return mm(a, b, ((0,), (0,)), precision)


def lift(gram, trans):
    return mm_tn(trans, mm(gram, trans, precision=HIGH), HIGH)


def halves(x):
    high = x.astype(B16).astype(F32)
    return high, x - high


def pair(x):
    return jnp.concatenate(halves(x), axis=1).astype(B16)


def twice(x):
    return jnp.concatenate([x, x], axis=1)


def tall(x):
    high, low = halves(x)
    high, low = high.astype(B16), low.astype(B16)
    return jnp.concatenate([high, high, low, low], axis=0)


def broad(x):
    high, low = halves(x)
    return jnp.concatenate([high, high, low, low], axis=1).astype(B16)


def fold(x):
    half = x.shape[1] // 2
    return x[:, :half] + x[:, half:]


def spread(value, at):
    return jnp.broadcast_to(value[at : at + 1, :], (SUB, LANES))


def added(terms):
    while len(terms) > 1:
        terms = [sum(terms[n : n + 2][1:], terms[n]) for n in range(0, len(terms), 2)]
    return terms[0]


def load_sets(flat, w_ref, alone=False):
    sets, groups, rank = w_ref.shape[0], w_ref.shape[1], w_ref.shape[2]
    for t in range(sets):
        for ib in range(groups):
            rows = [
                flat[pl.ds(t * SET * rank + ib * SUB + s, SET, stride=0 if alone else rank), :]
                for s in range(SUB)
            ]
            w_ref[t, ib] = jnp.concatenate(rows, axis=0).T


def eliminate(w_ref, g_ref, out, alone=False):
    sets, groups, rank = w_ref.shape[0], w_ref.shape[1], w_ref.shape[2]
    place = lax.broadcasted_iota(jnp.int32, (SUB, LANES), 0)
    lane = lax.broadcasted_iota(jnp.int32, (SUB, LANES), 1)
    group = lane // SET
    picks = [p * SET + lane % SET for p in range(SUB)]

    def tile(t, ib, jv):
        return w_ref[t, ib, pl.ds(jv * SUB, SUB), :]

    def picked(value, p):
        return jnp.take_along_axis(value, picks[p], axis=1, mode="promise_in_bounds")

    def corner(t, kb):
        diagonal = tile(t, kb, kb)
        rows = [picked(diagonal, p) for p in range(SUB)]
        pivot = spread(rows[0], 0)
        inverses, roots = [], []
        for q in range(SUB):
            unit = jnp.where(place == q, 1.0, rows[q])
            sides = {p: spread(rows[q], p) for p in range(q + 1, SUB)}
            inverse = pl.reciprocal(pivot, approx=True)
            inverses.append(inverse)
            roots.append(lax.rsqrt(pivot))
            if q + 1 < SUB:
                pivot = spread(rows[q + 1], q + 1) - sides[q + 1] * sides[q + 1] * inverse
            for p in range(q + 1, SUB):
                kept = jnp.where(place == q, 0.0, rows[p])
                rows[p] = kept - (sides[p] * unit) * inverse
        return rows, inverses, roots

    def merged(parts):
        value = parts[0]
        for p in range(1, SUB):
            value = jnp.where(group == p, parts[p], value)
        return value

    def copied(ref, row):
        return ref[pl.ds(row, SUB, stride=0), :]

    def panel(t, kb, rows):
        for p in range(SUB):
            g_ref[t, p, pl.ds(kb * SUB, SUB), :] = rows[p]
        for jv in [kb + 1 + n for n in range(groups - 1 - kb)] + list(range(kb)):
            value = tile(t, kb, jv)
            for p in range(SUB):
                g_ref[t, p, pl.ds(jv * SUB, SUB), :] = picked(value, p)
        return {
            (p, q): copied(g_ref.at[t, p], kb * SUB + q) for p in range(SUB) for q in range(p)
        }

    def store(t, kb, mult, rows, roots):
        root = merged(roots)
        zero = jnp.zeros((SUB, LANES), F32)
        lanes = [
            merged([mult[p, q] if p > q else zero for p in range(SUB)]) for q in range(SUB - 1)
        ]
        upper, lower = [], []
        for jv in range(groups):
            if jv == kb:
                final = merged(rows) * root
                upper.append(jnp.where(place >= group, final, 0.0))
                unit = jnp.where(place == group, root, 0.0)
                lower.append(jnp.where(place < group, final, unit))
                continue
            terms = [lanes[q] * g_ref[t, q, pl.ds(jv * SUB, SUB), :] for q in range(SUB - 1)]
            final = added([tile(t, kb, jv)] + terms) * root
            upper.append(final if jv > kb else zero)
            lower.append(final if jv < kb else zero)
        turned = jnp.concatenate(upper + lower, axis=0).T
        for s in range(SUB):
            if alone:
                out[pl.ds(kb * SUB + s, 1), :] = turned[s * SET : s * SET + 1]
            else:
                out[pl.ds(t * SET * rank + kb * SUB + s, SET, stride=rank), :] = turned[
                    s * SET : (s + 1) * SET
                ]

    def weights(t, kb, ib, mult, inverses):
        columns = [copied(w_ref.at[t, ib], kb * SUB + q) for q in range(SUB)]
        found = []
        for q in range(SUB):
            term = added([columns[q]] + [mult[q, r] * columns[r] for r in range(q)])
            found.append(term * inverses[q])
        return [
            added([found[r]] + [found[q] * mult[q, r] for q in range(r + 1, SUB)])
            for r in range(SUB)
        ]

    def trail(t, kb, ib, jv, found):
        if jv == kb:
            value = -found[0]
            for r in range(1, SUB):
                value = jnp.where(place == r, -found[r], value)
        else:
            terms = [found[r] * g_ref[t, r, pl.ds(jv * SUB, SUB), :] for r in range(SUB)]
            value = tile(t, ib, jv) - added(terms)
        w_ref[t, ib, pl.ds(jv * SUB, SUB), :] = value

    corners = [corner(t, 0) for t in range(sets)]
    for kb in range(groups):
        mults = [panel(t, kb, corners[t][0]) for t in range(sets)]
        ahead = []
        if kb + 1 < groups:
            for t in range(sets):
                found = weights(t, kb, kb + 1, mults[t], corners[t][1])
                for jv in [kb + 1] + [jv for jv in range(groups) if jv != kb + 1]:
                    trail(t, kb, kb + 1, jv, found)
            ahead = [corner(t, kb + 1) for t in range(sets)]
        for t in range(sets):
            for ib in range(kb + 2, groups):
                found = weights(t, kb, ib, mults[t], corners[t][1])
                for jv in range(groups):
                    trail(t, kb, ib, jv, found)
            store(t, kb, mults[t], corners[t][0], corners[t][2])
        corners = ahead


def pack(x):
    half = x.shape[0] // 2
    return jnp.concatenate([x[:half], x[half:]], axis=1)


def unpack(x):
    half = x.shape[1] // 2
    return jnp.concatenate([x[:, :half], x[:, half:]], axis=0)


def gram_kernel(steps, sets, basis_hbm, trans_hbm, dev_ref, *refs):
    grams_refs = refs[:sets]
    own_ref, lift_ref, basis_ref, trans_ref, basis_sem, trans_sem = refs[sets:]
    leaves, rank = basis_ref.shape[0], basis_ref.shape[1]
    chunk = leaves // steps
    copies = []
    for step in range(steps):
        span = pl.ds(step * chunk, chunk)
        copies.append(
            (
                pltpu.make_async_copy(basis_hbm.at[span], basis_ref.at[span], basis_sem.at[step]),
                pltpu.make_async_copy(trans_hbm.at[span], trans_ref.at[span], trans_sem.at[step]),
            )
        )
        for copy in copies[-1]:
            copy.start()
    groups = leaves // GROUP
    products, parts, edges, rights = {}, {}, {}, {}
    total = None
    for stage in range(groups + 3):
        if stage < groups:
            if stage * GROUP % chunk == 0:
                for copy in copies[stage * GROUP // chunk]:
                    copy.wait()
            twos = []
            for n in range(stage * GROUP, (stage + 1) * GROUP):
                twos.append(jnp.concatenate(halves(basis_ref[n]), axis=0).astype(B16))
            products[stage] = [mm_nt(two, two) for two in twos]
        group = stage - 1
        if 0 <= group < groups:
            edges[group] = [
                pair(trans_ref[n]) for n in range(group * GROUP, (group + 1) * GROUP)
            ]
            parts[group] = []
            for n, product in enumerate(products.pop(group)):
                gram = fold(product[:rank] + product[rank:])
                at = group * GROUP + n
                grams_refs[at // SET][at % SET] = gram
                both = jnp.concatenate(halves(gram), axis=0).astype(B16)
                parts[group].append(mm(both, edges[group][n]))
        group = stage - 2
        if 0 <= group < groups:
            rights[group] = [pair(fold(part[:rank] + part[rank:])) for part in parts.pop(group)]
        group = stage - 3
        if 0 <= group < groups and group % 2:
            left = jnp.concatenate(edges.pop(group - 1) + edges.pop(group), axis=0)
            right = jnp.concatenate(rights.pop(group - 1) + rights.pop(group), axis=0)
            term = mm_tn(left, right)
            total = term if total is None else total + term
    gram = fold(total[:rank] + total[rank:])
    own_ref[...] = pack(gram)
    lift_ref[...] = pack(lift(gram, dev_ref[0]))


def factor_kernel(grams_ref, after_ref, out_ref, token_ref, w_ref, g_ref):
    del after_ref
    count, rank = grams_ref.shape[0], grams_ref.shape[1]
    load_sets(grams_ref.reshape(count * rank, rank), w_ref)
    eliminate(w_ref, g_ref, out_ref.reshape(count * rank, 2 * rank))
    token_ref[...] = jnp.zeros(token_ref.shape, F32)


def own_kernel(own_ref, after_ref, out_ref, token_ref, full_ref, w_ref, g_ref):
    del after_ref
    full_ref[...] = unpack(own_ref[...])
    load_sets(full_ref, w_ref, alone=True)
    eliminate(w_ref, g_ref, out_ref, alone=True)
    token_ref[...] = jnp.zeros(token_ref.shape, F32)


def row_hop_kernel(
    bit, last, mine_ref, got_ref, own_ref, upper_ref, after_ref, path_ref, next_ref
):
    del after_ref
    n_rows, n_leaf = lax.axis_size("rows"), lax.axis_size("leaf")
    level = (n_rows * n_leaf).bit_length() - 2 - bit
    myself = lax.axis_index("leaf") * n_rows + lax.axis_index("rows")
    packed = mine_ref[...] + got_ref[...]
    path_ref[...] = packed
    lifted = pack(lift(unpack(packed), upper_ref[2**level - 2 + (myself >> (bit + 1))]))
    if last:
        half = lifted.shape[0]
        next_ref[:half] = lifted
        next_ref[half:] = own_ref[...]
    else:
        next_ref[...] = lifted


def packed_places(half):
    row = lax.broadcasted_iota(jnp.int32, (half, 4 * half), 0)
    lane = lax.broadcasted_iota(jnp.int32, (half, 4 * half), 1)
    return jnp.where(lane < 2 * half, row, row + half), lane % (2 * half)


def join(a, b):
    half = a.shape[0]
    row, column = packed_places(half)
    diagonal = jnp.sum(jnp.where(row == column, a, 0.0), axis=0, keepdims=True)
    joint = jnp.where(row > column, a, b)
    return jnp.concatenate([joint, jnp.broadcast_to(diagonal, (SUB, 4 * half))], axis=0)


def part(x):
    half = x.shape[0] - SUB
    joint = unpack(x[:half])
    turned = joint.T
    row = lax.broadcasted_iota(jnp.int32, joint.shape, 0)
    column = lax.broadcasted_iota(jnp.int32, joint.shape, 1)
    diagonal = jnp.broadcast_to(fold(x[half : half + 1]), joint.shape)
    first = jnp.where(row > column, joint, jnp.where(row == column, diagonal, turned))
    return first, jnp.where(row <= column, joint, turned)


def leaf_hop_kernel(bit, mine_ref, got_ref, upper_ref, after_ref, path_ref, next_ref):
    del after_ref
    half = path_ref.shape[0]
    level = lax.axis_size("leaf").bit_length() - 2 - bit
    packed = mine_ref[:half] + got_ref[:half]
    path_ref[...] = packed
    node = lax.axis_index("leaf") >> (bit + 1)
    next_ref[:half] = pack(lift(unpack(packed), upper_ref[2**level - 2 + node]))
    if bit == 0:
        next_ref[half:] = join(mine_ref[half:], got_ref[half:])
    else:
        size = mine_ref.shape[0] - half
        next_ref[half : half + size] = mine_ref[half:]
        next_ref[half + size :] = got_ref[half:]


def leaf_kernel(steps, sets, basis_ref, trans_ref, coup_ref, own_ref, after_ref, *refs):
    del after_ref
    factor_refs = refs[:sets]
    (
        orth_hbm,
        bridge_hbm,
        split_ref,
        orth_ref,
        bridge_ref,
        orth_sem,
        bridge_sem,
    ) = refs[sets:]
    leaves, rank = basis_ref.shape[0], basis_ref.shape[1]
    chunk = leaves // steps
    lane = lax.broadcasted_iota(jnp.int32, (rank, 2 * rank), 1)
    own_upper = twice(pair(own_ref[:, :rank]))
    own_inverse = broad(own_ref[:, rank:])
    copies = []

    def send(source, target, sem):
        copies.append(pltpu.make_async_copy(source, target, sem))
        copies[-1].start()

    for step in range(steps):
        moved = []
        for n in range(step * chunk, (step + 1) * chunk):
            high, low = halves(factor_refs[n // SET][n % SET])
            low = jnp.concatenate([low[:, rank:], low[:, :rank]], axis=1)
            upper = jnp.where(lane < rank, high, low).astype(B16)
            inverse = jnp.where(lane < rank, low, high).astype(B16)
            moved.append(mm(twice(upper), tall(trans_ref[n])))
            orth_ref[n] = mm(twice(inverse), tall(basis_ref[n]))
        span = pl.ds(step * chunk, chunk)
        send(orth_ref.at[span], orth_hbm.at[span], orth_sem.at[step])
        moved = twice(pair(jnp.concatenate(moved, axis=0)))
        bridge_ref[span] = mm_nt(moved, own_inverse).reshape(chunk, rank, rank)
        send(bridge_ref.at[span], bridge_hbm.at[span], bridge_sem.at[step])
    chunk = coup_ref.shape[0] // steps
    for step in range(steps):
        span = range(step * chunk, (step + 1) * chunk)
        values = [mm(own_upper, tall(coup_ref[b])) for b in span]
        for b, value in zip(span, values):
            split_ref[b] = pair(value)
    for copy in copies:
        copy.wait()


def top_kernel(n_rows, n_leaf, steps, mine_ref, got_ref, *refs):
    levels = (n_rows * n_leaf).bit_length() - 1
    path_refs = refs[: levels - 1]
    (
        upper_ref,
        dev_ref,
        own_ref,
        split_ref,
        offset_ref,
        fresh_hbm,
        coupled_hbm,
        grams_ref,
        factor_ref,
        cols_ref,
        fresh_ref,
        coupled_ref,
        fresh_sem,
        coupled_sem,
        w_ref,
        g_ref,
    ) = refs[levels - 1 :]
    rank = grams_ref.shape[1]
    branch, row = lax.axis_index("leaf"), lax.axis_index("rows")
    myself = branch * n_rows + row
    for n in range(levels - 1):
        grams_ref[n] = unpack(path_refs[n][...])
    half = rank // 2
    grams_ref[levels - 1] = unpack(mine_ref[:half] + got_ref[:half])
    pairs = n_leaf // 4
    for n in range(pairs):
        for place, ref in ((0, mine_ref), (pairs, got_ref)):
            joint = ref[pl.ds(half + n * (half + SUB), half + SUB), :]
            at = levels + 2 * (place + n)
            grams_ref[at], grams_ref[at + 1] = part(joint)
    count = grams_ref.shape[0]
    load_sets(grams_ref.reshape(count * rank, rank), w_ref)
    eliminate(w_ref, g_ref, factor_ref.reshape(count * rank, 2 * rank))
    for n in range(n_leaf):
        cols_ref[n] = broad(factor_ref[levels + n, :, :rank])
    copies = []

    def send(source, target, sem):
        copies.append(pltpu.make_async_copy(source, target, sem))
        copies[-1].start()

    lows, edges, inverses = [twice(pair(own_ref[:, :rank]))], [tall(dev_ref[0])], []
    for k in range(levels):
        inverses.append(broad(factor_ref[k, :, rank:]))
        if k:
            lows.append(twice(pair(factor_ref[k - 1, :, :rank])))
            edges.append(tall(upper_ref[2 ** (levels - k) - 2 + (myself >> k)]))
    inner = [mm(low, edge) for low, edge in zip(lows, edges)]
    inner = [twice(pair(value)) for value in inner]
    for k in range(levels):
        fresh_ref[0, k] = mm_nt(inner[k], inverses[k])
    send(fresh_ref, fresh_hbm, fresh_sem)
    blocks = split_ref.shape[0]
    chunk = blocks // steps
    for step in range(steps):
        for b in range(step * chunk, (step + 1) * chunk):
            target = lax.rem(myself + offset_ref[b], n_rows * n_leaf)
            column = cols_ref[(target // n_rows) ^ branch]
            coupled_ref[b] = mm_nt(twice(split_ref[b]), column)
        span = pl.ds(step * chunk, chunk)
        send(coupled_ref.at[span], coupled_hbm.at[span], coupled_sem.at[step])
    for copy in copies:
        copy.wait()


def swap(value, axis, bit):
    pairs = [(source, source ^ 2**bit) for source in range(lax.axis_size(axis))]
    return lax.ppermute(value, axis, pairs)


def cost(flops, moved):
    return pl.CostEstimate(flops=flops, bytes_accessed=moved, transcendentals=0)


def per_device(
    leaf_basis, leaf_transfer, device_transfer, upper_transfer, couplings, couple_offset
):
    n_rows = lax.axis_size("rows")
    n_leaf = lax.axis_size("leaf")
    row_bits = n_rows.bit_length() - 1
    leaf_bits = n_leaf.bit_length() - 1
    levels = row_bits + leaf_bits
    leaves, rank, _ = leaf_basis.shape
    blocks = couplings.shape[0]
    groups = rank // SUB
    params = pltpu.CompilerParams(vmem_limit_bytes=40 * 1024 * 1024)
    vmem = pl.BlockSpec(memory_space=pltpu.VMEM)
    smem = pl.BlockSpec(memory_space=pltpu.SMEM)
    hbm = pl.BlockSpec(memory_space=pltpu.HBM)
    steps = 4

    def like(array, kind=F32):
        return jax.ShapeDtypeStruct(array.shape, kind)

    def shape(*sizes, kind=F32):
        return jax.ShapeDtypeStruct(sizes, kind)

    def scratch(sets):
        return [
            pltpu.VMEM((sets, groups, rank, LANES), F32),
            pltpu.VMEM((sets, SUB, rank, LANES), F32),
        ]

    sets = leaves // SET
    half = rank // 2
    any_place = pl.BlockSpec(memory_space=pl.ANY)
    *grams, own_gram, own_lift = pl.pallas_call(
        functools.partial(gram_kernel, steps, sets),
        in_specs=[hbm, hbm, vmem],
        out_specs=[vmem] * (sets + 2),
        out_shape=[shape(SET, rank, rank)] * sets + [shape(half, 2 * rank)] * 2,
        scratch_shapes=[
            pltpu.VMEM(leaf_basis.shape, F32),
            pltpu.VMEM(leaf_transfer.shape, F32),
            pltpu.SemaphoreType.DMA((steps,)),
            pltpu.SemaphoreType.DMA((steps,)),
        ],
        compiler_params=pltpu.CompilerParams(vmem_limit_bytes=52 * 1024 * 1024),
        cost_estimate=cost(10**9, 4 * 10**6),
        name="gram",
    )(leaf_basis, leaf_transfer, device_transfer)
    path = []
    carry = own_lift
    for bit in range(row_bits):
        got = swap(carry, "rows", bit)
        last = bit == row_bits - 1
        if bit == 1:
            own_factor, token = pl.pallas_call(
                own_kernel,
                in_specs=[vmem, any_place],
                out_specs=[vmem, vmem],
                out_shape=[shape(rank, 2 * rank), shape(SUB, LANES)],
                scratch_shapes=[pltpu.VMEM((rank, rank), F32)] + scratch(1),
                compiler_params=params,
                cost_estimate=cost(5 * 10**9, 8 * 10**6),
                name="own",
            )(own_gram, carry)
        gram, carry = pl.pallas_call(
            functools.partial(row_hop_kernel, bit, last),
            in_specs=[vmem] * 4 + [any_place],
            out_specs=[vmem, vmem],
            out_shape=[shape(half, 2 * rank), shape(rank if last else half, 2 * rank)],
            compiler_params=params,
            name="row_hop",
        )(carry, got, own_gram, upper_transfer, token if bit == 1 else own_gram)
        path.append(gram)
    factors = []
    for bit in range(leaf_bits - 1):
        got = swap(carry, "leaf", bit)
        if len(factors) < sets:
            factor, token = pl.pallas_call(
                factor_kernel,
                in_specs=[vmem, any_place],
                out_specs=[vmem, vmem],
                out_shape=[shape(SET, rank, 2 * rank), shape(SUB, LANES)],
                scratch_shapes=scratch(1),
                compiler_params=params,
                cost_estimate=cost(5 * 10**9, 8 * 10**6),
                name="factor",
            )(grams[len(factors)], carry)
            factors.append(factor)
        gram, carry = pl.pallas_call(
            functools.partial(leaf_hop_kernel, bit),
            in_specs=[vmem] * 3 + [any_place],
            out_specs=[vmem, vmem],
            out_shape=[shape(half, 2 * rank), shape(half + (half + SUB) * 2**bit, 2 * rank)],
            compiler_params=params,
            name="leaf_hop",
        )(carry, got, upper_transfer, token)
        path.append(gram)
    got = swap(carry, "leaf", leaf_bits - 1)
    leaf_orth, leaf_bridge, split = pl.pallas_call(
        functools.partial(leaf_kernel, steps, sets),
        in_specs=[vmem] * 4 + [any_place] + [vmem] * sets,
        out_specs=[hbm, hbm, vmem],
        out_shape=[
            like(leaf_basis),
            like(leaf_transfer),
            shape(blocks, rank, 2 * rank, kind=B16),
        ],
        scratch_shapes=[
            pltpu.VMEM(leaf_basis.shape, F32),
            pltpu.VMEM(leaf_transfer.shape, F32),
            pltpu.SemaphoreType.DMA((steps,)),
            pltpu.SemaphoreType.DMA((steps,)),
        ],
        compiler_params=params,
        cost_estimate=cost(5 * 10**9, 8 * 10**6),
        name="leaf",
    )(leaf_basis, leaf_transfer, couplings, own_factor, carry, *factors)
    sets = -(-(levels + n_leaf) // SET)
    new_transfers, coupled = pl.pallas_call(
        functools.partial(top_kernel, n_rows, n_leaf, steps),
        in_specs=[vmem] * (levels + 5) + [smem],
        out_specs=[hbm, hbm],
        out_shape=[shape(1, levels, rank, rank), like(couplings)],
        scratch_shapes=[
            pltpu.VMEM((sets * SET, rank, rank), F32),
            pltpu.VMEM((sets * SET, rank, 2 * rank), F32),
            pltpu.VMEM((n_leaf, rank, 4 * rank), B16),
            pltpu.VMEM((1, levels, rank, rank), F32),
            pltpu.VMEM(couplings.shape, F32),
            pltpu.SemaphoreType.DMA(()),
            pltpu.SemaphoreType.DMA((steps,)),
        ]
        + scratch(sets),
        compiler_params=params,
        name="top",
    )(carry, got, *path, upper_transfer, device_transfer, own_factor, split, couple_offset)
    return (leaf_orth, leaf_bridge, new_transfers, coupled)


def solution(mesh):
    in_specs = (
        P(("leaf", "rows"), None, None),
        P(("leaf", "rows"), None, None),
        P(("leaf", "rows"), None, None),
        P(),
        P(("leaf", "rows"), None, None),
        P(("leaf", "rows")),
    )
    out_specs = (
        P(("leaf", "rows"), None, None),
        P(("leaf", "rows"), None, None),
        P(("leaf", "rows"), None, None, None),
        P(("leaf", "rows"), None, None),
    )
    return jax.shard_map(
        per_device, mesh=mesh, in_specs=in_specs, out_specs=out_specs, check_vma=False
    )
```
